32 devices in a mesh: parts: 2 (over x), dp: 8 (over z, y), mp: 2 (over core).
Axes of the slice: x: 2, y: 2, z: 4, core: 2. Of those that a mesh axis runs over, the one named last changes fastest.
Arguments:
- inputs: bfloat16 [3072, 8192], P(('parts', 'dp'), 'mp'), parts along dimension 0, may hold values from -6 to 6
- gate_pre: bfloat16 [3072, 14336], P(('parts', 'dp'), 'mp'), parts along dimension 0, may hold values from -8 to 8
- up_pre: bfloat16 [3072, 14336], P(('parts', 'dp'), 'mp'), parts along dimension 0, may hold values from -6 to 6
- hidden_grad: bfloat16 [3072, 14336], P(('parts', 'dp'), 'mp'), parts along dimension 0, may hold values from -6 to 6
- out_grad: bfloat16 [3072, 8192], P(('parts', 'dp'), 'mp'), parts along dimension 0, may hold values from -6 to 6
- example_ids: int32 [3072], P(('parts', 'dp')), parts along dimension 0, may hold values from 0 to 15, as said below
- gate_in: bfloat16 [8192, 64], P('mp'), may hold values from -0.0625 to 0.0625
- gate_out: bfloat16 [14336, 64], P('mp'), may hold values from -0.046875 to 0.046875
- up_in: bfloat16 [8192, 64], P('mp'), may hold values from -0.0625 to 0.0625
- up_out: bfloat16 [14336, 64], P('mp'), may hold values from -0.046875 to 0.046875
- down_in: bfloat16 [14336, 64], P('mp'), may hold values from -0.046875 to 0.046875
- down_out: bfloat16 [8192, 64], P('mp'), may hold values from -0.0625 to 0.0625
- queries: bfloat16 [512, 12288], P(None, ('dp', 'mp')), may hold values from -0.005859375 to 0.005859375
Outputs:
- scores: float32 [32, 512], P(('parts', 'dp', 'mp')), parts along dimension 0
The draws below stay inside these ranges and needn't reach their ends.
There are 2 independent parts, one for each index of `parts`. The reference program is written for one: setup_inputs(seed, part) draws one part's arguments, and reference() takes and returns one part's arrays. A program takes and returns all parts, laid end to end along the dimension named above; an argument that names none is the same for every part. Nothing has to cross between parts.
Inputs may be any that keep to these rules, and one draw needn't show every extreme that they name: example_ids never fall along the tokens: each example is one run of consecutive tokens; example 0 begins at token 0 and example e > 0 begins at a token in [e * 96, (e + 1) * 96).
All inputs are finite; a program needn't handle non-finite values.
Results may differ from the reference program's by a relative error of at most 0.0029.
Values may be sent and summed in bfloat16 or wider, within the bound.
No kernel may reach another device: no remote copies, remote signals or barrier semaphores. Data moves between devices by JAX's collectives and lax.ppermute only.
A program may use at most 128 MiB of HBM per device.

```python
import jax
import jax.numpy as jnp
from jax import lax

D = 8192
FW = 14336
K = 64
Q = 512
TOKENS = 1536
EXAMPLES = 16


def draw_example_ids(key, part):
    key = jax.random.fold_in(key, 5)
    stride = TOKENS // EXAMPLES
    offsets = jax.random.randint(key, (EXAMPLES - 1,), 0, stride, dtype=jnp.int32)
    starts = jnp.arange(1, EXAMPLES, dtype=jnp.int32) * stride + offsets
    positions = jnp.arange(TOKENS, dtype=jnp.int32)
    return jnp.sum((positions[:, None] >= starts[None, :]).astype(jnp.int32), axis=1).astype(jnp.int32)


def shard_levels(stream_key, shape, split, smallest, top_value):
    def one(axis_at, blocks):
        draws = jax.random.uniform(jax.random.fold_in(jax.random.fold_in(stream_key, 6), axis_at), (blocks,), jnp.float32, smallest / len(split), top_value / len(split))
        return jnp.repeat(jnp.exp(draws), shape[axis_at] // blocks).reshape((-1,) + (1,) * (len(shape) - axis_at - 1))

    loudness = one(*split[0])
    for cut in split[1:]:
        loudness = loudness * one(*cut)
    return loudness


def normal_values(stream_key, shape, deviation, reach, shards=(), held_as=jnp.bfloat16):
    result = jax.random.normal(stream_key, shape, jnp.float32) * deviation
    if len(shards) > 0:
        result = shard_levels(stream_key, shape, shards, -0.22, 0.18) * result
    return jnp.clip(result, min=-reach, max=reach).astype(held_as)


def setup_inputs(seed: int = 0, part: int = 0) -> dict:
    key_of = jax.random.split(jax.random.key(seed), 14)
    own_keys = jax.random.split(jax.random.fold_in(key_of[13], part), 14)
    inputs = normal_values(own_keys[0], (TOKENS, D), 1.0, 6.0, ((0, 8), (1, 2)))
    gate_pre = normal_values(own_keys[1], (TOKENS, FW), 1.5, 8.0, ((0, 8), (1, 2)))
    up_pre = normal_values(own_keys[2], (TOKENS, FW), 1.0, 6.0, ((0, 8), (1, 2)))
    hidden_grad = normal_values(own_keys[3], (TOKENS, FW), 1.0, 6.0, ((0, 8), (1, 2)))
    out_grad = normal_values(own_keys[4], (TOKENS, D), 1.0, 6.0, ((0, 8), (1, 2)))
    example_ids = draw_example_ids(jax.random.fold_in(jax.random.fold_in(key_of[13], part), 71), part)
    gate_in = normal_values(key_of[6], (D, K), D ** -0.5, 0.0625, ((0, 2),))
    gate_out = normal_values(key_of[7], (FW, K), FW ** -0.5, 0.046875, ((0, 2),))
    up_in = normal_values(key_of[8], (D, K), D ** -0.5, 0.0625, ((0, 2),))
    up_out = normal_values(key_of[9], (FW, K), FW ** -0.5, 0.046875, ((0, 2),))
    down_in = normal_values(key_of[10], (FW, K), FW ** -0.5, 0.046875, ((0, 2),))
    down_out = normal_values(key_of[11], (D, K), D ** -0.5, 0.0625, ((0, 2),))
    queries = normal_values(key_of[12], (Q, 3 * K * K), (3 * K * K * TOKENS // EXAMPLES) ** -0.5, 0.005859375, ((1, 16),))
    return {"inputs": inputs, "gate_pre": gate_pre, "up_pre": up_pre, "hidden_grad": hidden_grad, "out_grad": out_grad, "example_ids": example_ids, "gate_in": gate_in, "gate_out": gate_out, "up_in": up_in, "up_out": up_out, "down_in": down_in, "down_out": down_out, "queries": queries}


def per_example(onehot, left, right):
    weighted = (onehot[:, :, None] * left[:, None, :]).reshape(left.shape[0], -1)
    outer = jnp.einsum("tc,tj->cj", weighted, right, precision=lax.Precision.HIGHEST)
    return outer.reshape(onehot.shape[1], -1)


def reference(inputs, gate_pre, up_pre, hidden_grad, out_grad, example_ids, gate_in, gate_out, up_in, up_out, down_in, down_out, queries):
    gate_value = gate_pre.astype(jnp.float32)
    up_value = up_pre.astype(jnp.float32)
    sigmoid_gate = jax.nn.sigmoid(gate_value)
    hidden = (gate_value * sigmoid_gate * up_value).astype(jnp.bfloat16)
    back_value = hidden_grad.astype(jnp.float32)
    gate_grad = (back_value * up_value * sigmoid_gate * (1.0 + gate_value * (1.0 - sigmoid_gate))).astype(jnp.bfloat16)
    up_grad = (back_value * gate_value * sigmoid_gate).astype(jnp.bfloat16)
    a_gate = jnp.dot(inputs, gate_in, preferred_element_type=jnp.float32)
    b_gate = jnp.dot(gate_grad, gate_out, preferred_element_type=jnp.float32)
    a_up = jnp.dot(inputs, up_in, preferred_element_type=jnp.float32)
    b_up = jnp.dot(up_grad, up_out, preferred_element_type=jnp.float32)
    a_down = jnp.dot(hidden, down_in, preferred_element_type=jnp.float32)
    b_down = jnp.dot(out_grad, down_out, preferred_element_type=jnp.float32)
    labels = jnp.arange(EXAMPLES, dtype=jnp.int32)
    onehot = (example_ids[:, None] == labels[None, :]).astype(jnp.float32)
    example_grad = jnp.concatenate([per_example(onehot, a_gate, b_gate), per_example(onehot, a_up, b_up), per_example(onehot, a_down, b_down)], axis=1)
    return jnp.dot(example_grad, queries.astype(jnp.float32).T, precision=lax.Precision.HIGHEST)
```

```python
import jax
import jax.numpy as jnp
from jax import lax
from jax.sharding import PartitionSpec as P

HIGHEST = lax.Precision.HIGHEST


def body(
    inputs,
    gate_pre,
    up_pre,
    hidden_grad,
    out_grad,
    example_ids,
    gate_in,
    gate_out,
    up_in,
    up_out,
    down_in,
    down_out,
    queries,
):
    half_rows = inputs.shape[0] // 2
    width = gate_in.shape[1]
    count = lax.axis_size(("dp", "mp"))
    coords = queries.shape[1]
    gate_value = gate_pre.astype(jnp.float32)
    up_value = up_pre.astype(jnp.float32)
    sigmoid_gate = jax.nn.sigmoid(gate_value)
    hidden = (gate_value * sigmoid_gate * up_value).astype(jnp.bfloat16)
    back_value = hidden_grad.astype(jnp.float32)
    gate_grad = (
        back_value * up_value * sigmoid_gate * (1.0 + gate_value * (1.0 - sigmoid_gate))
    ).astype(jnp.bfloat16)
    up_grad = (back_value * gate_value * sigmoid_gate).astype(jnp.bfloat16)
    projected = jnp.concatenate(
        [
            jnp.dot(inputs, gate_in, preferred_element_type=jnp.float32),
            jnp.dot(gate_grad, gate_out, preferred_element_type=jnp.float32),
            jnp.dot(inputs, up_in, preferred_element_type=jnp.float32),
            jnp.dot(up_grad, up_out, preferred_element_type=jnp.float32),
            jnp.dot(hidden, down_in, preferred_element_type=jnp.float32),
            jnp.dot(out_grad, down_out, preferred_element_type=jnp.float32),
        ],
        axis=1,
    )
    core = lax.axis_index("mp")
    kept = lax.dynamic_slice_in_dim(projected, core * half_rows, half_rows, 0)
    given = lax.dynamic_slice_in_dim(projected, (1 - core) * half_rows, half_rows, 0)
    summed = kept + lax.ppermute(given, "mp", [(0, 1), (1, 0)])
    my_ids = lax.dynamic_slice_in_dim(example_ids, core * half_rows, half_rows, 0)
    labels = lax.axis_index(("dp", "mp")) + jnp.arange(-1, 1, dtype=jnp.int32)
    onehot = (my_ids[:, None] == labels[None, :]).astype(jnp.float32)
    modules = []
    for module in range(3):
        left = summed[:, 2 * module * width : (2 * module + 1) * width]
        right = summed[:, (2 * module + 1) * width : (2 * module + 2) * width]
        weighted = onehot.T[:, :, None] * left[None, :, :]
        modules.append(jnp.einsum("cti,tj->cij", weighted, right, precision=HIGHEST))
    partial_value = jnp.stack(modules, axis=1).reshape(2, count, coords)
    received = lax.all_to_all(partial_value, ("dp", "mp"), split_axis=1, concat_axis=0, tiled=True)
    received = received.reshape(count, 2, coords)
    rows = received[:, 1].at[:-1].add(received[1:, 0])
    scores = jnp.einsum("ec,qc->eq", rows, queries.astype(jnp.float32), precision=HIGHEST)
    pieces = lax.all_to_all(scores, ("dp", "mp"), split_axis=0, concat_axis=0, tiled=True)
    return jnp.sum(pieces, axis=0, keepdims=True)


def solution(mesh):
    placed = (
        P(("parts", "dp"), "mp"),
        P(("parts", "dp"), "mp"),
        P(("parts", "dp"), "mp"),
        P(("parts", "dp"), "mp"),
        P(("parts", "dp"), "mp"),
        P(("parts", "dp")),
        P("mp", None),
        P("mp", None),
        P("mp", None),
        P("mp", None),
        P("mp", None),
        P("mp", None),
        P(None, ("dp", "mp")),
    )
    return jax.shard_map(
        body, mesh=mesh, in_specs=placed, out_specs=P(("parts", "dp", "mp"), None), check_vma=False
    )
```

```python
import jax
import jax.numpy as jnp
from jax import lax
from jax.sharding import PartitionSpec as P

HIGHEST = lax.Precision.HIGHEST


def body(
    inputs,
    gate_pre,
    up_pre,
    hidden_grad,
    out_grad,
    example_ids,
    gate_in,
    gate_out,
    up_in,
    up_out,
    down_in,
    down_out,
    queries,
):
    half_rows = inputs.shape[0] // 2
    width = gate_in.shape[1]
    chips = lax.axis_size("dp")
    swap = [(0, 1), (1, 0)]
    other_queries = lax.ppermute(queries, "mp", swap)
    coords = queries.shape[1]
    gate_value = gate_pre.astype(jnp.float32)
    up_value = up_pre.astype(jnp.float32)
    sigmoid_gate = jax.nn.sigmoid(gate_value)
    hidden = (gate_value * sigmoid_gate * up_value).astype(jnp.bfloat16)
    back_value = hidden_grad.astype(jnp.float32)
    gate_grad = (
        back_value * up_value * sigmoid_gate * (1.0 + gate_value * (1.0 - sigmoid_gate))
    ).astype(jnp.bfloat16)
    up_grad = (back_value * gate_value * sigmoid_gate).astype(jnp.bfloat16)
    projected = jnp.concatenate(
        [
            jnp.dot(inputs, gate_in, preferred_element_type=jnp.float32),
            jnp.dot(gate_grad, gate_out, preferred_element_type=jnp.float32),
            jnp.dot(inputs, up_in, preferred_element_type=jnp.float32),
            jnp.dot(up_grad, up_out, preferred_element_type=jnp.float32),
            jnp.dot(hidden, down_in, preferred_element_type=jnp.float32),
            jnp.dot(out_grad, down_out, preferred_element_type=jnp.float32),
        ],
        axis=1,
    )
    core = lax.axis_index("mp")
    kept = lax.dynamic_slice_in_dim(projected, core * half_rows, half_rows, 0)
    given = lax.dynamic_slice_in_dim(projected, (1 - core) * half_rows, half_rows, 0)
    summed = kept + lax.ppermute(given, "mp", swap)
    my_ids = lax.dynamic_slice_in_dim(example_ids, core * half_rows, half_rows, 0)
    labels = lax.axis_index(("dp", "mp")) + jnp.arange(-1, 1, dtype=jnp.int32)
    onehot = (my_ids[:, None] == labels[None, :]).astype(jnp.float32)
    modules = []
    for module in range(3):
        left = summed[:, 2 * module * width : (2 * module + 1) * width]
        right = summed[:, (2 * module + 1) * width : (2 * module + 2) * width]
        weighted = onehot.T[:, :, None] * left[None, :, :]
        modules.append(jnp.einsum("cti,tj->cij", weighted, right, precision=HIGHEST))
    partial_value = jnp.stack(modules, axis=1).reshape(2, chips, 2 * coords)
    received = lax.all_to_all(partial_value, "dp", split_axis=1, concat_axis=0, tiled=True)
    received = received.reshape(2 * chips, 2, coords)
    first, second = jnp.where(core == 0, 0, 1), jnp.where(core == 0, 1, 0)
    pair_queries = jnp.concatenate([queries, other_queries], axis=1).astype(jnp.float32)
    swapped = jnp.concatenate(
        [jnp.take(received, first, axis=1), jnp.take(received, second, axis=1)], axis=1
    )
    scores = jnp.einsum("ec,qc->eq", swapped, pair_queries, precision=HIGHEST)
    scores = scores.reshape(chips, 2, -1)
    early = scores[:, 0]
    moved = jnp.concatenate([early[1:], jnp.zeros_like(early[:1])], axis=0)
    sent = jnp.where(core == 0, moved, early)
    mine = scores[:, 1] + lax.ppermute(sent, "mp", swap)
    pieces = lax.all_to_all(mine, "dp", split_axis=0, concat_axis=0, tiled=True)
    return jnp.sum(pieces, axis=0, keepdims=True)


def solution(mesh):
    placed = (
        P(("parts", "dp"), "mp"),
        P(("parts", "dp"), "mp"),
        P(("parts", "dp"), "mp"),
        P(("parts", "dp"), "mp"),
        P(("parts", "dp"), "mp"),
        P(("parts", "dp")),
        P("mp", None),
        P("mp", None),
        P("mp", None),
        P("mp", None),
        P("mp", None),
        P("mp", None),
        P(None, ("dp", "mp")),
    )
    return jax.shard_map(
        body, mesh=mesh, in_specs=placed, out_specs=P(("parts", "dp", "mp"), None), check_vma=False
    )
```

```python
import functools

import jax
import jax.numpy as jnp
from jax import lax
from jax.experimental import pallas as pl
from jax.experimental.pallas import tpu as pltpu
from jax.sharding import PartitionSpec as P

HIGHEST = lax.Precision.HIGHEST
NT = (((1,), (1,)), ((), ()))
STEP = 1024
ROWS = 16
AHEAD = 3


def project(
    inputs,
    gate_pre,
    up_pre,
    hidden_grad,
    out_grad,
    gate_in,
    gate_out,
    up_in,
    up_out,
    down_in,
    down_out,
    out,
    v_inputs,
    v_gate,
    v_up,
    v_back,
    v_out_grad,
    v_in,
    v_gate_out,
    v_up_out,
    v_down_in,
    v_down_out,
    made,
    sems,
):
    width = gate_in.shape[0]
    tokens = inputs.shape[0]
    hidden_steps = gate_pre.shape[1] // STEP
    model_steps = inputs.shape[1] // STEP
    copies = []

    def plan(pairs):
        made_here = []
        for source, target in pairs:
            copy = pltpu.make_async_copy(source, target, sems.at[sum(map(len, copies)) + len(made_here)])
            made_here.append(copy)
        copies.append(made_here)

    for step in range(hidden_steps):
        at = pl.ds(step * STEP, STEP)
        pairs = [
            (gate_pre.at[:, at], v_gate.at[:, at]),
            (up_pre.at[:, at], v_up.at[:, at]),
            (hidden_grad.at[:, at], v_back.at[:, at]),
            (gate_out.at[:, at], v_gate_out.at[:, at]),
            (up_out.at[:, at], v_up_out.at[:, at]),
            (down_in.at[:, at], v_down_in.at[:, at]),
        ]
        if step < model_steps:
            pairs += [
                (inputs.at[:, at], v_inputs.at[:, at]),
                (gate_in.at[:, at], v_in.at[pl.ds(0, width), at]),
                (up_in.at[:, at], v_in.at[pl.ds(width, width), at]),
                (out_grad.at[:, at], v_out_grad.at[:, at]),
                (down_out.at[:, at], v_down_out.at[:, at]),
            ]
        plan(pairs)

    def elementwise(step, target):
        for top in range(0, tokens, ROWS):
            for part in range(0, STEP, 256):
                at = (slice(top, top + ROWS), slice(step * STEP + part, step * STEP + part + 256))
                put = (slice(top, top + ROWS), slice(part, part + 256))
                gate = v_gate[at].astype(jnp.float32)
                up = v_up[at].astype(jnp.float32)
                back = v_back[at].astype(jnp.float32)
                sig = 0.5 * jnp.tanh(0.5 * gate) + 0.5
                silu = gate * sig
                made[(target, 0) + put] = (silu * up).astype(jnp.bfloat16)
                made[(target, 1) + put] = (back * silu).astype(jnp.bfloat16)
                slope = sig + silu * (1.0 - sig)
                made[(target, 2) + put] = (back * up * slope).astype(jnp.bfloat16)

    def dot(base, values):
        return lax.dot_general(base, values, NT, preferred_element_type=jnp.float32)

    def add(at, value, first):
        if first:
            out[at] = value
        else:
            out[at] += value

    def hidden_dots(step, target):
        at = slice(step * STEP, (step + 1) * STEP)
        add(slice(2 * width, 3 * width), dot(v_gate_out[:, at], made[target, 2]), step == 0)
        add(slice(3 * width, 4 * width), dot(v_up_out[:, at], made[target, 1]), step == 0)
        add(slice(4 * width, 5 * width), dot(v_down_in[:, at], made[target, 0]), step == 0)

    def model_dots(step):
        at = slice(step * STEP, (step + 1) * STEP)
        add(slice(0, 2 * width), dot(v_in[:, at], v_inputs[:, at]), step == 0)
        add(slice(5 * width, 6 * width), dot(v_down_out[:, at], v_out_grad[:, at]), step == 0)

    for step in range(min(AHEAD, hidden_steps)):
        for copy in copies[step]:
            copy.start()
    for step in range(hidden_steps):
        if step + AHEAD < hidden_steps:
            for copy in copies[step + AHEAD]:
                copy.start()
        for copy in copies[step]:
            copy.wait()
        elementwise(step, step % 2)
        if step >= 1:
            hidden_dots(step - 1, (step - 1) % 2)
        if step < model_steps:
            model_dots(step)
    hidden_dots(hidden_steps - 1, (hidden_steps - 1) % 2)


def projections(*operands):
    inputs, gate_pre = operands[:2]
    width = operands[5].shape[0]
    tokens, model = inputs.shape
    hidden = gate_pre.shape[1]
    assert hidden % STEP == 0 and model % STEP == 0 and model <= hidden
    assert tokens % ROWS == 0
    steps = 6 * (hidden // STEP) + 5 * (model // STEP)
    bf16 = jnp.bfloat16
    return pl.pallas_call(
        project,
        out_shape=jax.ShapeDtypeStruct((6 * width, tokens), jnp.float32),
        in_specs=[pl.BlockSpec(memory_space=pltpu.HBM)] * len(operands),
        out_specs=pl.BlockSpec(memory_space=pltpu.VMEM),
        scratch_shapes=[
            pltpu.VMEM((tokens, model), bf16),
            pltpu.VMEM((tokens, hidden), bf16),
            pltpu.VMEM((tokens, hidden), bf16),
            pltpu.VMEM((tokens, hidden), bf16),
            pltpu.VMEM((tokens, model), bf16),
            pltpu.VMEM((2 * width, model), bf16),
            pltpu.VMEM((width, hidden), bf16),
            pltpu.VMEM((width, hidden), bf16),
            pltpu.VMEM((width, hidden), bf16),
            pltpu.VMEM((width, model), bf16),
            pltpu.VMEM((2, 3, tokens, STEP), bf16),
            pltpu.SemaphoreType.DMA((steps,)),
        ],
        compiler_params=pltpu.CompilerParams(vmem_limit_bytes=40 * 2**20),
        cost_estimate=pl.CostEstimate(
            flops=6 * tokens * width * (model + hidden),
            bytes_accessed=2 * (2 * tokens * model + 3 * tokens * hidden),
            transcendentals=tokens * hidden,
        ),
        name="project",
    )(*operands)


def outer(chips, own, other, ids, *refs):
    outs, (summed, products, blocks) = refs[:chips], refs[chips:]
    chip, core = lax.axis_index("dp"), lax.axis_index("mp")
    width = own.shape[0] // 6
    half = width // 2
    span = 3 * half // chips
    summed[...] = own[...] + other[...]
    own_label = 2 * chip + core
    tail_label = jnp.where(core == 1, 2 * chip - 1, -1)
    masks = [(ids[...] == label).astype(jnp.float32) for label in (tail_label, own_label)]
    lane = lax.broadcasted_iota(jnp.int32, (half, 2 * width), 1)
    for module, (left, right) in enumerate(((0, 2), (1, 3), (4, 5))):
        factor = summed[left * width : (left + 1) * width, :]
        other_factor = summed[right * width : (right + 1) * width, :]
        products[module] = lax.dot_general(
            jnp.concatenate([factor * mask for mask in masks], axis=0),
            jnp.concatenate([other_factor, other_factor], axis=0),
            NT,
            precision=HIGHEST,
            preferred_element_type=jnp.float32,
        )
        for label in range(2):
            even = products[module, pl.ds(label * width, half, stride=2), :]
            odd = products[module, pl.ds(label * width + 1, half, stride=2), :]
            packed = jnp.where(lane < width, even, odd)
            row = 0
            while row < half:
                chip_to, inside = divmod(module * half + row, span)
                count = min(span - inside, half - row)
                put = slice(label * span + inside, label * span + inside + count)
                blocks[chip_to, put, :] = packed[row : row + count]
                row += count
    for flip in range(chips):
        outs[flip][...] = blocks[chip ^ flip]


def example_blocks(chips, own, other, ids):
    width = own.shape[0] // 6
    block = (3 * width // chips, 2 * width)
    return pl.pallas_call(
        functools.partial(outer, chips),
        out_shape=[jax.ShapeDtypeStruct(block, jnp.float32)] * chips,
        in_specs=[pl.BlockSpec(memory_space=pltpu.VMEM)] * 3,
        out_specs=[pl.BlockSpec(memory_space=pltpu.VMEM)] * chips,
        scratch_shapes=[
            pltpu.VMEM(own.shape, jnp.float32),
            pltpu.VMEM((3, 2 * width, 2 * width), jnp.float32),
            pltpu.VMEM((chips,) + block, jnp.float32),
        ],
        name="outer",
    )(own, other, ids)


def score(chips, queries, swapped, *refs):
    received, outs, (rows, result) = refs[:chips], refs[chips : 2 * chips], refs[2 * chips :]
    chip, core = lax.axis_index("dp"), lax.axis_index("mp")
    height, lanes = received[0].shape
    span = height // 2
    for flip in range(chips):
        rows[pl.ds(pl.multiple_of((chip ^ flip) * height, height), height), :] = received[flip][...]
    rows[chips * height :, :] = jnp.zeros((height, lanes), jnp.float32)
    grads = []
    for at in range(span):
        own = rows[pl.ds(span + at, chips, stride=height), :]
        tail = rows[pl.ds(height + at, chips, stride=height), :]
        grads.append(own + tail)
    grads = jnp.concatenate(grads, axis=1)
    high = grads.astype(jnp.bfloat16)
    rest = grads - high.astype(jnp.float32)
    middle = rest.astype(jnp.bfloat16)
    low = (rest - middle.astype(jnp.float32)).astype(jnp.bfloat16)
    terms = jnp.concatenate([high, middle, low], axis=0)
    coords = queries.shape[1]
    halves = (terms[:, :coords], terms[:, coords:])
    first = core == 0
    mine = jnp.where(first, halves[0], halves[1])
    theirs = jnp.where(first, halves[1], halves[0])
    scores = lax.dot_general(mine, queries[...], NT, preferred_element_type=jnp.float32)
    scores += lax.dot_general(theirs, swapped[...], NT, preferred_element_type=jnp.float32)
    result[:, 0, :] = scores[:chips] + scores[chips : 2 * chips] + scores[2 * chips :]
    for flip in range(chips):
        outs[flip][...] = result[chip ^ flip]


def partial_scores(chips, queries, swapped, received):
    height, lanes = received[0].shape
    total = queries.shape[0]
    return pl.pallas_call(
        functools.partial(score, chips),
        out_shape=[jax.ShapeDtypeStruct((1, total), jnp.float32)] * chips,
        in_specs=[pl.BlockSpec(memory_space=pltpu.VMEM)] * (2 + chips),
        out_specs=[pl.BlockSpec(memory_space=pltpu.VMEM)] * chips,
        scratch_shapes=[
            pltpu.VMEM(((chips + 1) * height, lanes), jnp.float32),
            pltpu.VMEM((chips, 1, total), jnp.float32),
        ],
        name="score",
    )(queries, swapped, *received)


def exchanged(blocks):
    chips = len(blocks)
    moved = {0: blocks[0]}
    for flip in reversed(range(1, chips)):
        moved[flip] = lax.ppermute(blocks[flip], "dp", [(i, i ^ flip) for i in range(chips)])
    return [moved[flip] for flip in range(chips)]


def body(
    inputs,
    gate_pre,
    up_pre,
    hidden_grad,
    out_grad,
    example_ids,
    gate_in,
    gate_out,
    up_in,
    up_out,
    down_in,
    down_out,
    queries,
):
    chips = lax.axis_size("dp")
    swap = [(0, 1), (1, 0)]
    swapped = lax.ppermute(queries, "mp", swap)
    bases = [base.T for base in (gate_in, gate_out, up_in, up_out, down_in, down_out)]
    own = projections(inputs, gate_pre, up_pre, hidden_grad, out_grad, *bases)
    other = lax.ppermute(own, "mp", swap)
    blocks = exchanged(example_blocks(chips, own, other, example_ids.reshape(1, -1)))
    pieces = exchanged(partial_scores(chips, queries, swapped, blocks))
    return functools.reduce(jnp.add, pieces)


def solution(mesh):
    placed = (
        P(("parts", "dp"), "mp"),
        P(("parts", "dp"), "mp"),
        P(("parts", "dp"), "mp"),
        P(("parts", "dp"), "mp"),
        P(("parts", "dp"), "mp"),
        P(("parts", "dp")),
        P("mp", None),
        P("mp", None),
        P("mp", None),
        P("mp", None),
        P("mp", None),
        P("mp", None),
        P(None, ("dp", "mp")),
    )
    return jax.shard_map(
        body, mesh=mesh, in_specs=placed, out_specs=P(("parts", "dp", "mp"), None), check_vma=False
    )
```

```python
import functools

import jax
import jax.numpy as jnp
from jax import lax
from jax.experimental import pallas as pl
from jax.experimental.pallas import tpu as pltpu
from jax.sharding import PartitionSpec as P

NT = (((1,), (1,)), ((), ()))
STEP = 1024
PART = 512
ROWS = 16
AHEAD = 3


def project(
    inputs,
    gate_pre,
    up_pre,
    hidden_grad,
    out_grad,
    gate_in,
    gate_out,
    up_in,
    up_out,
    down_in,
    down_out,
    out,
    v_inputs,
    v_gate,
    v_up,
    v_back,
    v_out_grad,
    v_in,
    v_gate_out,
    v_up_out,
    v_down_in,
    v_down_out,
    made_hidden,
    made_up,
    made_gate,
    sems,
):
    width = gate_in.shape[0]
    tokens = inputs.shape[0]
    hidden_steps = gate_pre.shape[1] // STEP
    model_steps = inputs.shape[1] // STEP
    copies = []

    def plan(pairs):
        made_here = []
        for source, target in pairs:
            copy = pltpu.make_async_copy(source, target, sems.at[sum(map(len, copies)) + len(made_here)])
            made_here.append(copy)
        copies.append(made_here)

    for step in range(hidden_steps):
        at = pl.ds(step * STEP, STEP)
        pairs = [
            (gate_pre.at[:, at], v_gate.at[:, at]),
            (up_pre.at[:, at], v_up.at[:, at]),
            (hidden_grad.at[:, at], v_back.at[:, at]),
            (gate_out.at[:, at], v_gate_out.at[:, at]),
            (up_out.at[:, at], v_up_out.at[:, at]),
            (down_in.at[:, at], v_down_in.at[:, at]),
        ]
        if step < model_steps:
            pairs += [
                (inputs.at[:, at], v_inputs.at[:, at]),
                (gate_in.at[:, at], v_in.at[pl.ds(0, width), at]),
                (up_in.at[:, at], v_in.at[pl.ds(width, width), at]),
                (out_grad.at[:, at], v_out_grad.at[:, at]),
                (down_out.at[:, at], v_down_out.at[:, at]),
            ]
        plan(pairs)

    def elementwise(step, part):
        target = step % 2
        for top in range(0, tokens, ROWS):
            for left in range(part * PART, (part + 1) * PART, 256):
                at = (slice(top, top + ROWS), slice(step * STEP + left, step * STEP + left + 256))
                put = (slice(top, top + ROWS), slice(left, left + 256))
                gate = v_gate[at].astype(jnp.float32)
                up = v_up[at].astype(jnp.float32)
                back = v_back[at].astype(jnp.float32)
                sig = 0.5 * jnp.tanh(0.5 * gate) + 0.5
                silu = gate * sig
                made_hidden[(target,) + put] = (silu * up).astype(jnp.bfloat16)
                made_up[(target,) + put] = (back * silu).astype(jnp.bfloat16)
                slope = sig + silu * (1.0 - sig)
                made_gate[(target,) + put] = (back * up * slope).astype(jnp.bfloat16)

    def add(low, high, base, values, first):
        value = lax.dot_general(base, values, NT, preferred_element_type=jnp.float32)
        if first:
            out[low * width : high * width, :] = value
        else:
            out[low * width : high * width, :] += value

    def hidden_dots(step, part):
        at = slice(step * STEP + part * PART, step * STEP + (part + 1) * PART)
        inner = (step % 2, slice(None), slice(part * PART, (part + 1) * PART))
        first = step == 0 and part == 0
        add(2, 3, v_gate_out[:, at], made_gate[inner], first)
        add(3, 4, v_up_out[:, at], made_up[inner], first)
        add(4, 5, v_down_in[:, at], made_hidden[inner], first)

    def model_dots(step, part):
        at = slice(step * STEP + part * PART, step * STEP + (part + 1) * PART)
        first = step == 0 and part == 0
        add(0, 2, v_in[:, at], v_inputs[:, at], first)
        add(5, 6, v_down_out[:, at], v_out_grad[:, at], first)

    for step in range(min(AHEAD, hidden_steps)):
        for copy in copies[step]:
            copy.start()
    for step in range(hidden_steps):
        if step + AHEAD < hidden_steps:
            for copy in copies[step + AHEAD]:
                copy.start()
        for copy in copies[step]:
            copy.wait()
        for part in range(STEP // PART):
            elementwise(step, part)
            if step >= 1:
                hidden_dots(step - 1, part)
            if step < model_steps:
                model_dots(step, part)
    for part in range(STEP // PART):
        hidden_dots(hidden_steps - 1, part)


def projections(*operands):
    inputs, gate_pre = operands[:2]
    width = operands[5].shape[0]
    tokens, model = inputs.shape
    hidden = gate_pre.shape[1]
    assert hidden % STEP == 0 and model % STEP == 0 and model <= hidden
    assert tokens % ROWS == 0
    steps = 6 * (hidden // STEP) + 5 * (model // STEP)
    bf16 = jnp.bfloat16
    return pl.pallas_call(
        project,
        out_shape=jax.ShapeDtypeStruct((6 * width, tokens), jnp.float32),
        in_specs=[pl.BlockSpec(memory_space=pltpu.HBM)] * len(operands),
        out_specs=pl.BlockSpec(memory_space=pltpu.VMEM),
        scratch_shapes=[
            pltpu.VMEM((tokens, model), bf16),
            pltpu.VMEM((tokens, hidden), bf16),
            pltpu.VMEM((tokens, hidden), bf16),
            pltpu.VMEM((tokens, hidden), bf16),
            pltpu.VMEM((tokens, model), bf16),
            pltpu.VMEM((2 * width, model), bf16),
            pltpu.VMEM((width, hidden), bf16),
            pltpu.VMEM((width, hidden), bf16),
            pltpu.VMEM((width, hidden), bf16),
            pltpu.VMEM((width, model), bf16),
            pltpu.VMEM((2, tokens, STEP), bf16),
            pltpu.VMEM((2, tokens, STEP), bf16),
            pltpu.VMEM((2, tokens, STEP), bf16),
            pltpu.SemaphoreType.DMA((steps,)),
        ],
        compiler_params=pltpu.CompilerParams(vmem_limit_bytes=60 * 2**20),
        cost_estimate=pl.CostEstimate(
            flops=6 * tokens * width * (model + hidden),
            bytes_accessed=2 * (2 * tokens * model + 3 * tokens * hidden),
            transcendentals=tokens * hidden,
        ),
        name="project",
    )(*operands)


def two_terms(value):
    high = value.astype(jnp.bfloat16)
    return high, (value - high.astype(jnp.float32)).astype(jnp.bfloat16)


def outer(chips, own, other, ids, out, summed, products):
    chip, core = lax.axis_index("dp"), lax.axis_index("mp")
    width = own.shape[0] // 6
    half = width // 2
    span = 3 * half // chips
    summed[...] = own[...] + other[...]
    own_label = 2 * chip + core
    tail_label = jnp.where(core == 1, 2 * chip - 1, -1)
    masks = [(ids[...] == label).astype(jnp.float32) for label in (tail_label, own_label)]
    lane = lax.broadcasted_iota(jnp.int32, (half, 2 * width), 1)
    for module, (left, right) in enumerate(((0, 2), (1, 3), (4, 5))):
        factor = summed[left * width : (left + 1) * width, :]
        high, low = two_terms(jnp.concatenate([factor * mask for mask in masks], axis=0))
        top, bottom = two_terms(summed[right * width : (right + 1) * width, :])
        product = None
        for one, two in ((high, top), (high, bottom), (low, top)):
            both = jnp.concatenate([two, two], axis=0)
            term = lax.dot_general(one, both, NT, preferred_element_type=jnp.float32)
            product = term if product is None else product + term
        products[module] = product
        for label in range(2):
            even = products[module, pl.ds(label * width, half, stride=2), :]
            odd = products[module, pl.ds(label * width + 1, half, stride=2), :]
            packed = jnp.where(lane < width, even, odd)
            row = 0
            while row < half:
                chip_to, inside = divmod(module * half + row, span)
                count = min(span - inside, half - row)
                put = slice(label * span + inside, label * span + inside + count)
                out[chip_to, put, :] = packed[row : row + count]
                row += count


def example_blocks(chips, own, other, ids):
    width = own.shape[0] // 6
    block = (3 * width // chips, 2 * width)
    return pl.pallas_call(
        functools.partial(outer, chips),
        out_shape=jax.ShapeDtypeStruct((chips,) + block, jnp.float32),
        in_specs=[pl.BlockSpec(memory_space=pltpu.VMEM)] * 3,
        out_specs=pl.BlockSpec(memory_space=pltpu.VMEM),
        scratch_shapes=[
            pltpu.VMEM(own.shape, jnp.float32),
            pltpu.VMEM((3, 2 * width, 2 * width), jnp.float32),
        ],
        compiler_params=pltpu.CompilerParams(vmem_limit_bytes=6 * 2**20),
        name="outer",
    )(own, other, ids)


def score(queries, swapped, received, out, rows):
    core = lax.axis_index("mp")
    chips, height, lanes = received.shape
    span = height // 2
    rows[: chips * height, :] = received[...].reshape(chips * height, lanes)
    rows[chips * height :, :] = jnp.zeros((8, lanes), jnp.float32)
    grads = []
    for at in range(span):
        own = rows[pl.ds(span + at, chips, stride=height), :]
        tail = rows[pl.ds(at, chips, stride=height), :]
        tail = jnp.concatenate([tail[1:], jnp.zeros_like(tail[:1])], axis=0)
        grads.append(own + tail)
    terms = jnp.concatenate(two_terms(jnp.concatenate(grads, axis=1)), axis=0)
    coords = queries.shape[1]
    first = core == 0
    mine = jnp.where(first, terms[:, :coords], terms[:, coords:])
    theirs = jnp.where(first, terms[:, coords:], terms[:, :coords])
    scores = lax.dot_general(mine, queries[...], NT, preferred_element_type=jnp.float32)
    scores += lax.dot_general(theirs, swapped[...], NT, preferred_element_type=jnp.float32)
    out[...] = scores[:chips] + scores[chips:]


def partial_scores(queries, swapped, received):
    chips, height, lanes = received.shape
    return pl.pallas_call(
        score,
        out_shape=jax.ShapeDtypeStruct((chips, queries.shape[0]), jnp.float32),
        in_specs=[pl.BlockSpec(memory_space=pltpu.VMEM)] * 3,
        out_specs=pl.BlockSpec(memory_space=pltpu.VMEM),
        scratch_shapes=[pltpu.VMEM((chips * height + 8, lanes), jnp.float32)],
        compiler_params=pltpu.CompilerParams(vmem_limit_bytes=6 * 2**20),
        name="score",
    )(queries, swapped, received)


def body(
    inputs,
    gate_pre,
    up_pre,
    hidden_grad,
    out_grad,
    example_ids,
    gate_in,
    gate_out,
    up_in,
    up_out,
    down_in,
    down_out,
    queries,
):
    chips = lax.axis_size("dp")
    swap = [(0, 1), (1, 0)]
    swapped = lax.ppermute(queries, "mp", swap)
    bases = [base.T for base in (gate_in, gate_out, up_in, up_out, down_in, down_out)]
    own = projections(inputs, gate_pre, up_pre, hidden_grad, out_grad, *bases)
    other = lax.ppermute(own, "mp", swap)
    blocks = example_blocks(chips, own, other, example_ids.reshape(1, -1))
    received = lax.all_to_all(blocks, "dp", split_axis=0, concat_axis=0, tiled=True)
    scores = lax.psum(partial_scores(queries, swapped, received), "dp")
    return lax.dynamic_slice_in_dim(scores, lax.axis_index("dp"), 1, 0)


def solution(mesh):
    placed = (
        P(("parts", "dp"), "mp"),
        P(("parts", "dp"), "mp"),
        P(("parts", "dp"), "mp"),
        P(("parts", "dp"), "mp"),
        P(("parts", "dp"), "mp"),
        P(("parts", "dp")),
        P("mp", None),
        P("mp", None),
        P("mp", None),
        P("mp", None),
        P("mp", None),
        P("mp", None),
        P(None, ("dp", "mp")),
    )
    return jax.shard_map(
        body, mesh=mesh, in_specs=placed, out_specs=P(("parts", "dp", "mp"), None), check_vma=False
    )
```

```python
import functools

import jax
import jax.numpy as jnp
from jax import lax
from jax.experimental import pallas as pl
from jax.experimental.pallas import tpu as pltpu
from jax.sharding import PartitionSpec as P

NT = (((1,), (1,)), ((), ()))
STEP = 1024
PART = 512
ROWS = 16
AHEAD = 3


def project(
    inputs,
    gate_pre,
    up_pre,
    hidden_grad,
    out_grad,
    gate_in,
    gate_out,
    up_in,
    up_out,
    down_in,
    down_out,
    out,
    v_inputs,
    v_gate,
    v_up,
    v_back,
    v_out_grad,
    v_in,
    v_gate_out,
    v_up_out,
    v_down_in,
    v_down_out,
    made_hidden,
    made_up,
    made_gate,
    sum_in,
    sums,
    sems,
):
    width = gate_in.shape[0]
    tokens = inputs.shape[0]
    hidden_steps = gate_pre.shape[1] // STEP
    model_steps = inputs.shape[1] // STEP
    copies = []

    def plan(pairs):
        made_here = []
        for source, target in pairs:
            copy = pltpu.make_async_copy(source, target, sems.at[sum(map(len, copies)) + len(made_here)])
            made_here.append(copy)
        copies.append(made_here)

    for step in range(hidden_steps):
        at = pl.ds(step * STEP, STEP)
        pairs = [
            (gate_pre.at[:, at], v_gate.at[:, at]),
            (up_pre.at[:, at], v_up.at[:, at]),
            (hidden_grad.at[:, at], v_back.at[:, at]),
            (gate_out.at[:, at], v_gate_out.at[:, at]),
            (up_out.at[:, at], v_up_out.at[:, at]),
            (down_in.at[:, at], v_down_in.at[:, at]),
        ]
        if step < model_steps:
            pairs += [
                (inputs.at[:, at], v_inputs.at[:, at]),
                (gate_in.at[:, at], v_in.at[pl.ds(0, width), at]),
                (up_in.at[:, at], v_in.at[pl.ds(width, width), at]),
                (out_grad.at[:, at], v_out_grad.at[:, at]),
                (down_out.at[:, at], v_down_out.at[:, at]),
            ]
        plan(pairs)

    def elementwise(step, part):
        target = step % 2
        for top in range(0, tokens, ROWS):
            for left in range(part * PART, (part + 1) * PART, 256):
                at = (slice(top, top + ROWS), slice(step * STEP + left, step * STEP + left + 256))
                put = (slice(top, top + ROWS), slice(left, left + 256))
                gate = v_gate[at].astype(jnp.float32)
                up = v_up[at].astype(jnp.float32)
                back = v_back[at].astype(jnp.float32)
                sig = 0.5 * jnp.tanh(0.5 * gate) + 0.5
                silu = gate * sig
                made_hidden[(target,) + put] = (silu * up).astype(jnp.bfloat16)
                made_up[(target,) + put] = (back * silu).astype(jnp.bfloat16)
                slope = sig + silu * (1.0 - sig)
                made_gate[(target,) + put] = (back * up * slope).astype(jnp.bfloat16)

    def add(total, values, base, first):
        value = lax.dot_general(values, base, NT, preferred_element_type=jnp.float32)
        if first:
            total[...] = value
        else:
            total[...] += value

    def hidden_dots(step, part):
        at = slice(step * STEP + part * PART, step * STEP + (part + 1) * PART)
        inner = (step % 2, slice(None), slice(part * PART, (part + 1) * PART))
        first = step == 0 and part == 0
        add(sums.at[0], made_gate[inner], v_gate_out[:, at], first)
        add(sums.at[1], made_up[inner], v_up_out[:, at], first)
        add(sums.at[2], made_hidden[inner], v_down_in[:, at], first)

    def model_dots(step, part):
        at = slice(step * STEP + part * PART, step * STEP + (part + 1) * PART)
        first = step == 0 and part == 0
        add(sum_in, v_inputs[:, at], v_in[:, at], first)
        add(sums.at[3], v_out_grad[:, at], v_down_out[:, at], first)

    for step in range(min(AHEAD, hidden_steps)):
        for copy in copies[step]:
            copy.start()
    for step in range(hidden_steps):
        if step + AHEAD < hidden_steps:
            for copy in copies[step + AHEAD]:
                copy.start()
        for copy in copies[step]:
            copy.wait()
        for part in range(STEP // PART):
            elementwise(step, part)
            if step >= 1:
                hidden_dots(step - 1, part)
            if step < model_steps:
                model_dots(step, part)
    for part in range(STEP // PART):
        hidden_dots(hidden_steps - 1, part)
    out[:, : 2 * width] = sum_in[...]
    out[:, 2 * width : 4 * width] = jnp.concatenate([sums[0], sums[1]], axis=1)
    out[:, 4 * width :] = jnp.concatenate([sums[2], sums[3]], axis=1)


def projections(*operands):
    inputs, gate_pre = operands[:2]
    width = operands[5].shape[0]
    tokens, model = inputs.shape
    hidden = gate_pre.shape[1]
    assert hidden % STEP == 0 and model % STEP == 0 and model <= hidden
    assert tokens % ROWS == 0
    steps = 6 * (hidden // STEP) + 5 * (model // STEP)
    bf16 = jnp.bfloat16
    return pl.pallas_call(
        project,
        out_shape=jax.ShapeDtypeStruct((tokens, 6 * width), jnp.float32),
        in_specs=[pl.BlockSpec(memory_space=pltpu.HBM)] * len(operands),
        out_specs=pl.BlockSpec(memory_space=pltpu.VMEM),
        scratch_shapes=[
            pltpu.VMEM((tokens, model), bf16),
            pltpu.VMEM((tokens, hidden), bf16),
            pltpu.VMEM((tokens, hidden), bf16),
            pltpu.VMEM((tokens, hidden), bf16),
            pltpu.VMEM((tokens, model), bf16),
            pltpu.VMEM((2 * width, model), bf16),
            pltpu.VMEM((width, hidden), bf16),
            pltpu.VMEM((width, hidden), bf16),
            pltpu.VMEM((width, hidden), bf16),
            pltpu.VMEM((width, model), bf16),
            pltpu.VMEM((2, tokens, STEP), bf16),
            pltpu.VMEM((2, tokens, STEP), bf16),
            pltpu.VMEM((2, tokens, STEP), bf16),
            pltpu.VMEM((tokens, 2 * width), jnp.float32),
            pltpu.VMEM((4, tokens, width), jnp.float32),
            pltpu.SemaphoreType.DMA((steps,)),
        ],
        compiler_params=pltpu.CompilerParams(vmem_limit_bytes=427 * 2**17),
        cost_estimate=pl.CostEstimate(
            flops=6 * tokens * width * (model + hidden),
            bytes_accessed=2 * (2 * tokens * model + 3 * tokens * hidden),
            transcendentals=tokens * hidden,
        ),
        name="project",
    )(*operands)


def two_terms(value):
    high = value.astype(jnp.bfloat16)
    return high, (value - high.astype(jnp.float32)).astype(jnp.bfloat16)


def outer(chips, own, other, ids, out, summed, products):
    chip, core = lax.axis_index("dp"), lax.axis_index("mp")
    width = own.shape[1] // 6
    half = width // 2
    span = 3 * half // chips
    summed[...] = (own[...] + other[...]).T
    own_label = 2 * chip + core
    tail_label = jnp.where(core == 1, 2 * chip - 1, -1)
    masks = [(ids[...] == label).astype(jnp.float32) for label in (tail_label, own_label)]
    lane = lax.broadcasted_iota(jnp.int32, (half, 2 * width), 1)
    for module, (left, right) in enumerate(((0, 2), (1, 3), (4, 5))):
        factor = summed[left * width : (left + 1) * width, :]
        high, low = two_terms(jnp.concatenate([factor * mask for mask in masks], axis=0))
        top, bottom = two_terms(summed[right * width : (right + 1) * width, :])
        product = None
        for one, two in ((high, top), (high, bottom), (low, top)):
            both = jnp.concatenate([two, two], axis=0)
            term = lax.dot_general(one, both, NT, preferred_element_type=jnp.float32)
            product = term if product is None else product + term
        products[module] = product
        for label in range(2):
            even = products[module, pl.ds(label * width, half, stride=2), :]
            odd = products[module, pl.ds(label * width + 1, half, stride=2), :]
            packed = jnp.where(lane < width, even, odd)
            row = 0
            while row < half:
                chip_to, inside = divmod(module * half + row, span)
                count = min(span - inside, half - row)
                put = slice(label * span + inside, label * span + inside + count)
                out[chip_to, put, :] = packed[row : row + count]
                row += count


def example_blocks(chips, own, other, ids):
    width = own.shape[1] // 6
    block = (3 * width // chips, 2 * width)
    return pl.pallas_call(
        functools.partial(outer, chips),
        out_shape=jax.ShapeDtypeStruct((chips,) + block, jnp.float32),
        in_specs=[pl.BlockSpec(memory_space=pltpu.VMEM)] * 3,
        out_specs=pl.BlockSpec(memory_space=pltpu.VMEM),
        scratch_shapes=[
            pltpu.VMEM(own.shape[::-1], jnp.float32),
            pltpu.VMEM((3, 2 * width, 2 * width), jnp.float32),
        ],
        compiler_params=pltpu.CompilerParams(vmem_limit_bytes=6 * 2**20),
        name="outer",
    )(own, other, ids)


def score(queries, swapped, received, out, rows):
    core = lax.axis_index("mp")
    chips, height, lanes = received.shape
    span = height // 2
    rows[: chips * height, :] = received[...].reshape(chips * height, lanes)
    rows[chips * height :, :] = jnp.zeros((8, lanes), jnp.float32)
    grads = []
    for at in range(span):
        own = rows[pl.ds(span + at, chips, stride=height), :]
        tail = rows[pl.ds(at, chips, stride=height), :]
        tail = jnp.concatenate([tail[1:], jnp.zeros_like(tail[:1])], axis=0)
        grads.append(own + tail)
    terms = jnp.concatenate(two_terms(jnp.concatenate(grads, axis=1)), axis=0)
    coords = queries.shape[1]
    first = core == 0
    mine = jnp.where(first, terms[:, :coords], terms[:, coords:])
    theirs = jnp.where(first, terms[:, coords:], terms[:, :coords])
    scores = lax.dot_general(mine, queries[...], NT, preferred_element_type=jnp.float32)
    scores += lax.dot_general(theirs, swapped[...], NT, preferred_element_type=jnp.float32)
    out[...] = scores[:chips] + scores[chips:]


def partial_scores(queries, swapped, received):
    chips, height, lanes = received.shape
    return pl.pallas_call(
        score,
        out_shape=jax.ShapeDtypeStruct((chips, queries.shape[0]), jnp.float32),
        in_specs=[pl.BlockSpec(memory_space=pltpu.VMEM)] * 3,
        out_specs=pl.BlockSpec(memory_space=pltpu.VMEM),
        scratch_shapes=[pltpu.VMEM((chips * height + 8, lanes), jnp.float32)],
        compiler_params=pltpu.CompilerParams(vmem_limit_bytes=6 * 2**20),
        name="score",
    )(queries, swapped, received)


def body(
    inputs,
    gate_pre,
    up_pre,
    hidden_grad,
    out_grad,
    example_ids,
    gate_in,
    gate_out,
    up_in,
    up_out,
    down_in,
    down_out,
    queries,
):
    chips = lax.axis_size("dp")
    swap = [(0, 1), (1, 0)]
    swapped = lax.ppermute(queries, "mp", swap)
    bases = [base.T for base in (gate_in, gate_out, up_in, up_out, down_in, down_out)]
    own = projections(inputs, gate_pre, up_pre, hidden_grad, out_grad, *bases)
    other = lax.ppermute(own, "mp", swap)
    blocks = example_blocks(chips, own, other, example_ids.reshape(1, -1))
    received = lax.all_to_all(blocks, "dp", split_axis=0, concat_axis=0, tiled=True)
    scores = partial_scores(queries, swapped, received)[:, None]
    pieces = lax.all_to_all(scores, "dp", split_axis=0, concat_axis=0, tiled=True)
    return jnp.sum(pieces, axis=0)


def solution(mesh):
    placed = (
        P(("parts", "dp"), "mp"),
        P(("parts", "dp"), "mp"),
        P(("parts", "dp"), "mp"),
        P(("parts", "dp"), "mp"),
        P(("parts", "dp"), "mp"),
        P(("parts", "dp")),
        P("mp", None),
        P("mp", None),
        P("mp", None),
        P("mp", None),
        P("mp", None),
        P("mp", None),
        P(None, ("dp", "mp")),
    )
    return jax.shard_map(
        body, mesh=mesh, in_specs=placed, out_specs=P(("parts", "dp", "mp"), None), check_vma=False
    )
```

```python
import functools

import jax
import jax.numpy as jnp
from jax import lax
from jax.experimental import pallas as pl
from jax.experimental.pallas import tpu as pltpu
from jax.sharding import PartitionSpec as P

NT = (((1,), (1,)), ((), ()))
STEP = 512
ROWS = 16
AHEAD = 6


def project(
    inputs,
    gate_pre,
    up_pre,
    hidden_grad,
    out_grad,
    gate_in,
    gate_out,
    up_in,
    up_out,
    down_in,
    down_out,
    out,
    v_inputs,
    v_gate,
    v_up,
    v_back,
    v_out_grad,
    v_in,
    v_gate_out,
    v_up_out,
    v_down_in,
    v_down_out,
    tanhs,
    made_hidden,
    made_up,
    made_gate,
    sum_in,
    sums,
    sems,
):
    width = gate_in.shape[0]
    tokens = inputs.shape[0]
    hidden_steps = gate_pre.shape[1] // STEP
    model_steps = inputs.shape[1] // STEP
    copies = []
    for step in range(hidden_steps + model_steps):
        if step < hidden_steps:
            at = pl.ds(step * STEP, STEP)
            pairs = [
                (gate_pre.at[:, at], v_gate.at[:, at]),
                (up_pre.at[:, at], v_up.at[:, at]),
                (hidden_grad.at[:, at], v_back.at[:, at]),
                (gate_out.at[:, at], v_gate_out.at[:, at]),
                (up_out.at[:, at], v_up_out.at[:, at]),
                (down_in.at[:, at], v_down_in.at[:, at]),
            ]
        else:
            at = pl.ds((step - hidden_steps) * STEP, STEP)
            pairs = [
                (inputs.at[:, at], v_inputs.at[:, at]),
                (gate_in.at[:, at], v_in.at[pl.ds(0, width), at]),
                (up_in.at[:, at], v_in.at[pl.ds(width, width), at]),
                (out_grad.at[:, at], v_out_grad.at[:, at]),
                (down_out.at[:, at], v_down_out.at[:, at]),
            ]
        first = sum(map(len, copies))
        copies.append(
            [
                pltpu.make_async_copy(source, target, sems.at[first + i])
                for i, (source, target) in enumerate(pairs)
            ]
        )

    def columns(step):
        return slice(step * STEP, (step + 1) * STEP)

    def squash(step, rows):
        half = 0.5 * v_gate[rows, columns(step)].astype(jnp.float32)
        tanhs[step % 2, rows, :] = jnp.tanh(half)

    def products(step, rows):
        at = (rows, columns(step))
        put = (step % 2, rows, slice(None))
        tanh = tanhs[put]
        up = v_up[at].astype(jnp.float32)
        back = v_back[at].astype(jnp.float32)
        plus = 1.0 + tanh
        silu = 0.5 * v_gate[at].astype(jnp.float32) * plus
        made_hidden[put] = (silu * up).astype(jnp.bfloat16)
        made_up[put] = (back * silu).astype(jnp.bfloat16)
        made_gate[put] = (back * up * (plus + silu * (1.0 - tanh))).astype(jnp.bfloat16)

    def add(total, values, base, first):
        value = lax.dot_general(values, base, NT, preferred_element_type=jnp.float32)
        if first:
            total[...] = value
        else:
            total[...] += value

    def hidden_dot(step, which):
        made = (made_gate, made_up, made_hidden)[which]
        base = (v_gate_out, v_up_out, v_down_in)[which]
        add(sums.at[which], made[step % 2], base[:, columns(step)], step == 0)

    def model_dots(step):
        at = columns(step)
        add(sum_in, v_inputs[:, at], v_in[:, at], step == 0)
        add(sums.at[3], v_out_grad[:, at], v_down_out[:, at], step == 0)

    steps = hidden_steps + model_steps
    for step in range(AHEAD):
        for copy in copies[step]:
            copy.start()
    for block in range(steps):
        if block + AHEAD < steps:
            for copy in copies[block + AHEAD]:
                copy.start()
        for copy in copies[block]:
            copy.wait()
        groups = tokens // ROWS
        for group in range(groups):
            rows = slice(group * ROWS, (group + 1) * ROWS)
            if 0 <= block - 2 < hidden_steps and group % (groups // 3) == 0:
                hidden_dot(block - 2, group // (groups // 3))
            if 0 <= block - 1 < hidden_steps:
                products(block - 1, rows)
            if block < hidden_steps:
                squash(block, rows)
        if block >= hidden_steps:
            model_dots(block - hidden_steps)
    out[:, : 2 * width] = sum_in[...]
    out[:, 2 * width : 4 * width] = jnp.concatenate([0.5 * sums[0], sums[1]], axis=1)
    out[:, 4 * width :] = jnp.concatenate([sums[2], sums[3]], axis=1)


def projections(*operands):
    inputs, gate_pre = operands[:2]
    width = operands[5].shape[0]
    tokens, model = inputs.shape
    hidden = gate_pre.shape[1]
    assert hidden % STEP == 0 and model % STEP == 0 and model >= 2 * STEP
    assert tokens % (3 * ROWS) == 0
    steps = 6 * (hidden // STEP) + 5 * (model // STEP)
    bf16 = jnp.bfloat16
    return pl.pallas_call(
        project,
        out_shape=jax.ShapeDtypeStruct((tokens, 6 * width), jnp.float32),
        in_specs=[pl.BlockSpec(memory_space=pltpu.HBM)] * len(operands),
        out_specs=pl.BlockSpec(memory_space=pltpu.VMEM),
        scratch_shapes=[
            pltpu.VMEM((tokens, model), bf16),
            pltpu.VMEM((tokens, hidden), bf16),
            pltpu.VMEM((tokens, hidden), bf16),
            pltpu.VMEM((tokens, hidden), bf16),
            pltpu.VMEM((tokens, model), bf16),
            pltpu.VMEM((2 * width, model), bf16),
            pltpu.VMEM((width, hidden), bf16),
            pltpu.VMEM((width, hidden), bf16),
            pltpu.VMEM((width, hidden), bf16),
            pltpu.VMEM((width, model), bf16),
            pltpu.VMEM((2, tokens, STEP), jnp.float32),
            pltpu.VMEM((2, tokens, STEP), bf16),
            pltpu.VMEM((2, tokens, STEP), bf16),
            pltpu.VMEM((2, tokens, STEP), bf16),
            pltpu.VMEM((tokens, 2 * width), jnp.float32),
            pltpu.VMEM((4, tokens, width), jnp.float32),
            pltpu.SemaphoreType.DMA((steps,)),
        ],
        compiler_params=pltpu.CompilerParams(vmem_limit_bytes=427 * 2**17),
        cost_estimate=pl.CostEstimate(
            flops=6 * tokens * width * (model + hidden),
            bytes_accessed=2 * (2 * tokens * model + 3 * tokens * hidden),
            transcendentals=tokens * hidden,
        ),
        name="project",
    )(*operands)


def two_terms(value):
    high = value.astype(jnp.bfloat16)
    return high, (value - high.astype(jnp.float32)).astype(jnp.bfloat16)


def outer(chips, own, other, ids, out, summed, products):
    chip, core = lax.axis_index("dp"), lax.axis_index("mp")
    width = own.shape[1] // 6
    half = width // 2
    span = 3 * half // chips
    summed[...] = (own[...] + other[...]).T
    own_label = 2 * chip + core
    tail_label = jnp.where(core == 1, 2 * chip - 1, -1)
    masks = [(ids[...] == label).astype(jnp.float32) for label in (tail_label, own_label)]
    lane = lax.broadcasted_iota(jnp.int32, (half, 2 * width), 1)
    for module, (left, right) in enumerate(((0, 2), (1, 3), (4, 5))):
        factor = summed[left * width : (left + 1) * width, :]
        high, low = two_terms(jnp.concatenate([factor * mask for mask in masks], axis=0))
        top, bottom = two_terms(summed[right * width : (right + 1) * width, :])
        product = None
        for one, two in ((high, top), (high, bottom), (low, top)):
            both = jnp.concatenate([two, two], axis=0)
            term = lax.dot_general(one, both, NT, preferred_element_type=jnp.float32)
            product = term if product is None else product + term
        products[module] = product
        for label in range(2):
            even = products[module, pl.ds(label * width, half, stride=2), :]
            odd = products[module, pl.ds(label * width + 1, half, stride=2), :]
            packed = jnp.where(lane < width, even, odd)
            row = 0
            while row < half:
                chip_to, inside = divmod(module * half + row, span)
                count = min(span - inside, half - row)
                put = slice(label * span + inside, label * span + inside + count)
                out[chip_to, put, :] = packed[row : row + count]
                row += count


def example_blocks(chips, own, other, ids):
    width = own.shape[1] // 6
    block = (3 * width // chips, 2 * width)
    return pl.pallas_call(
        functools.partial(outer, chips),
        out_shape=jax.ShapeDtypeStruct((chips,) + block, jnp.float32),
        in_specs=[pl.BlockSpec(memory_space=pltpu.VMEM)] * 3,
        out_specs=pl.BlockSpec(memory_space=pltpu.VMEM),
        scratch_shapes=[
            pltpu.VMEM(own.shape[::-1], jnp.float32),
            pltpu.VMEM((3, 2 * width, 2 * width), jnp.float32),
        ],
        compiler_params=pltpu.CompilerParams(vmem_limit_bytes=6 * 2**20),
        name="outer",
    )(own, other, ids)


def score(queries, swapped, received, out, rows):
    core = lax.axis_index("mp")
    chips, height, lanes = received.shape
    span = height // 2
    rows[: chips * height, :] = received[...].reshape(chips * height, lanes)
    rows[chips * height :, :] = jnp.zeros((8, lanes), jnp.float32)
    grads = []
    for at in range(span):
        own = rows[pl.ds(span + at, chips, stride=height), :]
        tail = rows[pl.ds(at, chips, stride=height), :]
        tail = jnp.concatenate([tail[1:], jnp.zeros_like(tail[:1])], axis=0)
        grads.append(own + tail)
    terms = jnp.concatenate(two_terms(jnp.concatenate(grads, axis=1)), axis=0)
    coords = queries.shape[1]
    first = core == 0
    mine = jnp.where(first, terms[:, :coords], terms[:, coords:])
    theirs = jnp.where(first, terms[:, coords:], terms[:, :coords])
    scores = lax.dot_general(mine, queries[...], NT, preferred_element_type=jnp.float32)
    scores += lax.dot_general(theirs, swapped[...], NT, preferred_element_type=jnp.float32)
    out[...] = scores[:chips] + scores[chips:]


def partial_scores(queries, swapped, received):
    chips, height, lanes = received.shape
    return pl.pallas_call(
        score,
        out_shape=jax.ShapeDtypeStruct((chips, queries.shape[0]), jnp.float32),
        in_specs=[pl.BlockSpec(memory_space=pltpu.VMEM)] * 3,
        out_specs=pl.BlockSpec(memory_space=pltpu.VMEM),
        scratch_shapes=[pltpu.VMEM((chips * height + 8, lanes), jnp.float32)],
        compiler_params=pltpu.CompilerParams(vmem_limit_bytes=6 * 2**20),
        name="score",
    )(queries, swapped, received)


def body(
    inputs,
    gate_pre,
    up_pre,
    hidden_grad,
    out_grad,
    example_ids,
    gate_in,
    gate_out,
    up_in,
    up_out,
    down_in,
    down_out,
    queries,
):
    chips = lax.axis_size("dp")
    swap = [(0, 1), (1, 0)]
    swapped = lax.ppermute(queries, "mp", swap)
    bases = [base.T for base in (gate_in, gate_out, up_in, up_out, down_in, down_out)]
    own = projections(inputs, gate_pre, up_pre, hidden_grad, out_grad, *bases)
    other = lax.ppermute(own, "mp", swap)
    blocks = example_blocks(chips, own, other, example_ids.reshape(1, -1))
    received = lax.all_to_all(blocks, "dp", split_axis=0, concat_axis=0, tiled=True)
    scores = partial_scores(queries, swapped, received)[:, None]
    pieces = lax.all_to_all(scores, "dp", split_axis=0, concat_axis=0, tiled=True)
    return jnp.sum(pieces, axis=0)


def solution(mesh):
    placed = (
        P(("parts", "dp"), "mp"),
        P(("parts", "dp"), "mp"),
        P(("parts", "dp"), "mp"),
        P(("parts", "dp"), "mp"),
        P(("parts", "dp"), "mp"),
        P(("parts", "dp")),
        P("mp", None),
        P("mp", None),
        P("mp", None),
        P("mp", None),
        P("mp", None),
        P("mp", None),
        P(None, ("dp", "mp")),
    )
    return jax.shard_map(
        body, mesh=mesh, in_specs=placed, out_specs=P(("parts", "dp", "mp"), None), check_vma=False
    )
```

```python
import functools

import jax
import jax.numpy as jnp
from jax import lax
from jax.experimental import pallas as pl
from jax.experimental.pallas import tpu as pltpu
from jax.sharding import PartitionSpec as P

NT = (((1,), (1,)), ((), ()))
PIECE = 2048
ROWS = 16
DEPTH = 512


def project(
    inputs,
    gate_pre,
    up_pre,
    hidden_grad,
    out_grad,
    gate_in,
    gate_out,
    up_in,
    up_out,
    down_in,
    down_out,
    out,
    v_inputs,
    v_gate,
    v_up,
    v_back,
    v_out_grad,
    v_in,
    v_gate_out,
    v_up_out,
    v_down_in,
    v_down_out,
    made_hidden,
    made_up,
    made_gate,
    sum_in,
    sums,
    sems,
):
    width = gate_in.shape[0]
    tokens = inputs.shape[0]
    hidden, model = gate_pre.shape[1], inputs.shape[1]
    copies = []

    def copy(source, target):
        copies.append(pltpu.make_async_copy(source, target, sems.at[len(copies)]))
        return copies[-1]

    def whole(*pairs):
        return [copy(source, target) for source, target in pairs]

    def piece(at, *pairs):
        return [copy(source.at[:, at], target.at[:, at]) for source, target in pairs]

    edges = [0] + list(range(PIECE // 2, hidden, PIECE)) + [hidden]
    pieces = [slice(low, high) for low, high in zip(edges, edges[1:])]
    activations = ((gate_pre, v_gate), (up_pre, v_up), (hidden_grad, v_back))
    arrivals = [piece(pl.ds(0, pieces[0].stop), *activations)]
    hidden_bases = whole((gate_out, v_gate_out), (up_out, v_up_out), (down_in, v_down_in))
    for at in pieces[1:]:
        arrivals.append(piece(pl.ds(at.start, at.stop - at.start), *activations))
    for_inputs = whole(
        (gate_in, v_in.at[pl.ds(0, width), :]),
        (up_in, v_in.at[pl.ds(width, width), :]),
        (inputs, v_inputs),
    )
    for_out_grad = whole((down_out, v_down_out))
    halves = [slice(0, model // 2), slice(model // 2, model)]
    for_halves = [piece(pl.ds(at.start, model // 2), (out_grad, v_out_grad)) for at in halves]

    def products(top, low, slot, left):
        rows = slice(top, top + ROWS)
        at = (rows, slice(low, low + 256))
        put = (slot, rows, slice(left, left + 256))
        half = 0.5 * v_gate[at].astype(jnp.float32)
        up = v_up[at].astype(jnp.float32)
        back = v_back[at].astype(jnp.float32)
        tanh = jnp.tanh(half)
        plus = 1.0 + tanh
        silu = half * plus
        made_hidden[put] = (silu * up).astype(jnp.bfloat16)
        made_up[put] = (back * silu).astype(jnp.bfloat16)
        made_gate[put] = (back * up * (plus + silu * (1.0 - tanh))).astype(jnp.bfloat16)

    started = set()

    def add(name, total, values, base):
        value = lax.dot_general(values, base, NT, preferred_element_type=jnp.float32)
        if name in started:
            total[...] += value
        else:
            total[...] = value
        started.add(name)

    def hidden_dots(low, slot, left):
        at = slice(low, low + DEPTH)
        inner = (slot, slice(None), slice(left, left + DEPTH))
        add("gate", sums.at[0], made_gate[inner], v_gate_out[:, at])
        add("up", sums.at[1], made_up[inner], v_up_out[:, at])
        add("hidden", sums.at[2], made_hidden[inner], v_down_in[:, at])

    for each in copies:
        each.start()
    for index, at in enumerate(pieces):
        for each in arrivals[index]:
            each.wait()
        if index == 1:
            for each in hidden_bases:
                each.wait()
        length = at.stop - at.start
        before = pieces[index - 1] if index > 0 else slice(0, 0)
        for left in range(0, length, DEPTH):
            for top in range(0, tokens, ROWS):
                for inner in range(left, left + DEPTH, 256):
                    products(top, at.start + inner, index % 2, inner)
            if before.start + left < before.stop:
                hidden_dots(before.start + left, (index - 1) % 2, left)
    for each in for_inputs:
        each.wait()
    last = pieces[-1]
    for left in range(0, last.stop - last.start, DEPTH):
        hidden_dots(last.start + left, (len(pieces) - 1) % 2, left)
    add("inputs", sum_in, v_inputs[...], v_in[...])
    for each in for_out_grad:
        each.wait()
    for arrival, at in zip(for_halves, halves):
        for each in arrival:
            each.wait()
        add("out_grad", sums.at[3], v_out_grad[:, at], v_down_out[:, at])
    out[:, : 2 * width] = sum_in[...]
    out[:, 2 * width : 4 * width] = jnp.concatenate([0.5 * sums[0], sums[1]], axis=1)
    out[:, 4 * width :] = jnp.concatenate([sums[2], sums[3]], axis=1)


def projections(*operands):
    inputs, gate_pre = operands[:2]
    width = operands[5].shape[0]
    tokens, model = inputs.shape
    hidden = gate_pre.shape[1]
    assert hidden % PIECE == PIECE // 2 and model % (2 * DEPTH) == 0 and tokens % ROWS == 0
    copies = 3 * (hidden // PIECE + 1) + 9
    bf16 = jnp.bfloat16
    return pl.pallas_call(
        project,
        out_shape=jax.ShapeDtypeStruct((tokens, 6 * width), jnp.float32),
        in_specs=[pl.BlockSpec(memory_space=pltpu.HBM)] * len(operands),
        out_specs=pl.BlockSpec(memory_space=pltpu.VMEM),
        scratch_shapes=[
            pltpu.VMEM((tokens, model), bf16),
            pltpu.VMEM((tokens, hidden), bf16),
            pltpu.VMEM((tokens, hidden), bf16),
            pltpu.VMEM((tokens, hidden), bf16),
            pltpu.VMEM((tokens, model), bf16),
            pltpu.VMEM((2 * width, model), bf16),
            pltpu.VMEM((width, hidden), bf16),
            pltpu.VMEM((width, hidden), bf16),
            pltpu.VMEM((width, hidden), bf16),
            pltpu.VMEM((width, model), bf16),
            pltpu.VMEM((2, tokens, PIECE), bf16),
            pltpu.VMEM((2, tokens, PIECE), bf16),
            pltpu.VMEM((2, tokens, PIECE), bf16),
            pltpu.VMEM((tokens, 2 * width), jnp.float32),
            pltpu.VMEM((4, tokens, width), jnp.float32),
            pltpu.SemaphoreType.DMA((copies,)),
        ],
        compiler_params=pltpu.CompilerParams(vmem_limit_bytes=427 * 2**17),
        cost_estimate=pl.CostEstimate(
            flops=6 * tokens * width * (model + hidden),
            bytes_accessed=2 * (2 * tokens * model + 3 * tokens * hidden),
            transcendentals=tokens * hidden,
        ),
        name="project",
    )(*operands)


def two_terms(value):
    high = value.astype(jnp.bfloat16)
    return high, (value - high.astype(jnp.float32)).astype(jnp.bfloat16)


def outer(chips, own, other, ids, out, summed, products):
    chip, core = lax.axis_index("dp"), lax.axis_index("mp")
    width = own.shape[1] // 6
    half = width // 2
    span = 3 * half // chips
    summed[...] = (own[...] + other[...]).T
    own_label = 2 * chip + core
    tail_label = jnp.where(core == 1, 2 * chip - 1, -1)
    masks = [(ids[...] == label).astype(jnp.float32) for label in (tail_label, own_label)]
    lane = lax.broadcasted_iota(jnp.int32, (half, 2 * width), 1)
    for module, (left, right) in enumerate(((0, 2), (1, 3), (4, 5))):
        factor = summed[left * width : (left + 1) * width, :]
        high, low = two_terms(jnp.concatenate([factor * mask for mask in masks], axis=0))
        top, bottom = two_terms(summed[right * width : (right + 1) * width, :])
        product = None
        for one, two in ((high, top), (high, bottom), (low, top)):
            both = jnp.concatenate([two, two], axis=0)
            term = lax.dot_general(one, both, NT, preferred_element_type=jnp.float32)
            product = term if product is None else product + term
        products[module] = product
        for label in range(2):
            even = products[module, pl.ds(label * width, half, stride=2), :]
            odd = products[module, pl.ds(label * width + 1, half, stride=2), :]
            packed = jnp.where(lane < width, even, odd)
            row = 0
            while row < half:
                chip_to, inside = divmod(module * half + row, span)
                count = min(span - inside, half - row)
                put = slice(label * span + inside, label * span + inside + count)
                out[chip_to, put, :] = packed[row : row + count]
                row += count


def example_blocks(chips, own, other, ids):
    width = own.shape[1] // 6
    block = (3 * width // chips, 2 * width)
    return pl.pallas_call(
        functools.partial(outer, chips),
        out_shape=jax.ShapeDtypeStruct((chips,) + block, jnp.float32),
        in_specs=[pl.BlockSpec(memory_space=pltpu.VMEM)] * 3,
        out_specs=pl.BlockSpec(memory_space=pltpu.VMEM),
        scratch_shapes=[
            pltpu.VMEM(own.shape[::-1], jnp.float32),
            pltpu.VMEM((3, 2 * width, 2 * width), jnp.float32),
        ],
        compiler_params=pltpu.CompilerParams(vmem_limit_bytes=6 * 2**20),
        name="outer",
    )(own, other, ids)


def score(queries, swapped, received, out, rows):
    core = lax.axis_index("mp")
    chips, height, lanes = received.shape
    span = height // 2
    rows[: chips * height, :] = received[...].reshape(chips * height, lanes)
    rows[chips * height :, :] = jnp.zeros((8, lanes), jnp.float32)
    grads = []
    for at in range(span):
        own = rows[pl.ds(span + at, chips, stride=height), :]
        tail = rows[pl.ds(at, chips, stride=height), :]
        tail = jnp.concatenate([tail[1:], jnp.zeros_like(tail[:1])], axis=0)
        grads.append(own + tail)
    terms = jnp.concatenate(two_terms(jnp.concatenate(grads, axis=1)), axis=0)
    coords = queries.shape[1]
    first = core == 0
    mine = jnp.where(first, terms[:, :coords], terms[:, coords:])
    theirs = jnp.where(first, terms[:, coords:], terms[:, :coords])
    scores = lax.dot_general(mine, queries[...], NT, preferred_element_type=jnp.float32)
    scores += lax.dot_general(theirs, swapped[...], NT, preferred_element_type=jnp.float32)
    out[...] = scores[:chips] + scores[chips:]


def partial_scores(queries, swapped, received):
    chips, height, lanes = received.shape
    return pl.pallas_call(
        score,
        out_shape=jax.ShapeDtypeStruct((chips, queries.shape[0]), jnp.float32),
        in_specs=[pl.BlockSpec(memory_space=pltpu.VMEM)] * 3,
        out_specs=pl.BlockSpec(memory_space=pltpu.VMEM),
        scratch_shapes=[pltpu.VMEM((chips * height + 8, lanes), jnp.float32)],
        compiler_params=pltpu.CompilerParams(vmem_limit_bytes=6 * 2**20),
        name="score",
    )(queries, swapped, received)


def body(
    inputs,
    gate_pre,
    up_pre,
    hidden_grad,
    out_grad,
    example_ids,
    gate_in,
    gate_out,
    up_in,
    up_out,
    down_in,
    down_out,
    queries,
):
    chips = lax.axis_size("dp")
    swap = [(0, 1), (1, 0)]
    swapped = lax.ppermute(queries, "mp", swap)
    bases = [base.T for base in (gate_in, gate_out, up_in, up_out, down_in, down_out)]
    own = projections(inputs, gate_pre, up_pre, hidden_grad, out_grad, *bases)
    other = lax.ppermute(own, "mp", swap)
    blocks = example_blocks(chips, own, other, example_ids.reshape(1, -1))
    received = lax.all_to_all(blocks, "dp", split_axis=0, concat_axis=0, tiled=True)
    scores = partial_scores(queries, swapped, received)[:, None]
    pieces = lax.all_to_all(scores, "dp", split_axis=0, concat_axis=0, tiled=True)
    return jnp.sum(pieces, axis=0)


def solution(mesh):
    placed = (
        P(("parts", "dp"), "mp"),
        P(("parts", "dp"), "mp"),
        P(("parts", "dp"), "mp"),
        P(("parts", "dp"), "mp"),
        P(("parts", "dp"), "mp"),
        P(("parts", "dp")),
        P("mp", None),
        P("mp", None),
        P("mp", None),
        P("mp", None),
        P("mp", None),
        P("mp", None),
        P(None, ("dp", "mp")),
    )
    return jax.shard_map(
        body, mesh=mesh, in_specs=placed, out_specs=P(("parts", "dp", "mp"), None), check_vma=False
    )
```

```python
import functools

import jax
import jax.numpy as jnp
from jax import lax
from jax.experimental import pallas as pl
from jax.experimental.pallas import tpu as pltpu
from jax.sharding import PartitionSpec as P

NT = (((1,), (1,)), ((), ()))
STEP = 1024
PART = 512
ROWS = 16
AHEAD = 2


def project(
    inputs,
    gate_pre,
    up_pre,
    hidden_grad,
    out_grad,
    gate_in,
    gate_out,
    up_in,
    up_out,
    down_in,
    down_out,
    out,
    v_inputs,
    v_gate,
    v_up,
    v_back,
    v_out_grad,
    v_in,
    v_gate_out,
    v_up_out,
    v_down_in,
    v_down_out,
    made_hidden,
    made_up,
    made_gate,
    sum_in,
    sums,
    sems,
):
    width = gate_in.shape[0]
    tokens = inputs.shape[0]
    hidden_steps = gate_pre.shape[1] // STEP
    model_steps = inputs.shape[1] // STEP
    copies = []

    def plan(pairs):
        made_here = []
        for source, target in pairs:
            copy = pltpu.make_async_copy(source, target, sems.at[sum(map(len, copies)) + len(made_here)])
            made_here.append(copy)
        copies.append(made_here)

    for step in range(hidden_steps):
        at = pl.ds(step * STEP, STEP)
        pairs = [
            (gate_pre.at[:, at], v_gate.at[:, at]),
            (up_pre.at[:, at], v_up.at[:, at]),
            (hidden_grad.at[:, at], v_back.at[:, at]),
            (gate_out.at[:, at], v_gate_out.at[:, at]),
            (up_out.at[:, at], v_up_out.at[:, at]),
            (down_in.at[:, at], v_down_in.at[:, at]),
        ]
        if step < model_steps:
            pairs += [
                (inputs.at[:, at], v_inputs.at[:, at]),
                (gate_in.at[:, at], v_in.at[pl.ds(0, width), at]),
                (up_in.at[:, at], v_in.at[pl.ds(width, width), at]),
                (out_grad.at[:, at], v_out_grad.at[:, at]),
                (down_out.at[:, at], v_down_out.at[:, at]),
            ]
        plan(pairs)

    def elementwise(step, part):
        target = step % 2
        for top in range(0, tokens, ROWS):
            for left in range(part * PART, (part + 1) * PART, 256):
                at = (slice(top, top + ROWS), slice(step * STEP + left, step * STEP + left + 256))
                put = (slice(top, top + ROWS), slice(left, left + 256))
                gate = v_gate[at].astype(jnp.float32)
                up = v_up[at].astype(jnp.float32)
                back = v_back[at].astype(jnp.float32)
                half = 0.5 * gate
                tanh = jnp.tanh(half)
                plus = 1.0 + tanh
                silu = half * plus
                made_hidden[(target,) + put] = (silu * up).astype(jnp.bfloat16)
                made_up[(target,) + put] = (back * silu).astype(jnp.bfloat16)
                slope = plus + silu * (1.0 - tanh)
                made_gate[(target,) + put] = (back * up * slope).astype(jnp.bfloat16)

    def add(total, values, base, first):
        value = lax.dot_general(values, base, NT, preferred_element_type=jnp.float32)
        if first:
            total[...] = value
        else:
            total[...] += value

    def hidden_dots(step, part):
        at = slice(step * STEP + part * PART, step * STEP + (part + 1) * PART)
        inner = (step % 2, slice(None), slice(part * PART, (part + 1) * PART))
        first = step == 0 and part == 0
        add(sums.at[0], made_gate[inner], v_gate_out[:, at], first)
        add(sums.at[1], made_up[inner], v_up_out[:, at], first)
        add(sums.at[2], made_hidden[inner], v_down_in[:, at], first)

    def model_dots(step, part):
        at = slice(step * STEP + part * PART, step * STEP + (part + 1) * PART)
        first = step == 0 and part == 0
        add(sum_in, v_inputs[:, at], v_in[:, at], first)
        add(sums.at[3], v_out_grad[:, at], v_down_out[:, at], first)

    for step in range(min(AHEAD, hidden_steps)):
        for copy in copies[step]:
            copy.start()
    for step in range(hidden_steps):
        if step + AHEAD < hidden_steps:
            for copy in copies[step + AHEAD]:
                copy.start()
        for copy in copies[step]:
            copy.wait()
        for part in range(STEP // PART):
            elementwise(step, part)
            if step >= 1:
                hidden_dots(step - 1, part)
            if step < model_steps:
                model_dots(step, part)
    for part in range(STEP // PART):
        hidden_dots(hidden_steps - 1, part)
    out[:, : 2 * width] = sum_in[...]
    out[:, 2 * width : 4 * width] = jnp.concatenate([0.5 * sums[0], sums[1]], axis=1)
    out[:, 4 * width :] = jnp.concatenate([sums[2], sums[3]], axis=1)


def projections(*operands):
    inputs, gate_pre = operands[:2]
    width = operands[5].shape[0]
    tokens, model = inputs.shape
    hidden = gate_pre.shape[1]
    assert hidden % STEP == 0 and model % STEP == 0 and model <= hidden
    assert tokens % ROWS == 0
    steps = 6 * (hidden // STEP) + 5 * (model // STEP)
    bf16 = jnp.bfloat16
    return pl.pallas_call(
        project,
        out_shape=jax.ShapeDtypeStruct((tokens, 6 * width), jnp.float32),
        in_specs=[pl.BlockSpec(memory_space=pltpu.HBM)] * len(operands),
        out_specs=pl.BlockSpec(memory_space=pltpu.VMEM),
        scratch_shapes=[
            pltpu.VMEM((tokens, model), bf16),
            pltpu.VMEM((tokens, hidden), bf16),
            pltpu.VMEM((tokens, hidden), bf16),
            pltpu.VMEM((tokens, hidden), bf16),
            pltpu.VMEM((tokens, model), bf16),
            pltpu.VMEM((2 * width, model), bf16),
            pltpu.VMEM((width, hidden), bf16),
            pltpu.VMEM((width, hidden), bf16),
            pltpu.VMEM((width, hidden), bf16),
            pltpu.VMEM((width, model), bf16),
            pltpu.VMEM((2, tokens, STEP), bf16),
            pltpu.VMEM((2, tokens, STEP), bf16),
            pltpu.VMEM((2, tokens, STEP), bf16),
            pltpu.VMEM((tokens, 2 * width), jnp.float32),
            pltpu.VMEM((4, tokens, width), jnp.float32),
            pltpu.SemaphoreType.DMA((steps,)),
        ],
        compiler_params=pltpu.CompilerParams(vmem_limit_bytes=427 * 2**17),
        cost_estimate=pl.CostEstimate(
            flops=6 * tokens * width * (model + hidden),
            bytes_accessed=2 * (2 * tokens * model + 3 * tokens * hidden),
            transcendentals=tokens * hidden,
        ),
        name="project",
    )(*operands)


def two_terms(value):
    high = value.astype(jnp.bfloat16)
    return high, (value - high.astype(jnp.float32)).astype(jnp.bfloat16)


def outer(chips, own, other, ids, out, summed, products):
    chip, core = lax.axis_index("dp"), lax.axis_index("mp")
    width = own.shape[1] // 6
    half = width // 2
    span = 3 * half // chips
    summed[...] = (own[...] + other[...]).T
    own_label = 2 * chip + core
    tail_label = jnp.where(core == 1, 2 * chip - 1, -1)
    masks = [(ids[...] == label).astype(jnp.float32) for label in (tail_label, own_label)]
    lane = lax.broadcasted_iota(jnp.int32, (half, 2 * width), 1)
    for module, (left, right) in enumerate(((0, 2), (1, 3), (4, 5))):
        factor = summed[left * width : (left + 1) * width, :]
        high, low = two_terms(jnp.concatenate([factor * mask for mask in masks], axis=0))
        top, bottom = two_terms(summed[right * width : (right + 1) * width, :])
        product = None
        for one, two in ((high, top), (high, bottom), (low, top)):
            both = jnp.concatenate([two, two], axis=0)
            term = lax.dot_general(one, both, NT, preferred_element_type=jnp.float32)
            product = term if product is None else product + term
        products[module] = product
        for label in range(2):
            even = products[module, pl.ds(label * width, half, stride=2), :]
            odd = products[module, pl.ds(label * width + 1, half, stride=2), :]
            packed = jnp.where(lane < width, even, odd)
            row = 0
            while row < half:
                chip_to, inside = divmod(module * half + row, span)
                count = min(span - inside, half - row)
                put = slice(label * span + inside, label * span + inside + count)
                out[chip_to, put, :] = packed[row : row + count]
                row += count


def example_blocks(chips, own, other, ids):
    width = own.shape[1] // 6
    block = (3 * width // chips, 2 * width)
    return pl.pallas_call(
        functools.partial(outer, chips),
        out_shape=jax.ShapeDtypeStruct((chips,) + block, jnp.float32),
        in_specs=[pl.BlockSpec(memory_space=pltpu.VMEM)] * 3,
        out_specs=pl.BlockSpec(memory_space=pltpu.VMEM),
        scratch_shapes=[
            pltpu.VMEM(own.shape[::-1], jnp.float32),
            pltpu.VMEM((3, 2 * width, 2 * width), jnp.float32),
        ],
        compiler_params=pltpu.CompilerParams(vmem_limit_bytes=6 * 2**20),
        name="outer",
    )(own, other, ids)


def score(queries, swapped, received, out, rows):
    core = lax.axis_index("mp")
    chips, height, lanes = received.shape
    span = height // 2
    rows[: chips * height, :] = received[...].reshape(chips * height, lanes)
    rows[chips * height :, :] = jnp.zeros((8, lanes), jnp.float32)
    grads = []
    for at in range(span):
        own = rows[pl.ds(span + at, chips, stride=height), :]
        tail = rows[pl.ds(at, chips, stride=height), :]
        tail = jnp.concatenate([tail[1:], jnp.zeros_like(tail[:1])], axis=0)
        grads.append(own + tail)
    terms = jnp.concatenate(two_terms(jnp.concatenate(grads, axis=1)), axis=0)
    coords = queries.shape[1]
    first = core == 0
    mine = jnp.where(first, terms[:, :coords], terms[:, coords:])
    theirs = jnp.where(first, terms[:, coords:], terms[:, :coords])
    scores = lax.dot_general(mine, queries[...], NT, preferred_element_type=jnp.float32)
    scores += lax.dot_general(theirs, swapped[...], NT, preferred_element_type=jnp.float32)
    out[...] = scores[:chips] + scores[chips:]


def partial_scores(queries, swapped, received):
    chips, height, lanes = received.shape
    return pl.pallas_call(
        score,
        out_shape=jax.ShapeDtypeStruct((chips, queries.shape[0]), jnp.float32),
        in_specs=[pl.BlockSpec(memory_space=pltpu.VMEM)] * 3,
        out_specs=pl.BlockSpec(memory_space=pltpu.VMEM),
        scratch_shapes=[pltpu.VMEM((chips * height + 8, lanes), jnp.float32)],
        compiler_params=pltpu.CompilerParams(vmem_limit_bytes=6 * 2**20),
        name="score",
    )(queries, swapped, received)


def body(
    inputs,
    gate_pre,
    up_pre,
    hidden_grad,
    out_grad,
    example_ids,
    gate_in,
    gate_out,
    up_in,
    up_out,
    down_in,
    down_out,
    queries,
):
    chips = lax.axis_size("dp")
    swap = [(0, 1), (1, 0)]
    swapped = lax.ppermute(queries, "mp", swap)
    bases = [base.T for base in (gate_in, gate_out, up_in, up_out, down_in, down_out)]
    own = projections(inputs, gate_pre, up_pre, hidden_grad, out_grad, *bases)
    other = lax.ppermute(own, "mp", swap)
    blocks = example_blocks(chips, own, other, example_ids.reshape(1, -1))
    received = lax.all_to_all(blocks, "dp", split_axis=0, concat_axis=0, tiled=True)
    scores = partial_scores(queries, swapped, received)[:, None]
    pieces = lax.all_to_all(scores, "dp", split_axis=0, concat_axis=0, tiled=True)
    return jnp.sum(pieces, axis=0)


def solution(mesh):
    placed = (
        P(("parts", "dp"), "mp"),
        P(("parts", "dp"), "mp"),
        P(("parts", "dp"), "mp"),
        P(("parts", "dp"), "mp"),
        P(("parts", "dp"), "mp"),
        P(("parts", "dp")),
        P("mp", None),
        P("mp", None),
        P("mp", None),
        P("mp", None),
        P("mp", None),
        P("mp", None),
        P(None, ("dp", "mp")),
    )
    return jax.shard_map(
        body, mesh=mesh, in_specs=placed, out_specs=P(("parts", "dp", "mp"), None), check_vma=False
    )
```

```python
import functools

import jax
import jax.numpy as jnp
from jax import lax
from jax.experimental import pallas as pl
from jax.experimental.pallas import tpu as pltpu
from jax.sharding import PartitionSpec as P

NT = (((1,), (1,)), ((), ()))
STEP = 1024
PART = 1024
ROWS = 16
AHEAD = 2


def project(
    inputs,
    gate_pre,
    up_pre,
    hidden_grad,
    out_grad,
    gate_in,
    gate_out,
    up_in,
    up_out,
    down_in,
    down_out,
    out,
    v_inputs,
    v_gate,
    v_up,
    v_back,
    v_out_grad,
    v_in,
    v_gate_out,
    v_up_out,
    v_down_in,
    v_down_out,
    made_hidden,
    made_up,
    made_gate,
    sum_in,
    sums,
    sems,
):
    width = gate_in.shape[0]
    tokens = inputs.shape[0]
    hidden_steps = gate_pre.shape[1] // STEP
    model_steps = inputs.shape[1] // STEP
    copies = []

    def plan(pairs):
        made_here = []
        for source, target in pairs:
            copy = pltpu.make_async_copy(source, target, sems.at[sum(map(len, copies)) + len(made_here)])
            made_here.append(copy)
        copies.append(made_here)

    for step in range(hidden_steps):
        at = pl.ds(step * STEP, STEP)
        pairs = [
            (gate_pre.at[:, at], v_gate.at[:, at]),
            (up_pre.at[:, at], v_up.at[:, at]),
            (hidden_grad.at[:, at], v_back.at[:, at]),
            (gate_out.at[:, at], v_gate_out.at[:, at]),
            (up_out.at[:, at], v_up_out.at[:, at]),
            (down_in.at[:, at], v_down_in.at[:, at]),
        ]
        if step < model_steps:
            pairs += [
                (inputs.at[:, at], v_inputs.at[:, at]),
                (gate_in.at[:, at], v_in.at[pl.ds(0, width), at]),
                (up_in.at[:, at], v_in.at[pl.ds(width, width), at]),
                (out_grad.at[:, at], v_out_grad.at[:, at]),
                (down_out.at[:, at], v_down_out.at[:, at]),
            ]
        plan(pairs)

    def elementwise(step, part):
        target = step % 2
        for top in range(0, tokens, ROWS):
            for left in range(part * PART, (part + 1) * PART, 256):
                at = (slice(top, top + ROWS), slice(step * STEP + left, step * STEP + left + 256))
                put = (slice(top, top + ROWS), slice(left, left + 256))
                gate = v_gate[at].astype(jnp.float32)
                up = v_up[at].astype(jnp.float32)
                back = v_back[at].astype(jnp.float32)
                half = 0.5 * gate
                tanh = jnp.tanh(half)
                plus = 1.0 + tanh
                silu = half * plus
                made_hidden[(target,) + put] = (silu * up).astype(jnp.bfloat16)
                made_up[(target,) + put] = (back * silu).astype(jnp.bfloat16)
                slope = plus + silu * (1.0 - tanh)
                made_gate[(target,) + put] = (back * up * slope).astype(jnp.bfloat16)

    def add(total, values, base, first):
        value = lax.dot_general(values, base, NT, preferred_element_type=jnp.float32)
        if first:
            total[...] = value
        else:
            total[...] += value

    def hidden_dots(step, part):
        at = slice(step * STEP + part * PART, step * STEP + (part + 1) * PART)
        inner = (step % 2, slice(None), slice(part * PART, (part + 1) * PART))
        first = step == 0 and part == 0
        add(sums.at[0], made_gate[inner], v_gate_out[:, at], first)
        add(sums.at[1], made_up[inner], v_up_out[:, at], first)
        add(sums.at[2], made_hidden[inner], v_down_in[:, at], first)

    def model_dots(step, part):
        at = slice(step * STEP + part * PART, step * STEP + (part + 1) * PART)
        first = step == 0 and part == 0
        add(sum_in, v_inputs[:, at], v_in[:, at], first)
        add(sums.at[3], v_out_grad[:, at], v_down_out[:, at], first)

    for step in range(min(AHEAD, hidden_steps)):
        for copy in copies[step]:
            copy.start()
    for step in range(hidden_steps):
        if step + AHEAD < hidden_steps:
            for copy in copies[step + AHEAD]:
                copy.start()
        for copy in copies[step]:
            copy.wait()
        for part in range(STEP // PART):
            elementwise(step, part)
            if step >= 1:
                hidden_dots(step - 1, part)
            if step < model_steps:
                model_dots(step, part)
    for part in range(STEP // PART):
        hidden_dots(hidden_steps - 1, part)
    out[:, : 2 * width] = sum_in[...]
    out[:, 2 * width : 4 * width] = jnp.concatenate([0.5 * sums[0], sums[1]], axis=1)
    out[:, 4 * width :] = jnp.concatenate([sums[2], sums[3]], axis=1)


def projections(*operands):
    inputs, gate_pre = operands[:2]
    width = operands[5].shape[0]
    tokens, model = inputs.shape
    hidden = gate_pre.shape[1]
    assert hidden % STEP == 0 and model % STEP == 0 and model <= hidden
    assert tokens % ROWS == 0
    steps = 6 * (hidden // STEP) + 5 * (model // STEP)
    bf16 = jnp.bfloat16
    return pl.pallas_call(
        project,
        out_shape=jax.ShapeDtypeStruct((tokens, 6 * width), jnp.float32),
        in_specs=[pl.BlockSpec(memory_space=pltpu.HBM)] * len(operands),
        out_specs=pl.BlockSpec(memory_space=pltpu.VMEM),
        scratch_shapes=[
            pltpu.VMEM((tokens, model), bf16),
            pltpu.VMEM((tokens, hidden), bf16),
            pltpu.VMEM((tokens, hidden), bf16),
            pltpu.VMEM((tokens, hidden), bf16),
            pltpu.VMEM((tokens, model), bf16),
            pltpu.VMEM((2 * width, model), bf16),
            pltpu.VMEM((width, hidden), bf16),
            pltpu.VMEM((width, hidden), bf16),
            pltpu.VMEM((width, hidden), bf16),
            pltpu.VMEM((width, model), bf16),
            pltpu.VMEM((2, tokens, STEP), bf16),
            pltpu.VMEM((2, tokens, STEP), bf16),
            pltpu.VMEM((2, tokens, STEP), bf16),
            pltpu.VMEM((tokens, 2 * width), jnp.float32),
            pltpu.VMEM((4, tokens, width), jnp.float32),
            pltpu.SemaphoreType.DMA((steps,)),
        ],
        compiler_params=pltpu.CompilerParams(vmem_limit_bytes=427 * 2**17),
        cost_estimate=pl.CostEstimate(
            flops=6 * tokens * width * (model + hidden),
            bytes_accessed=2 * (2 * tokens * model + 3 * tokens * hidden),
            transcendentals=tokens * hidden,
        ),
        name="project",
    )(*operands)


def two_terms(value):
    high = value.astype(jnp.bfloat16)
    return high, (value - high.astype(jnp.float32)).astype(jnp.bfloat16)


def outer(chips, own, other, ids, out, summed, products):
    chip, core = lax.axis_index("dp"), lax.axis_index("mp")
    width = own.shape[1] // 6
    half = width // 2
    span = 3 * half // chips
    summed[...] = (own[...] + other[...]).T
    own_label = 2 * chip + core
    tail_label = jnp.where(core == 1, 2 * chip - 1, -1)
    masks = [(ids[...] == label).astype(jnp.float32) for label in (tail_label, own_label)]
    lane = lax.broadcasted_iota(jnp.int32, (half, 2 * width), 1)
    for module, (left, right) in enumerate(((0, 2), (1, 3), (4, 5))):
        factor = summed[left * width : (left + 1) * width, :]
        high, low = two_terms(jnp.concatenate([factor * mask for mask in masks], axis=0))
        top, bottom = two_terms(summed[right * width : (right + 1) * width, :])
        product = None
        for one, two in ((high, top), (high, bottom), (low, top)):
            both = jnp.concatenate([two, two], axis=0)
            term = lax.dot_general(one, both, NT, preferred_element_type=jnp.float32)
            product = term if product is None else product + term
        products[module] = product
        for label in range(2):
            even = products[module, pl.ds(label * width, half, stride=2), :]
            odd = products[module, pl.ds(label * width + 1, half, stride=2), :]
            packed = jnp.where(lane < width, even, odd)
            row = 0
            while row < half:
                chip_to, inside = divmod(module * half + row, span)
                count = min(span - inside, half - row)
                put = slice(label * span + inside, label * span + inside + count)
                out[chip_to, put, :] = packed[row : row + count]
                row += count


def example_blocks(chips, own, other, ids):
    width = own.shape[1] // 6
    block = (3 * width // chips, 2 * width)
    return pl.pallas_call(
        functools.partial(outer, chips),
        out_shape=jax.ShapeDtypeStruct((chips,) + block, jnp.float32),
        in_specs=[pl.BlockSpec(memory_space=pltpu.VMEM)] * 3,
        out_specs=pl.BlockSpec(memory_space=pltpu.VMEM),
        scratch_shapes=[
            pltpu.VMEM(own.shape[::-1], jnp.float32),
            pltpu.VMEM((3, 2 * width, 2 * width), jnp.float32),
        ],
        compiler_params=pltpu.CompilerParams(vmem_limit_bytes=6 * 2**20),
        name="outer",
    )(own, other, ids)


def score(queries, swapped, received, out, rows):
    core = lax.axis_index("mp")
    chips, height, lanes = received.shape
    span = height // 2
    rows[: chips * height, :] = received[...].reshape(chips * height, lanes)
    rows[chips * height :, :] = jnp.zeros((8, lanes), jnp.float32)
    grads = []
    for at in range(span):
        own = rows[pl.ds(span + at, chips, stride=height), :]
        tail = rows[pl.ds(at, chips, stride=height), :]
        tail = jnp.concatenate([tail[1:], jnp.zeros_like(tail[:1])], axis=0)
        grads.append(own + tail)
    terms = jnp.concatenate(two_terms(jnp.concatenate(grads, axis=1)), axis=0)
    coords = queries.shape[1]
    first = core == 0
    mine = jnp.where(first, terms[:, :coords], terms[:, coords:])
    theirs = jnp.where(first, terms[:, coords:], terms[:, :coords])
    scores = lax.dot_general(mine, queries[...], NT, preferred_element_type=jnp.float32)
    scores += lax.dot_general(theirs, swapped[...], NT, preferred_element_type=jnp.float32)
    out[...] = scores[:chips] + scores[chips:]


def partial_scores(queries, swapped, received):
    chips, height, lanes = received.shape
    return pl.pallas_call(
        score,
        out_shape=jax.ShapeDtypeStruct((chips, queries.shape[0]), jnp.float32),
        in_specs=[pl.BlockSpec(memory_space=pltpu.VMEM)] * 3,
        out_specs=pl.BlockSpec(memory_space=pltpu.VMEM),
        scratch_shapes=[pltpu.VMEM((chips * height + 8, lanes), jnp.float32)],
        compiler_params=pltpu.CompilerParams(vmem_limit_bytes=6 * 2**20),
        name="score",
    )(queries, swapped, received)


def body(
    inputs,
    gate_pre,
    up_pre,
    hidden_grad,
    out_grad,
    example_ids,
    gate_in,
    gate_out,
    up_in,
    up_out,
    down_in,
    down_out,
    queries,
):
    chips = lax.axis_size("dp")
    swap = [(0, 1), (1, 0)]
    swapped = lax.ppermute(queries, "mp", swap)
    bases = [base.T for base in (gate_in, gate_out, up_in, up_out, down_in, down_out)]
    own = projections(inputs, gate_pre, up_pre, hidden_grad, out_grad, *bases)
    other = lax.ppermute(own, "mp", swap)
    blocks = example_blocks(chips, own, other, example_ids.reshape(1, -1))
    received = lax.all_to_all(blocks, "dp", split_axis=0, concat_axis=0, tiled=True)
    scores = partial_scores(queries, swapped, received)[:, None]
    pieces = lax.all_to_all(scores, "dp", split_axis=0, concat_axis=0, tiled=True)
    return jnp.sum(pieces, axis=0)


def solution(mesh):
    placed = (
        P(("parts", "dp"), "mp"),
        P(("parts", "dp"), "mp"),
        P(("parts", "dp"), "mp"),
        P(("parts", "dp"), "mp"),
        P(("parts", "dp"), "mp"),
        P(("parts", "dp")),
        P("mp", None),
        P("mp", None),
        P("mp", None),
        P("mp", None),
        P("mp", None),
        P("mp", None),
        P(None, ("dp", "mp")),
    )
    return jax.shard_map(
        body, mesh=mesh, in_specs=placed, out_specs=P(("parts", "dp", "mp"), None), check_vma=False
    )
```

```python
import functools

import jax
import jax.numpy as jnp
from jax import lax
from jax.experimental import pallas as pl
from jax.experimental.pallas import tpu as pltpu
from jax.sharding import PartitionSpec as P

NT = (((1,), (1,)), ((), ()))
STEP = 1024
TILE = 256
ROWS = 16
AHEAD = 2


def project(
    inputs,
    gate_pre,
    up_pre,
    hidden_grad,
    out_grad,
    gate_in,
    gate_out,
    up_in,
    up_out,
    down_in,
    down_out,
    out,
    v_inputs,
    v_gate,
    v_up,
    v_back,
    v_out_grad,
    v_in,
    v_gate_out,
    v_up_out,
    v_down_in,
    v_down_out,
    sum_in,
    sums,
    sems,
):
    width = gate_in.shape[0]
    tokens = inputs.shape[0]
    hidden_steps = gate_pre.shape[1] // STEP
    model_steps = inputs.shape[1] // STEP
    copies = []

    def plan(pairs):
        made_here = []
        for source, target in pairs:
            copy = pltpu.make_async_copy(source, target, sems.at[sum(map(len, copies)) + len(made_here)])
            made_here.append(copy)
        copies.append(made_here)

    for step in range(hidden_steps):
        at = pl.ds(step * STEP, STEP)
        pairs = [
            (gate_pre.at[:, at], v_gate.at[:, at]),
            (up_pre.at[:, at], v_up.at[:, at]),
            (hidden_grad.at[:, at], v_back.at[:, at]),
            (gate_out.at[:, at], v_gate_out.at[:, at]),
            (up_out.at[:, at], v_up_out.at[:, at]),
            (down_in.at[:, at], v_down_in.at[:, at]),
        ]
        if step < model_steps:
            pairs += [
                (inputs.at[:, at], v_inputs.at[:, at]),
                (gate_in.at[:, at], v_in.at[pl.ds(0, width), at]),
                (up_in.at[:, at], v_in.at[pl.ds(width, width), at]),
                (out_grad.at[:, at], v_out_grad.at[:, at]),
                (down_out.at[:, at], v_down_out.at[:, at]),
            ]
        plan(pairs)

    def products(step, left):
        parts = []
        for top in range(0, tokens, ROWS):
            at = (slice(top, top + ROWS), slice(step * STEP + left, step * STEP + left + TILE))
            half = 0.5 * v_gate[at].astype(jnp.float32)
            up = v_up[at].astype(jnp.float32)
            back = v_back[at].astype(jnp.float32)
            tanh = jnp.tanh(half)
            plus = 1.0 + tanh
            silu = half * plus
            slope = plus + silu * (1.0 - tanh)
            values = (back * up * slope, back * silu, silu * up)
            parts.append([value.astype(jnp.bfloat16) for value in values])
        return [jnp.concatenate(column, axis=0) for column in zip(*parts)]

    def add(total, values, base, first):
        value = lax.dot_general(values, base, NT, preferred_element_type=jnp.float32)
        if first:
            total[...] = value
        else:
            total[...] += value

    def hidden_dots(step, left):
        at = slice(step * STEP + left, step * STEP + left + TILE)
        bases = (v_gate_out, v_up_out, v_down_in)
        for which, value in enumerate(products(step, left)):
            add(sums.at[which], value, bases[which][:, at], step == 0 and left == 0)

    def model_dots(step):
        at = slice(step * STEP, (step + 1) * STEP)
        add(sum_in, v_inputs[:, at], v_in[:, at], step == 0)
        add(sums.at[3], v_out_grad[:, at], v_down_out[:, at], step == 0)

    for step in range(min(AHEAD, hidden_steps)):
        for copy in copies[step]:
            copy.start()
    for step in range(hidden_steps):
        if step + AHEAD < hidden_steps:
            for copy in copies[step + AHEAD]:
                copy.start()
        for copy in copies[step]:
            copy.wait()
        for left in range(0, STEP, TILE):
            hidden_dots(step, left)
        if step < model_steps:
            model_dots(step)
    out[:, : 2 * width] = sum_in[...]
    out[:, 2 * width : 4 * width] = jnp.concatenate([0.5 * sums[0], sums[1]], axis=1)
    out[:, 4 * width :] = jnp.concatenate([sums[2], sums[3]], axis=1)


def projections(*operands):
    inputs, gate_pre = operands[:2]
    width = operands[5].shape[0]
    tokens, model = inputs.shape
    hidden = gate_pre.shape[1]
    assert hidden % STEP == 0 and model % STEP == 0 and model <= hidden
    assert tokens % ROWS == 0
    steps = 6 * (hidden // STEP) + 5 * (model // STEP)
    bf16 = jnp.bfloat16
    return pl.pallas_call(
        project,
        out_shape=jax.ShapeDtypeStruct((tokens, 6 * width), jnp.float32),
        in_specs=[pl.BlockSpec(memory_space=pltpu.HBM)] * len(operands),
        out_specs=pl.BlockSpec(memory_space=pltpu.VMEM),
        scratch_shapes=[
            pltpu.VMEM((tokens, model), bf16),
            pltpu.VMEM((tokens, hidden), bf16),
            pltpu.VMEM((tokens, hidden), bf16),
            pltpu.VMEM((tokens, hidden), bf16),
            pltpu.VMEM((tokens, model), bf16),
            pltpu.VMEM((2 * width, model), bf16),
            pltpu.VMEM((width, hidden), bf16),
            pltpu.VMEM((width, hidden), bf16),
            pltpu.VMEM((width, hidden), bf16),
            pltpu.VMEM((width, model), bf16),
            pltpu.VMEM((tokens, 2 * width), jnp.float32),
            pltpu.VMEM((4, tokens, width), jnp.float32),
            pltpu.SemaphoreType.DMA((steps,)),
        ],
        compiler_params=pltpu.CompilerParams(vmem_limit_bytes=427 * 2**17),
        cost_estimate=pl.CostEstimate(
            flops=6 * tokens * width * (model + hidden),
            bytes_accessed=2 * (2 * tokens * model + 3 * tokens * hidden),
            transcendentals=tokens * hidden,
        ),
        name="project",
    )(*operands)


def two_terms(value):
    high = value.astype(jnp.bfloat16)
    return high, (value - high.astype(jnp.float32)).astype(jnp.bfloat16)


def outer(chips, own, other, ids, out, summed, products):
    chip, core = lax.axis_index("dp"), lax.axis_index("mp")
    width = own.shape[1] // 6
    half = width // 2
    span = 3 * half // chips
    summed[...] = (own[...] + other[...]).T
    own_label = 2 * chip + core
    tail_label = jnp.where(core == 1, 2 * chip - 1, -1)
    masks = [(ids[...] == label).astype(jnp.float32) for label in (tail_label, own_label)]
    lane = lax.broadcasted_iota(jnp.int32, (half, 2 * width), 1)
    for module, (left, right) in enumerate(((0, 2), (1, 3), (4, 5))):
        factor = summed[left * width : (left + 1) * width, :]
        high, low = two_terms(jnp.concatenate([factor * mask for mask in masks], axis=0))
        top, bottom = two_terms(summed[right * width : (right + 1) * width, :])
        product = None
        for one, two in ((high, top), (high, bottom), (low, top)):
            both = jnp.concatenate([two, two], axis=0)
            term = lax.dot_general(one, both, NT, preferred_element_type=jnp.float32)
            product = term if product is None else product + term
        products[module] = product
        for label in range(2):
            even = products[module, pl.ds(label * width, half, stride=2), :]
            odd = products[module, pl.ds(label * width + 1, half, stride=2), :]
            packed = jnp.where(lane < width, even, odd)
            row = 0
            while row < half:
                chip_to, inside = divmod(module * half + row, span)
                count = min(span - inside, half - row)
                put = slice(label * span + inside, label * span + inside + count)
                out[chip_to, put, :] = packed[row : row + count]
                row += count


def example_blocks(chips, own, other, ids):
    width = own.shape[1] // 6
    block = (3 * width // chips, 2 * width)
    return pl.pallas_call(
        functools.partial(outer, chips),
        out_shape=jax.ShapeDtypeStruct((chips,) + block, jnp.float32),
        in_specs=[pl.BlockSpec(memory_space=pltpu.VMEM)] * 3,
        out_specs=pl.BlockSpec(memory_space=pltpu.VMEM),
        scratch_shapes=[
            pltpu.VMEM(own.shape[::-1], jnp.float32),
            pltpu.VMEM((3, 2 * width, 2 * width), jnp.float32),
        ],
        compiler_params=pltpu.CompilerParams(vmem_limit_bytes=6 * 2**20),
        name="outer",
    )(own, other, ids)


def score(queries, swapped, received, out, rows):
    core = lax.axis_index("mp")
    chips, height, lanes = received.shape
    span = height // 2
    rows[: chips * height, :] = received[...].reshape(chips * height, lanes)
    rows[chips * height :, :] = jnp.zeros((8, lanes), jnp.float32)
    grads = []
    for at in range(span):
        own = rows[pl.ds(span + at, chips, stride=height), :]
        tail = rows[pl.ds(at, chips, stride=height), :]
        tail = jnp.concatenate([tail[1:], jnp.zeros_like(tail[:1])], axis=0)
        grads.append(own + tail)
    terms = jnp.concatenate(two_terms(jnp.concatenate(grads, axis=1)), axis=0)
    coords = queries.shape[1]
    first = core == 0
    mine = jnp.where(first, terms[:, :coords], terms[:, coords:])
    theirs = jnp.where(first, terms[:, coords:], terms[:, :coords])
    scores = lax.dot_general(mine, queries[...], NT, preferred_element_type=jnp.float32)
    scores += lax.dot_general(theirs, swapped[...], NT, preferred_element_type=jnp.float32)
    out[...] = scores[:chips] + scores[chips:]


def partial_scores(queries, swapped, received):
    chips, height, lanes = received.shape
    return pl.pallas_call(
        score,
        out_shape=jax.ShapeDtypeStruct((chips, queries.shape[0]), jnp.float32),
        in_specs=[pl.BlockSpec(memory_space=pltpu.VMEM)] * 3,
        out_specs=pl.BlockSpec(memory_space=pltpu.VMEM),
        scratch_shapes=[pltpu.VMEM((chips * height + 8, lanes), jnp.float32)],
        compiler_params=pltpu.CompilerParams(vmem_limit_bytes=6 * 2**20),
        name="score",
    )(queries, swapped, received)


def body(
    inputs,
    gate_pre,
    up_pre,
    hidden_grad,
    out_grad,
    example_ids,
    gate_in,
    gate_out,
    up_in,
    up_out,
    down_in,
    down_out,
    queries,
):
    chips = lax.axis_size("dp")
    swap = [(0, 1), (1, 0)]
    swapped = lax.ppermute(queries, "mp", swap)
    bases = [base.T for base in (gate_in, gate_out, up_in, up_out, down_in, down_out)]
    own = projections(inputs, gate_pre, up_pre, hidden_grad, out_grad, *bases)
    other = lax.ppermute(own, "mp", swap)
    blocks = example_blocks(chips, own, other, example_ids.reshape(1, -1))
    received = lax.all_to_all(blocks, "dp", split_axis=0, concat_axis=0, tiled=True)
    scores = partial_scores(queries, swapped, received)[:, None]
    pieces = lax.all_to_all(scores, "dp", split_axis=0, concat_axis=0, tiled=True)
    return jnp.sum(pieces, axis=0)


def solution(mesh):
    placed = (
        P(("parts", "dp"), "mp"),
        P(("parts", "dp"), "mp"),
        P(("parts", "dp"), "mp"),
        P(("parts", "dp"), "mp"),
        P(("parts", "dp"), "mp"),
        P(("parts", "dp")),
        P("mp", None),
        P("mp", None),
        P("mp", None),
        P("mp", None),
        P("mp", None),
        P("mp", None),
        P(None, ("dp", "mp")),
    )
    return jax.shard_map(
        body, mesh=mesh, in_specs=placed, out_specs=P(("parts", "dp", "mp"), None), check_vma=False
    )
```

```python
import functools

import jax
import jax.numpy as jnp
from jax import lax
from jax.experimental import pallas as pl
from jax.experimental.pallas import tpu as pltpu
from jax.sharding import PartitionSpec as P

NT = (((1,), (1,)), ((), ()))
STEP = 1024
TILE = 256
ROWS = 16
AHEAD = 3


def project(
    inputs,
    gate_pre,
    up_pre,
    hidden_grad,
    out_grad,
    gate_in,
    gate_out,
    up_in,
    up_out,
    down_in,
    down_out,
    out,
    rounded,
    v_inputs,
    v_gate,
    v_up,
    v_back,
    v_out_grad,
    v_in,
    v_gate_out,
    v_up_out,
    v_down_in,
    v_down_out,
    sum_in,
    sums,
    sems,
):
    width = gate_in.shape[0]
    tokens = inputs.shape[0]
    hidden, model = gate_pre.shape[1], inputs.shape[1]
    edges = [0, STEP // 2] + list(range(STEP, hidden - STEP + 1, STEP)) + [hidden - STEP // 2, hidden]
    steps = [slice(low, high) for low, high in zip(edges, edges[1:])]
    first_model = 2
    copies = []
    for step, at in enumerate(steps):
        pairs = [
            (gate_pre, v_gate),
            (up_pre, v_up),
            (hidden_grad, v_back),
            (gate_out, v_gate_out),
            (up_out, v_up_out),
            (down_in, v_down_in),
        ]
        pairs = [
            (source.at[:, pl.ds(at.start, at.stop - at.start)], target.at[:, pl.ds(at.start, at.stop - at.start)])
            for source, target in pairs
        ]
        if 0 <= step - first_model < model // STEP:
            at = pl.ds((step - first_model) * STEP, STEP)
            pairs += [
                (inputs.at[:, at], v_inputs.at[:, at]),
                (gate_in.at[:, at], v_in.at[pl.ds(0, width), at]),
                (up_in.at[:, at], v_in.at[pl.ds(width, width), at]),
                (out_grad.at[:, at], v_out_grad.at[:, at]),
                (down_out.at[:, at], v_down_out.at[:, at]),
            ]
        known = sum(map(len, copies))
        copies.append(
            [
                pltpu.make_async_copy(source, target, sems.at[known + i])
                for i, (source, target) in enumerate(pairs)
            ]
        )

    def products(left):
        parts = []
        for top in range(0, tokens, ROWS):
            at = (slice(top, top + ROWS), slice(left, left + TILE))
            half = 0.5 * v_gate[at].astype(jnp.float32)
            up = v_up[at].astype(jnp.float32)
            back = v_back[at].astype(jnp.float32)
            tanh = jnp.tanh(half)
            plus = 1.0 + tanh
            silu = half * plus
            slope = plus + silu * (1.0 - tanh)
            values = (back * up * slope, back * silu, silu * up)
            parts.append([value.astype(jnp.bfloat16) for value in values])
        return [jnp.concatenate(column, axis=0) for column in zip(*parts)]

    def add(total, values, base, first):
        value = lax.dot_general(values, base, NT, preferred_element_type=jnp.float32)
        if first:
            total[...] = value
        else:
            total[...] += value

    def hidden_dots(left):
        at = slice(left, left + TILE)
        bases = (v_gate_out, v_up_out, v_down_in)
        for which, value in enumerate(products(left)):
            add(sums.at[which], value, bases[which][:, at], left == 0)

    def model_dots(step):
        at = slice(step * STEP, (step + 1) * STEP)
        add(sum_in, v_inputs[:, at], v_in[:, at], step == 0)
        add(sums.at[3], v_out_grad[:, at], v_down_out[:, at], step == 0)

    for step in range(AHEAD):
        for copy in copies[step]:
            copy.start()
    for step, at in enumerate(steps):
        if step + AHEAD < len(steps):
            for copy in copies[step + AHEAD]:
                copy.start()
        for copy in copies[step]:
            copy.wait()
        for left in range(at.start, at.stop, TILE):
            hidden_dots(left)
        if 0 <= step - first_model < model // STEP:
            model_dots(step - first_model)
    out[:, : 2 * width] = sum_in[...]
    out[:, 2 * width : 4 * width] = jnp.concatenate([0.5 * sums[0], sums[1]], axis=1)
    out[:, 4 * width :] = jnp.concatenate([sums[2], sums[3]], axis=1)
    rounded[...] = out[...].astype(jnp.bfloat16)


def projections(*operands):
    inputs, gate_pre = operands[:2]
    width = operands[5].shape[0]
    tokens, model = inputs.shape
    hidden = gate_pre.shape[1]
    assert hidden % STEP == 0 and model % STEP == 0 and model + 2 * STEP <= hidden
    assert tokens % ROWS == 0
    copies = 6 * (hidden // STEP + 2) + 5 * (model // STEP)
    bf16 = jnp.bfloat16
    return pl.pallas_call(
        project,
        out_shape=[jax.ShapeDtypeStruct((tokens, 6 * width), kind) for kind in (jnp.float32, bf16)],
        in_specs=[pl.BlockSpec(memory_space=pltpu.HBM)] * len(operands),
        out_specs=[pl.BlockSpec(memory_space=pltpu.VMEM)] * 2,
        scratch_shapes=[
            pltpu.VMEM((tokens, model), bf16),
            pltpu.VMEM((tokens, hidden), bf16),
            pltpu.VMEM((tokens, hidden), bf16),
            pltpu.VMEM((tokens, hidden), bf16),
            pltpu.VMEM((tokens, model), bf16),
            pltpu.VMEM((2 * width, model), bf16),
            pltpu.VMEM((width, hidden), bf16),
            pltpu.VMEM((width, hidden), bf16),
            pltpu.VMEM((width, hidden), bf16),
            pltpu.VMEM((width, model), bf16),
            pltpu.VMEM((tokens, 2 * width), jnp.float32),
            pltpu.VMEM((4, tokens, width), jnp.float32),
            pltpu.SemaphoreType.DMA((copies,)),
        ],
        compiler_params=pltpu.CompilerParams(vmem_limit_bytes=427 * 2**17),
        cost_estimate=pl.CostEstimate(
            flops=6 * tokens * width * (model + hidden),
            bytes_accessed=2 * (2 * tokens * model + 3 * tokens * hidden),
            transcendentals=tokens * hidden,
        ),
        name="project",
    )(*operands)


def two_terms(value):
    high = value.astype(jnp.bfloat16)
    return high, (value - high.astype(jnp.float32)).astype(jnp.bfloat16)


def outer(chips, own, other, ids, out, summed, products, blocks):
    chip, core = lax.axis_index("dp"), lax.axis_index("mp")
    width = own.shape[1] // 6
    half = width // 2
    span = 3 * half // chips
    summed[...] = (own[...] + other[...].astype(jnp.float32)).T
    own_label = 2 * chip + core
    tail_label = jnp.where(core == 1, 2 * chip - 1, -1)
    masks = [(ids[...] == label).astype(jnp.float32) for label in (tail_label, own_label)]
    lane = lax.broadcasted_iota(jnp.int32, (half, 2 * width), 1)
    for module, (left, right) in enumerate(((0, 2), (1, 3), (4, 5))):
        factor = summed[left * width : (left + 1) * width, :]
        high, low = two_terms(jnp.concatenate([factor * mask for mask in masks], axis=0))
        top, bottom = two_terms(summed[right * width : (right + 1) * width, :])
        product = None
        for one, two in ((high, top), (high, bottom), (low, top)):
            both = jnp.concatenate([two, two], axis=0)
            term = lax.dot_general(one, both, NT, preferred_element_type=jnp.float32)
            product = term if product is None else product + term
        products[module] = product
        for label in range(2):
            even = products[module, pl.ds(label * width, half, stride=2), :]
            odd = products[module, pl.ds(label * width + 1, half, stride=2), :]
            packed = jnp.where(lane < width, even, odd)
            row = 0
            while row < half:
                chip_to, inside = divmod(module * half + row, span)
                count = min(span - inside, half - row)
                put = slice(label * span + inside, label * span + inside + count)
                blocks[chip_to, put, :] = packed[row : row + count]
                row += count
    out[...] = blocks[...].astype(jnp.bfloat16)


def example_blocks(chips, own, other, ids):
    width = own.shape[1] // 6
    block = (3 * width // chips, 2 * width)
    return pl.pallas_call(
        functools.partial(outer, chips),
        out_shape=jax.ShapeDtypeStruct((chips,) + block, jnp.bfloat16),
        in_specs=[pl.BlockSpec(memory_space=pltpu.VMEM)] * 3,
        out_specs=pl.BlockSpec(memory_space=pltpu.VMEM),
        scratch_shapes=[
            pltpu.VMEM(own.shape[::-1], jnp.float32),
            pltpu.VMEM((3, 2 * width, 2 * width), jnp.float32),
            pltpu.VMEM((chips,) + block, jnp.float32),
        ],
        compiler_params=pltpu.CompilerParams(vmem_limit_bytes=6 * 2**20),
        name="outer",
    )(own, other, ids)


def score(queries, swapped, received, out, rows):
    core = lax.axis_index("mp")
    chips, height, lanes = received.shape
    span = height // 2
    rows[: chips * height, :] = received[...].astype(jnp.float32).reshape(chips * height, lanes)
    rows[chips * height :, :] = jnp.zeros((8, lanes), jnp.float32)
    grads = []
    for at in range(span):
        own = rows[pl.ds(span + at, chips, stride=height), :]
        tail = rows[pl.ds(at, chips, stride=height), :]
        tail = jnp.concatenate([tail[1:], jnp.zeros_like(tail[:1])], axis=0)
        grads.append(own + tail)
    terms = jnp.concatenate(two_terms(jnp.concatenate(grads, axis=1)), axis=0)
    coords = queries.shape[1]
    first = core == 0
    mine = jnp.where(first, terms[:, :coords], terms[:, coords:])
    theirs = jnp.where(first, terms[:, coords:], terms[:, :coords])
    scores = lax.dot_general(mine, queries[...], NT, preferred_element_type=jnp.float32)
    scores += lax.dot_general(theirs, swapped[...], NT, preferred_element_type=jnp.float32)
    out[...] = scores[:chips] + scores[chips:]


def partial_scores(queries, swapped, received):
    chips, height, lanes = received.shape
    return pl.pallas_call(
        score,
        out_shape=jax.ShapeDtypeStruct((chips, queries.shape[0]), jnp.float32),
        in_specs=[pl.BlockSpec(memory_space=pltpu.VMEM)] * 3,
        out_specs=pl.BlockSpec(memory_space=pltpu.VMEM),
        scratch_shapes=[pltpu.VMEM((chips * height + 8, lanes), jnp.float32)],
        compiler_params=pltpu.CompilerParams(vmem_limit_bytes=6 * 2**20),
        name="score",
    )(queries, swapped, received)


def body(
    inputs,
    gate_pre,
    up_pre,
    hidden_grad,
    out_grad,
    example_ids,
    gate_in,
    gate_out,
    up_in,
    up_out,
    down_in,
    down_out,
    queries,
):
    chips = lax.axis_size("dp")
    swap = [(0, 1), (1, 0)]
    swapped = lax.ppermute(queries, "mp", swap)
    bases = [base.T for base in (gate_in, gate_out, up_in, up_out, down_in, down_out)]
    own, rounded = projections(inputs, gate_pre, up_pre, hidden_grad, out_grad, *bases)
    other = lax.ppermute(rounded, "mp", swap)
    blocks = example_blocks(chips, own, other, example_ids.reshape(1, -1))
    received = lax.all_to_all(blocks, "dp", split_axis=0, concat_axis=0, tiled=True)
    scores = partial_scores(queries, swapped, received)[:, None]
    pieces = lax.all_to_all(scores, "dp", split_axis=0, concat_axis=0, tiled=True)
    return jnp.sum(pieces, axis=0)


def solution(mesh):
    placed = (
        P(("parts", "dp"), "mp"),
        P(("parts", "dp"), "mp"),
        P(("parts", "dp"), "mp"),
        P(("parts", "dp"), "mp"),
        P(("parts", "dp"), "mp"),
        P(("parts", "dp")),
        P("mp", None),
        P("mp", None),
        P("mp", None),
        P("mp", None),
        P("mp", None),
        P("mp", None),
        P(None, ("dp", "mp")),
    )
    return jax.shard_map(
        body, mesh=mesh, in_specs=placed, out_specs=P(("parts", "dp", "mp"), None), check_vma=False
    )
```

```python
import functools

import jax
import jax.numpy as jnp
from jax import lax
from jax.experimental import pallas as pl
from jax.experimental.pallas import tpu as pltpu
from jax.sharding import PartitionSpec as P

NT = (((1,), (1,)), ((), ()))
STEP = 1024
TILE = 256
ROWS = 16
AHEAD = 4


def project(
    inputs,
    gate_pre,
    up_pre,
    hidden_grad,
    out_grad,
    gate_in,
    gate_out,
    up_in,
    up_out,
    down_in,
    down_out,
    out,
    v_inputs,
    v_gate,
    v_up,
    v_back,
    v_out_grad,
    v_in,
    v_gate_out,
    v_up_out,
    v_down_in,
    v_down_out,
    sum_in,
    sums,
    sems,
):
    width = gate_in.shape[0]
    tokens = inputs.shape[0]
    hidden, model = gate_pre.shape[1], inputs.shape[1]
    edges = [0] + list(range(STEP // 2, hidden, STEP)) + [hidden]
    pieces = [slice(low, high) for low, high in zip(edges, edges[1:])]
    sides = [slice(0, hidden // 2), slice(hidden // 2, hidden)]
    known = []

    def copies(pairs, at=None):
        group = []
        for source, target in pairs:
            if at is not None:
                window = pl.ds(at.start, at.stop - at.start)
                source, target = source.at[:, window], target.at[:, window]
            group.append(pltpu.make_async_copy(source, target, sems.at[len(known)]))
            known.append(group[-1])
        return group

    activations = ((gate_pre, v_gate), (up_pre, v_up), (hidden_grad, v_back))
    bases = ((gate_out, v_gate_out), (up_out, v_up_out), (down_in, v_down_in))
    for_inputs = (
        (gate_in, v_in.at[pl.ds(0, width), :]),
        (up_in, v_in.at[pl.ds(width, width), :]),
        (inputs, v_inputs),
    )
    for_out_grad = ((down_out, v_down_out), (out_grad, v_out_grad))
    groups = []
    for index, at in enumerate(pieces):
        groups.append((copies(activations, at), ("hidden", at)))
        if index == 0:
            groups.append((copies(bases, sides[0]), None))
        if index == 2:
            groups.append((copies(bases, sides[1]), None))
        if index == 3:
            groups.append((copies(for_inputs), ("inputs", None)))
        if index == 5:
            groups.append((copies(for_out_grad), ("out_grad", None)))
    groups[0], groups[1] = (groups[0][0], None), (groups[1][0], groups[0][1])

    def products(left):
        parts = []
        for top in range(0, tokens, ROWS):
            at = (slice(top, top + ROWS), slice(left, left + TILE))
            half = 0.5 * v_gate[at].astype(jnp.float32)
            up = v_up[at].astype(jnp.float32)
            back = v_back[at].astype(jnp.float32)
            tanh = jnp.tanh(half)
            plus = 1.0 + tanh
            silu = half * plus
            slope = plus + silu * (1.0 - tanh)
            values = (back * up * slope, back * silu, silu * up)
            parts.append([value.astype(jnp.bfloat16) for value in values])
        return [jnp.concatenate(column, axis=0) for column in zip(*parts)]

    def add(total, values, base, first):
        value = lax.dot_general(values, base, NT, preferred_element_type=jnp.float32)
        if first:
            total[...] = value
        else:
            total[...] += value

    def hidden_dots(left):
        at = slice(left, left + TILE)
        for which, value in enumerate(products(left)):
            add(sums.at[which], value, bases[which][1][:, at], left == 0)

    for group, _ in groups[:AHEAD]:
        for copy in group:
            copy.start()
    for index, (group, work) in enumerate(groups):
        for later, _ in groups[index + AHEAD : index + AHEAD + 1]:
            for copy in later:
                copy.start()
        for copy in group:
            copy.wait()
        if work is None:
            continue
        kind, at = work
        if kind == "hidden":
            for left in range(at.start, at.stop, TILE):
                hidden_dots(left)
        if kind == "inputs":
            add(sum_in, v_inputs[...], v_in[...], True)
        if kind == "out_grad":
            add(sums.at[3], v_out_grad[...], v_down_out[...], True)
    out[:, : 2 * width] = sum_in[...]
    out[:, 2 * width : 4 * width] = jnp.concatenate([0.5 * sums[0], sums[1]], axis=1)
    out[:, 4 * width :] = jnp.concatenate([sums[2], sums[3]], axis=1)


def projections(*operands):
    inputs, gate_pre = operands[:2]
    width = operands[5].shape[0]
    tokens, model = inputs.shape
    hidden = gate_pre.shape[1]
    assert hidden % STEP == 0 and hidden >= 6 * STEP and tokens % ROWS == 0
    copies = 3 * (hidden // STEP + 1) + 11
    bf16 = jnp.bfloat16
    return pl.pallas_call(
        project,
        out_shape=jax.ShapeDtypeStruct((tokens, 6 * width), jnp.float32),
        in_specs=[pl.BlockSpec(memory_space=pltpu.HBM)] * len(operands),
        out_specs=pl.BlockSpec(memory_space=pltpu.VMEM),
        scratch_shapes=[
            pltpu.VMEM((tokens, model), bf16),
            pltpu.VMEM((tokens, hidden), bf16),
            pltpu.VMEM((tokens, hidden), bf16),
            pltpu.VMEM((tokens, hidden), bf16),
            pltpu.VMEM((tokens, model), bf16),
            pltpu.VMEM((2 * width, model), bf16),
            pltpu.VMEM((width, hidden), bf16),
            pltpu.VMEM((width, hidden), bf16),
            pltpu.VMEM((width, hidden), bf16),
            pltpu.VMEM((width, model), bf16),
            pltpu.VMEM((tokens, 2 * width), jnp.float32),
            pltpu.VMEM((4, tokens, width), jnp.float32),
            pltpu.SemaphoreType.DMA((copies,)),
        ],
        compiler_params=pltpu.CompilerParams(vmem_limit_bytes=427 * 2**17),
        cost_estimate=pl.CostEstimate(
            flops=6 * tokens * width * (model + hidden),
            bytes_accessed=2 * (2 * tokens * model + 3 * tokens * hidden),
            transcendentals=tokens * hidden,
        ),
        name="project",
    )(*operands)


def two_terms(value):
    high = value.astype(jnp.bfloat16)
    return high, (value - high.astype(jnp.float32)).astype(jnp.bfloat16)


def outer(chips, own, other, ids, out, summed, products):
    chip, core = lax.axis_index("dp"), lax.axis_index("mp")
    width = own.shape[1] // 6
    half = width // 2
    span = 3 * half // chips
    summed[...] = (own[...] + other[...]).T
    own_label = 2 * chip + core
    tail_label = jnp.where(core == 1, 2 * chip - 1, -1)
    masks = [(ids[...] == label).astype(jnp.float32) for label in (tail_label, own_label)]
    lane = lax.broadcasted_iota(jnp.int32, (half, 2 * width), 1)
    for module, (left, right) in enumerate(((0, 2), (1, 3), (4, 5))):
        factor = summed[left * width : (left + 1) * width, :]
        high, low = two_terms(jnp.concatenate([factor * mask for mask in masks], axis=0))
        top, bottom = two_terms(summed[right * width : (right + 1) * width, :])
        product = None
        for one, two in ((high, top), (high, bottom), (low, top)):
            both = jnp.concatenate([two, two], axis=0)
            term = lax.dot_general(one, both, NT, preferred_element_type=jnp.float32)
            product = term if product is None else product + term
        products[module] = product
        for label in range(2):
            even = products[module, pl.ds(label * width, half, stride=2), :]
            odd = products[module, pl.ds(label * width + 1, half, stride=2), :]
            packed = jnp.where(lane < width, even, odd)
            row = 0
            while row < half:
                chip_to, inside = divmod(module * half + row, span)
                count = min(span - inside, half - row)
                put = slice(label * span + inside, label * span + inside + count)
                out[chip_to, put, :] = packed[row : row + count]
                row += count


def example_blocks(chips, own, other, ids):
    width = own.shape[1] // 6
    block = (3 * width // chips, 2 * width)
    return pl.pallas_call(
        functools.partial(outer, chips),
        out_shape=jax.ShapeDtypeStruct((chips,) + block, jnp.float32),
        in_specs=[pl.BlockSpec(memory_space=pltpu.VMEM)] * 3,
        out_specs=pl.BlockSpec(memory_space=pltpu.VMEM),
        scratch_shapes=[
            pltpu.VMEM(own.shape[::-1], jnp.float32),
            pltpu.VMEM((3, 2 * width, 2 * width), jnp.float32),
        ],
        compiler_params=pltpu.CompilerParams(vmem_limit_bytes=6 * 2**20),
        name="outer",
    )(own, other, ids)


def score(queries, swapped, received, out, rows):
    core = lax.axis_index("mp")
    chips, height, lanes = received.shape
    span = height // 2
    rows[: chips * height, :] = received[...].reshape(chips * height, lanes)
    rows[chips * height :, :] = jnp.zeros((8, lanes), jnp.float32)
    grads = []
    for at in range(span):
        own = rows[pl.ds(span + at, chips, stride=height), :]
        tail = rows[pl.ds(at, chips, stride=height), :]
        tail = jnp.concatenate([tail[1:], jnp.zeros_like(tail[:1])], axis=0)
        grads.append(own + tail)
    terms = jnp.concatenate(two_terms(jnp.concatenate(grads, axis=1)), axis=0)
    coords = queries.shape[1]
    first = core == 0
    mine = jnp.where(first, terms[:, :coords], terms[:, coords:])
    theirs = jnp.where(first, terms[:, coords:], terms[:, :coords])
    scores = lax.dot_general(mine, queries[...], NT, preferred_element_type=jnp.float32)
    scores += lax.dot_general(theirs, swapped[...], NT, preferred_element_type=jnp.float32)
    out[...] = scores[:chips] + scores[chips:]


def partial_scores(queries, swapped, received):
    chips, height, lanes = received.shape
    return pl.pallas_call(
        score,
        out_shape=jax.ShapeDtypeStruct((chips, queries.shape[0]), jnp.float32),
        in_specs=[pl.BlockSpec(memory_space=pltpu.VMEM)] * 3,
        out_specs=pl.BlockSpec(memory_space=pltpu.VMEM),
        scratch_shapes=[pltpu.VMEM((chips * height + 8, lanes), jnp.float32)],
        compiler_params=pltpu.CompilerParams(vmem_limit_bytes=6 * 2**20),
        name="score",
    )(queries, swapped, received)


def body(
    inputs,
    gate_pre,
    up_pre,
    hidden_grad,
    out_grad,
    example_ids,
    gate_in,
    gate_out,
    up_in,
    up_out,
    down_in,
    down_out,
    queries,
):
    chips = lax.axis_size("dp")
    swap = [(0, 1), (1, 0)]
    swapped = lax.ppermute(queries, "mp", swap)
    bases = [base.T for base in (gate_in, gate_out, up_in, up_out, down_in, down_out)]
    own = projections(inputs, gate_pre, up_pre, hidden_grad, out_grad, *bases)
    other = lax.ppermute(own, "mp", swap)
    blocks = example_blocks(chips, own, other, example_ids.reshape(1, -1))
    received = lax.all_to_all(blocks, "dp", split_axis=0, concat_axis=0, tiled=True)
    scores = partial_scores(queries, swapped, received)[:, None]
    pieces = lax.all_to_all(scores, "dp", split_axis=0, concat_axis=0, tiled=True)
    return jnp.sum(pieces, axis=0)


def solution(mesh):
    placed = (
        P(("parts", "dp"), "mp"),
        P(("parts", "dp"), "mp"),
        P(("parts", "dp"), "mp"),
        P(("parts", "dp"), "mp"),
        P(("parts", "dp"), "mp"),
        P(("parts", "dp")),
        P("mp", None),
        P("mp", None),
        P("mp", None),
        P("mp", None),
        P("mp", None),
        P("mp", None),
        P(None, ("dp", "mp")),
    )
    return jax.shard_map(
        body, mesh=mesh, in_specs=placed, out_specs=P(("parts", "dp", "mp"), None), check_vma=False
    )
```

```python
import functools

import jax
import jax.numpy as jnp
from jax import lax
from jax.experimental import pallas as pl
from jax.experimental.pallas import tpu as pltpu
from jax.sharding import PartitionSpec as P

NT = (((1,), (1,)), ((), ()))
STEP = 1024
TILE = 256
ROWS = 16
AHEAD = 2


def project(
    inputs,
    gate_pre,
    up_pre,
    hidden_grad,
    out_grad,
    gate_in,
    gate_out,
    up_in,
    up_out,
    down_in,
    down_out,
    out,
    v_inputs,
    v_gate,
    v_up,
    v_back,
    v_out_grad,
    v_in,
    v_gate_out,
    v_up_out,
    v_down_in,
    v_down_out,
    sum_in,
    sums,
    sems,
):
    width = gate_in.shape[0]
    tokens = inputs.shape[0]
    hidden_steps = gate_pre.shape[1] // STEP
    model_steps = inputs.shape[1] // STEP
    copies = []

    def plan(pairs):
        made_here = []
        for source, target in pairs:
            copy = pltpu.make_async_copy(source, target, sems.at[sum(map(len, copies)) + len(made_here)])
            made_here.append(copy)
        copies.append(made_here)

    for step in range(hidden_steps):
        at = pl.ds(step * STEP, STEP)
        pairs = [
            (gate_pre.at[:, at], v_gate.at[:, at]),
            (up_pre.at[:, at], v_up.at[:, at]),
            (hidden_grad.at[:, at], v_back.at[:, at]),
            (gate_out.at[:, at], v_gate_out.at[:, at]),
            (up_out.at[:, at], v_up_out.at[:, at]),
            (down_in.at[:, at], v_down_in.at[:, at]),
        ]
        if step < model_steps:
            pairs += [
                (inputs.at[:, at], v_inputs.at[:, at]),
                (gate_in.at[:, at], v_in.at[pl.ds(0, width), at]),
                (up_in.at[:, at], v_in.at[pl.ds(width, width), at]),
                (out_grad.at[:, at], v_out_grad.at[:, at]),
                (down_out.at[:, at], v_down_out.at[:, at]),
            ]
        plan(pairs)

    def products(step, left):
        parts = []
        for top in range(0, tokens, ROWS):
            at = (slice(top, top + ROWS), slice(step * STEP + left, step * STEP + left + TILE))
            half = 0.5 * v_gate[at].astype(jnp.float32)
            up = v_up[at].astype(jnp.float32)
            back = v_back[at].astype(jnp.float32)
            tanh = jnp.tanh(half)
            plus = 1.0 + tanh
            silu = half * plus
            slope = plus + silu * (1.0 - tanh)
            values = (back * up * slope, back * silu, silu * up)
            parts.append([value.astype(jnp.bfloat16) for value in values])
        return [jnp.concatenate(column, axis=0) for column in zip(*parts)]

    def add(total, values, base, first):
        value = lax.dot_general(values, base, NT, preferred_element_type=jnp.float32)
        if first:
            total[...] = value
        else:
            total[...] += value

    def hidden_dots(step, left):
        at = slice(step * STEP + left, step * STEP + left + TILE)
        bases = (v_gate_out, v_up_out, v_down_in)
        for which, value in enumerate(products(step, left)):
            add(sums.at[which], value, bases[which][:, at], step == 0 and left == 0)

    def model_dots(left):
        at = slice(left, left + TILE)
        add(sum_in, v_inputs[:, at], v_in[:, at], left == 0)
        add(sums.at[3], v_out_grad[:, at], v_down_out[:, at], left == 0)

    for step in range(min(AHEAD, hidden_steps)):
        for copy in copies[step]:
            copy.start()
    for step in range(hidden_steps):
        if step + AHEAD < hidden_steps:
            for copy in copies[step + AHEAD]:
                copy.start()
        for copy in copies[step]:
            copy.wait()
        for left in range(0, STEP, TILE):
            hidden_dots(step, left)
            if step < model_steps:
                model_dots(step * STEP + left)
    out[:, : 2 * width] = sum_in[...]
    out[:, 2 * width : 4 * width] = jnp.concatenate([0.5 * sums[0], sums[1]], axis=1)
    out[:, 4 * width :] = jnp.concatenate([sums[2], sums[3]], axis=1)


def projections(*operands):
    inputs, gate_pre = operands[:2]
    width = operands[5].shape[0]
    tokens, model = inputs.shape
    hidden = gate_pre.shape[1]
    assert hidden % STEP == 0 and model % STEP == 0 and model <= hidden
    assert tokens % ROWS == 0
    steps = 6 * (hidden // STEP) + 5 * (model // STEP)
    bf16 = jnp.bfloat16
    return pl.pallas_call(
        project,
        out_shape=jax.ShapeDtypeStruct((tokens, 6 * width), jnp.float32),
        in_specs=[pl.BlockSpec(memory_space=pltpu.HBM)] * len(operands),
        out_specs=pl.BlockSpec(memory_space=pltpu.VMEM),
        scratch_shapes=[
            pltpu.VMEM((tokens, model), bf16),
            pltpu.VMEM((tokens, hidden), bf16),
            pltpu.VMEM((tokens, hidden), bf16),
            pltpu.VMEM((tokens, hidden), bf16),
            pltpu.VMEM((tokens, model), bf16),
            pltpu.VMEM((2 * width, model), bf16),
            pltpu.VMEM((width, hidden), bf16),
            pltpu.VMEM((width, hidden), bf16),
            pltpu.VMEM((width, hidden), bf16),
            pltpu.VMEM((width, model), bf16),
            pltpu.VMEM((tokens, 2 * width), jnp.float32),
            pltpu.VMEM((4, tokens, width), jnp.float32),
            pltpu.SemaphoreType.DMA((steps,)),
        ],
        compiler_params=pltpu.CompilerParams(vmem_limit_bytes=427 * 2**17),
        cost_estimate=pl.CostEstimate(
            flops=6 * tokens * width * (model + hidden),
            bytes_accessed=2 * (2 * tokens * model + 3 * tokens * hidden),
            transcendentals=tokens * hidden,
        ),
        name="project",
    )(*operands)


def two_terms(value):
    high = value.astype(jnp.bfloat16)
    return high, (value - high.astype(jnp.float32)).astype(jnp.bfloat16)


def outer(chips, own, other, ids, out, summed, products):
    chip, core = lax.axis_index("dp"), lax.axis_index("mp")
    width = own.shape[1] // 6
    half = width // 2
    span = 3 * half // chips
    summed[...] = (own[...] + other[...]).T
    own_label = 2 * chip + core
    tail_label = jnp.where(core == 1, 2 * chip - 1, -1)
    masks = [(ids[...] == label).astype(jnp.float32) for label in (tail_label, own_label)]
    lane = lax.broadcasted_iota(jnp.int32, (half, 2 * width), 1)
    for module, (left, right) in enumerate(((0, 2), (1, 3), (4, 5))):
        factor = summed[left * width : (left + 1) * width, :]
        high, low = two_terms(jnp.concatenate([factor * mask for mask in masks], axis=0))
        top, bottom = two_terms(summed[right * width : (right + 1) * width, :])
        product = None
        for one, two in ((high, top), (high, bottom), (low, top)):
            both = jnp.concatenate([two, two], axis=0)
            term = lax.dot_general(one, both, NT, preferred_element_type=jnp.float32)
            product = term if product is None else product + term
        products[module] = product
        for label in range(2):
            even = products[module, pl.ds(label * width, half, stride=2), :]
            odd = products[module, pl.ds(label * width + 1, half, stride=2), :]
            packed = jnp.where(lane < width, even, odd)
            row = 0
            while row < half:
                chip_to, inside = divmod(module * half + row, span)
                count = min(span - inside, half - row)
                put = slice(label * span + inside, label * span + inside + count)
                out[chip_to, put, :] = packed[row : row + count]
                row += count


def example_blocks(chips, own, other, ids):
    width = own.shape[1] // 6
    block = (3 * width // chips, 2 * width)
    return pl.pallas_call(
        functools.partial(outer, chips),
        out_shape=jax.ShapeDtypeStruct((chips,) + block, jnp.float32),
        in_specs=[pl.BlockSpec(memory_space=pltpu.VMEM)] * 3,
        out_specs=pl.BlockSpec(memory_space=pltpu.VMEM),
        scratch_shapes=[
            pltpu.VMEM(own.shape[::-1], jnp.float32),
            pltpu.VMEM((3, 2 * width, 2 * width), jnp.float32),
        ],
        compiler_params=pltpu.CompilerParams(vmem_limit_bytes=6 * 2**20),
        name="outer",
    )(own, other, ids)


def score(queries, swapped, received, out, rows):
    core = lax.axis_index("mp")
    chips, height, lanes = received.shape
    span = height // 2
    rows[: chips * height, :] = received[...].reshape(chips * height, lanes)
    rows[chips * height :, :] = jnp.zeros((8, lanes), jnp.float32)
    grads = []
    for at in range(span):
        own = rows[pl.ds(span + at, chips, stride=height), :]
        tail = rows[pl.ds(at, chips, stride=height), :]
        tail = jnp.concatenate([tail[1:], jnp.zeros_like(tail[:1])], axis=0)
        grads.append(own + tail)
    terms = jnp.concatenate(two_terms(jnp.concatenate(grads, axis=1)), axis=0)
    coords = queries.shape[1]
    first = core == 0
    mine = jnp.where(first, terms[:, :coords], terms[:, coords:])
    theirs = jnp.where(first, terms[:, coords:], terms[:, :coords])
    scores = lax.dot_general(mine, queries[...], NT, preferred_element_type=jnp.float32)
    scores += lax.dot_general(theirs, swapped[...], NT, preferred_element_type=jnp.float32)
    out[...] = scores[:chips] + scores[chips:]


def partial_scores(queries, swapped, received):
    chips, height, lanes = received.shape
    return pl.pallas_call(
        score,
        out_shape=jax.ShapeDtypeStruct((chips, queries.shape[0]), jnp.float32),
        in_specs=[pl.BlockSpec(memory_space=pltpu.VMEM)] * 3,
        out_specs=pl.BlockSpec(memory_space=pltpu.VMEM),
        scratch_shapes=[pltpu.VMEM((chips * height + 8, lanes), jnp.float32)],
        compiler_params=pltpu.CompilerParams(vmem_limit_bytes=6 * 2**20),
        name="score",
    )(queries, swapped, received)


def body(
    inputs,
    gate_pre,
    up_pre,
    hidden_grad,
    out_grad,
    example_ids,
    gate_in,
    gate_out,
    up_in,
    up_out,
    down_in,
    down_out,
    queries,
):
    chips = lax.axis_size("dp")
    swap = [(0, 1), (1, 0)]
    swapped = lax.ppermute(queries, "mp", swap)
    bases = [base.T for base in (gate_in, gate_out, up_in, up_out, down_in, down_out)]
    own = projections(inputs, gate_pre, up_pre, hidden_grad, out_grad, *bases)
    other = lax.ppermute(own, "mp", swap)
    blocks = example_blocks(chips, own, other, example_ids.reshape(1, -1))
    received = lax.all_to_all(blocks, "dp", split_axis=0, concat_axis=0, tiled=True)
    scores = partial_scores(queries, swapped, received)[:, None]
    pieces = lax.all_to_all(scores, "dp", split_axis=0, concat_axis=0, tiled=True)
    return jnp.sum(pieces, axis=0)


def solution(mesh):
    placed = (
        P(("parts", "dp"), "mp"),
        P(("parts", "dp"), "mp"),
        P(("parts", "dp"), "mp"),
        P(("parts", "dp"), "mp"),
        P(("parts", "dp"), "mp"),
        P(("parts", "dp")),
        P("mp", None),
        P("mp", None),
        P("mp", None),
        P("mp", None),
        P("mp", None),
        P("mp", None),
        P(None, ("dp", "mp")),
    )
    return jax.shard_map(
        body, mesh=mesh, in_specs=placed, out_specs=P(("parts", "dp", "mp"), None), check_vma=False
    )
```

```python
import functools

import jax
import jax.numpy as jnp
from jax import lax
from jax.experimental import pallas as pl
from jax.experimental.pallas import tpu as pltpu
from jax.sharding import PartitionSpec as P

NT = (((1,), (1,)), ((), ()))
STEP = 1024
TILE = 512
ROWS = 16
AHEAD = 2


def project(
    inputs,
    gate_pre,
    up_pre,
    hidden_grad,
    out_grad,
    gate_in,
    gate_out,
    up_in,
    up_out,
    down_in,
    down_out,
    out,
    v_inputs,
    v_gate,
    v_up,
    v_back,
    v_out_grad,
    v_in,
    v_gate_out,
    v_up_out,
    v_down_in,
    v_down_out,
    sum_in,
    sums,
    sems,
):
    width = gate_in.shape[0]
    tokens = inputs.shape[0]
    hidden_steps = gate_pre.shape[1] // STEP
    model_steps = inputs.shape[1] // STEP
    copies = []

    def plan(pairs):
        made_here = []
        for source, target in pairs:
            copy = pltpu.make_async_copy(source, target, sems.at[sum(map(len, copies)) + len(made_here)])
            made_here.append(copy)
        copies.append(made_here)

    for step in range(hidden_steps):
        at = pl.ds(step * STEP, STEP)
        pairs = [
            (gate_pre.at[:, at], v_gate.at[:, at]),
            (up_pre.at[:, at], v_up.at[:, at]),
            (hidden_grad.at[:, at], v_back.at[:, at]),
            (gate_out.at[:, at], v_gate_out.at[:, at]),
            (up_out.at[:, at], v_up_out.at[:, at]),
            (down_in.at[:, at], v_down_in.at[:, at]),
        ]
        if step < model_steps:
            pairs += [
                (inputs.at[:, at], v_inputs.at[:, at]),
                (gate_in.at[:, at], v_in.at[pl.ds(0, width), at]),
                (up_in.at[:, at], v_in.at[pl.ds(width, width), at]),
                (out_grad.at[:, at], v_out_grad.at[:, at]),
                (down_out.at[:, at], v_down_out.at[:, at]),
            ]
        plan(pairs)

    def products(step, left):
        parts = []
        for top in range(0, tokens, ROWS):
            at = (slice(top, top + ROWS), slice(step * STEP + left, step * STEP + left + TILE))
            half = 0.5 * v_gate[at].astype(jnp.float32)
            up = v_up[at].astype(jnp.float32)
            back = v_back[at].astype(jnp.float32)
            tanh = jnp.tanh(half)
            plus = 1.0 + tanh
            silu = half * plus
            slope = plus + silu * (1.0 - tanh)
            values = (back * up * slope, back * silu, silu * up)
            parts.append([value.astype(jnp.bfloat16) for value in values])
        return [jnp.concatenate(column, axis=0) for column in zip(*parts)]

    def add(total, values, base, first):
        value = lax.dot_general(values, base, NT, preferred_element_type=jnp.float32)
        if first:
            total[...] = value
        else:
            total[...] += value

    def hidden_dots(step, left):
        at = slice(step * STEP + left, step * STEP + left + TILE)
        bases = (v_gate_out, v_up_out, v_down_in)
        for which, value in enumerate(products(step, left)):
            add(sums.at[which], value, bases[which][:, at], step == 0 and left == 0)

    def model_dots(left):
        at = slice(left, left + TILE)
        add(sum_in, v_inputs[:, at], v_in[:, at], left == 0)
        add(sums.at[3], v_out_grad[:, at], v_down_out[:, at], left == 0)

    for step in range(min(AHEAD, hidden_steps)):
        for copy in copies[step]:
            copy.start()
    for step in range(hidden_steps):
        if step + AHEAD < hidden_steps:
            for copy in copies[step + AHEAD]:
                copy.start()
        for copy in copies[step]:
            copy.wait()
        for left in range(0, STEP, TILE):
            hidden_dots(step, left)
            if step < model_steps:
                model_dots(step * STEP + left)
    out[:, : 2 * width] = sum_in[...]
    out[:, 2 * width : 4 * width] = jnp.concatenate([0.5 * sums[0], sums[1]], axis=1)
    out[:, 4 * width :] = jnp.concatenate([sums[2], sums[3]], axis=1)


def projections(*operands):
    inputs, gate_pre = operands[:2]
    width = operands[5].shape[0]
    tokens, model = inputs.shape
    hidden = gate_pre.shape[1]
    assert hidden % STEP == 0 and model % STEP == 0 and model <= hidden
    assert tokens % ROWS == 0
    steps = 6 * (hidden // STEP) + 5 * (model // STEP)
    bf16 = jnp.bfloat16
    return pl.pallas_call(
        project,
        out_shape=jax.ShapeDtypeStruct((tokens, 6 * width), jnp.float32),
        in_specs=[pl.BlockSpec(memory_space=pltpu.HBM)] * len(operands),
        out_specs=pl.BlockSpec(memory_space=pltpu.VMEM),
        scratch_shapes=[
            pltpu.VMEM((tokens, model), bf16),
            pltpu.VMEM((tokens, hidden), bf16),
            pltpu.VMEM((tokens, hidden), bf16),
            pltpu.VMEM((tokens, hidden), bf16),
            pltpu.VMEM((tokens, model), bf16),
            pltpu.VMEM((2 * width, model), bf16),
            pltpu.VMEM((width, hidden), bf16),
            pltpu.VMEM((width, hidden), bf16),
            pltpu.VMEM((width, hidden), bf16),
            pltpu.VMEM((width, model), bf16),
            pltpu.VMEM((tokens, 2 * width), jnp.float32),
            pltpu.VMEM((4, tokens, width), jnp.float32),
            pltpu.SemaphoreType.DMA((steps,)),
        ],
        compiler_params=pltpu.CompilerParams(vmem_limit_bytes=427 * 2**17),
        cost_estimate=pl.CostEstimate(
            flops=6 * tokens * width * (model + hidden),
            bytes_accessed=2 * (2 * tokens * model + 3 * tokens * hidden),
            transcendentals=tokens * hidden,
        ),
        name="project",
    )(*operands)


def two_terms(value):
    high = value.astype(jnp.bfloat16)
    return high, (value - high.astype(jnp.float32)).astype(jnp.bfloat16)


def outer(chips, own, other, ids, out, summed, products):
    chip, core = lax.axis_index("dp"), lax.axis_index("mp")
    width = own.shape[1] // 6
    half = width // 2
    span = 3 * half // chips
    summed[...] = (own[...] + other[...]).T
    own_label = 2 * chip + core
    tail_label = jnp.where(core == 1, 2 * chip - 1, -1)
    masks = [(ids[...] == label).astype(jnp.float32) for label in (tail_label, own_label)]
    lane = lax.broadcasted_iota(jnp.int32, (half, 2 * width), 1)
    for module, (left, right) in enumerate(((0, 2), (1, 3), (4, 5))):
        factor = summed[left * width : (left + 1) * width, :]
        high, low = two_terms(jnp.concatenate([factor * mask for mask in masks], axis=0))
        top, bottom = two_terms(summed[right * width : (right + 1) * width, :])
        product = None
        for one, two in ((high, top), (high, bottom), (low, top)):
            both = jnp.concatenate([two, two], axis=0)
            term = lax.dot_general(one, both, NT, preferred_element_type=jnp.float32)
            product = term if product is None else product + term
        products[module] = product
        for label in range(2):
            even = products[module, pl.ds(label * width, half, stride=2), :]
            odd = products[module, pl.ds(label * width + 1, half, stride=2), :]
            packed = jnp.where(lane < width, even, odd)
            row = 0
            while row < half:
                chip_to, inside = divmod(module * half + row, span)
                count = min(span - inside, half - row)
                put = slice(label * span + inside, label * span + inside + count)
                out[chip_to, put, :] = packed[row : row + count]
                row += count


def example_blocks(chips, own, other, ids):
    width = own.shape[1] // 6
    block = (3 * width // chips, 2 * width)
    return pl.pallas_call(
        functools.partial(outer, chips),
        out_shape=jax.ShapeDtypeStruct((chips,) + block, jnp.float32),
        in_specs=[pl.BlockSpec(memory_space=pltpu.VMEM)] * 3,
        out_specs=pl.BlockSpec(memory_space=pltpu.VMEM),
        scratch_shapes=[
            pltpu.VMEM(own.shape[::-1], jnp.float32),
            pltpu.VMEM((3, 2 * width, 2 * width), jnp.float32),
        ],
        compiler_params=pltpu.CompilerParams(vmem_limit_bytes=6 * 2**20),
        name="outer",
    )(own, other, ids)


def score(queries, swapped, received, out, rows):
    core = lax.axis_index("mp")
    chips, height, lanes = received.shape
    span = height // 2
    rows[: chips * height, :] = received[...].reshape(chips * height, lanes)
    rows[chips * height :, :] = jnp.zeros((8, lanes), jnp.float32)
    grads = []
    for at in range(span):
        own = rows[pl.ds(span + at, chips, stride=height), :]
        tail = rows[pl.ds(at, chips, stride=height), :]
        tail = jnp.concatenate([tail[1:], jnp.zeros_like(tail[:1])], axis=0)
        grads.append(own + tail)
    terms = jnp.concatenate(two_terms(jnp.concatenate(grads, axis=1)), axis=0)
    coords = queries.shape[1]
    first = core == 0
    mine = jnp.where(first, terms[:, :coords], terms[:, coords:])
    theirs = jnp.where(first, terms[:, coords:], terms[:, :coords])
    scores = lax.dot_general(mine, queries[...], NT, preferred_element_type=jnp.float32)
    scores += lax.dot_general(theirs, swapped[...], NT, preferred_element_type=jnp.float32)
    out[...] = scores[:chips] + scores[chips:]


def partial_scores(queries, swapped, received):
    chips, height, lanes = received.shape
    return pl.pallas_call(
        score,
        out_shape=jax.ShapeDtypeStruct((chips, queries.shape[0]), jnp.float32),
        in_specs=[pl.BlockSpec(memory_space=pltpu.VMEM)] * 3,
        out_specs=pl.BlockSpec(memory_space=pltpu.VMEM),
        scratch_shapes=[pltpu.VMEM((chips * height + 8, lanes), jnp.float32)],
        compiler_params=pltpu.CompilerParams(vmem_limit_bytes=6 * 2**20),
        name="score",
    )(queries, swapped, received)


def body(
    inputs,
    gate_pre,
    up_pre,
    hidden_grad,
    out_grad,
    example_ids,
    gate_in,
    gate_out,
    up_in,
    up_out,
    down_in,
    down_out,
    queries,
):
    chips = lax.axis_size("dp")
    swap = [(0, 1), (1, 0)]
    swapped = lax.ppermute(queries, "mp", swap)
    bases = [base.T for base in (gate_in, gate_out, up_in, up_out, down_in, down_out)]
    own = projections(inputs, gate_pre, up_pre, hidden_grad, out_grad, *bases)
    other = lax.ppermute(own, "mp", swap)
    blocks = example_blocks(chips, own, other, example_ids.reshape(1, -1))
    received = lax.all_to_all(blocks, "dp", split_axis=0, concat_axis=0, tiled=True)
    scores = partial_scores(queries, swapped, received)[:, None]
    pieces = lax.all_to_all(scores, "dp", split_axis=0, concat_axis=0, tiled=True)
    return jnp.sum(pieces, axis=0)


def solution(mesh):
    placed = (
        P(("parts", "dp"), "mp"),
        P(("parts", "dp"), "mp"),
        P(("parts", "dp"), "mp"),
        P(("parts", "dp"), "mp"),
        P(("parts", "dp"), "mp"),
        P(("parts", "dp")),
        P("mp", None),
        P("mp", None),
        P("mp", None),
        P("mp", None),
        P("mp", None),
        P("mp", None),
        P(None, ("dp", "mp")),
    )
    return jax.shard_map(
        body, mesh=mesh, in_specs=placed, out_specs=P(("parts", "dp", "mp"), None), check_vma=False
    )
```

```python
import functools

import jax
import jax.numpy as jnp
from jax import lax
from jax.experimental import pallas as pl
from jax.experimental.pallas import tpu as pltpu
from jax.sharding import PartitionSpec as P

NT = (((1,), (1,)), ((), ()))
STEP = 1024
TILE = 256
ROWS = 16
AHEAD = 2


def project(
    inputs,
    gate_pre,
    up_pre,
    hidden_grad,
    out_grad,
    gate_in,
    gate_out,
    up_in,
    up_out,
    down_in,
    down_out,
    out,
    v_inputs,
    v_gate,
    v_up,
    v_back,
    v_out_grad,
    v_in,
    v_gate_out,
    v_up_out,
    v_down_in,
    v_down_out,
    sum_in,
    sums,
    sems,
):
    width = gate_in.shape[0]
    tokens = inputs.shape[0]
    hidden_steps = gate_pre.shape[1] // STEP
    model_steps = inputs.shape[1] // STEP
    copies = []

    def plan(pairs):
        made_here = []
        for source, target in pairs:
            copy = pltpu.make_async_copy(source, target, sems.at[sum(map(len, copies)) + len(made_here)])
            made_here.append(copy)
        copies.append(made_here)

    for step in range(hidden_steps):
        at = pl.ds(step * STEP, STEP)
        pairs = [
            (gate_pre.at[:, at], v_gate.at[:, at]),
            (up_pre.at[:, at], v_up.at[:, at]),
            (hidden_grad.at[:, at], v_back.at[:, at]),
            (gate_out.at[:, at], v_gate_out.at[:, at]),
            (up_out.at[:, at], v_up_out.at[:, at]),
            (down_in.at[:, at], v_down_in.at[:, at]),
        ]
        if step < model_steps:
            pairs += [
                (inputs.at[:, at], v_inputs.at[:, at]),
                (gate_in.at[:, at], v_in.at[pl.ds(0, width), at]),
                (up_in.at[:, at], v_in.at[pl.ds(width, width), at]),
                (out_grad.at[:, at], v_out_grad.at[:, at]),
                (down_out.at[:, at], v_down_out.at[:, at]),
            ]
        plan(pairs)

    def products(step, left):
        parts = []
        for top in range(0, tokens, ROWS):
            at = (slice(top, top + ROWS), slice(step * STEP + left, step * STEP + left + TILE))
            half = 0.5 * v_gate[at].astype(jnp.float32)
            up = v_up[at].astype(jnp.float32)
            back = v_back[at].astype(jnp.float32)
            tanh = jnp.tanh(half)
            plus = 1.0 + tanh
            silu = half * plus
            slope = plus + silu * (1.0 - tanh)
            values = (back * up * slope, back * silu, silu * up)
            parts.append([value.astype(jnp.bfloat16) for value in values])
        return [jnp.concatenate(column, axis=0) for column in zip(*parts)]

    def add(total, values, base, first):
        value = lax.dot_general(values, base, NT, preferred_element_type=jnp.float32)
        if first:
            total[...] = value
        else:
            total[...] += value

    def hidden_dots(step, left):
        at = slice(step * STEP + left, step * STEP + left + TILE)
        bases = (v_gate_out, v_up_out, v_down_in)
        for which, value in enumerate(products(step, left)):
            add(sums.at[which], value, bases[which][:, at], step == 0 and left == 0)

    def model_dots(left):
        at = slice(left, left + TILE)
        add(sum_in, v_inputs[:, at], v_in[:, at], left == 0)
        add(sums.at[3], v_out_grad[:, at], v_down_out[:, at], left == 0)

    for step in range(min(AHEAD, hidden_steps)):
        for copy in copies[step]:
            copy.start()
    for step in range(hidden_steps):
        if step + AHEAD < hidden_steps:
            for copy in copies[step + AHEAD]:
                copy.start()
        for copy in copies[step]:
            copy.wait()
        for left in range(0, STEP, TILE):
            hidden_dots(step, left)
            if step < model_steps:
                model_dots(step * STEP + left)
    out[:, : 2 * width] = sum_in[...]
    out[:, 2 * width : 4 * width] = jnp.concatenate([0.5 * sums[0], sums[1]], axis=1)
    out[:, 4 * width :] = jnp.concatenate([sums[2], sums[3]], axis=1)


def projections(*operands):
    inputs, gate_pre = operands[:2]
    width = operands[5].shape[0]
    tokens, model = inputs.shape
    hidden = gate_pre.shape[1]
    assert hidden % STEP == 0 and model % STEP == 0 and model <= hidden
    assert tokens % ROWS == 0
    steps = 6 * (hidden // STEP) + 5 * (model // STEP)
    bf16 = jnp.bfloat16
    return pl.pallas_call(
        project,
        out_shape=jax.ShapeDtypeStruct((tokens, 6 * width), jnp.float32),
        in_specs=[pl.BlockSpec(memory_space=pltpu.HBM)] * len(operands),
        out_specs=pl.BlockSpec(memory_space=pltpu.VMEM),
        scratch_shapes=[
            pltpu.VMEM((tokens, model), bf16),
            pltpu.VMEM((tokens, hidden), bf16),
            pltpu.VMEM((tokens, hidden), bf16),
            pltpu.VMEM((tokens, hidden), bf16),
            pltpu.VMEM((tokens, model), bf16),
            pltpu.VMEM((2 * width, model), bf16),
            pltpu.VMEM((width, hidden), bf16),
            pltpu.VMEM((width, hidden), bf16),
            pltpu.VMEM((width, hidden), bf16),
            pltpu.VMEM((width, model), bf16),
            pltpu.VMEM((tokens, 2 * width), jnp.float32),
            pltpu.VMEM((4, tokens, width), jnp.float32),
            pltpu.SemaphoreType.DMA((steps,)),
        ],
        compiler_params=pltpu.CompilerParams(vmem_limit_bytes=427 * 2**17),
        cost_estimate=pl.CostEstimate(
            flops=6 * tokens * width * (model + hidden),
            bytes_accessed=2 * (2 * tokens * model + 3 * tokens * hidden),
            transcendentals=tokens * hidden,
        ),
        name="project",
    )(*operands)


def two_terms(value):
    high = value.astype(jnp.bfloat16)
    return high, (value - high.astype(jnp.float32)).astype(jnp.bfloat16)


def outer(chips, own, other, ids, out, summed, products):
    chip, core = lax.axis_index("dp"), lax.axis_index("mp")
    width = own.shape[1] // 6
    half = width // 2
    span = 3 * half // chips
    summed[...] = (own[...] + other[...]).T
    own_label = 2 * chip + core
    tail_label = jnp.where(core == 1, 2 * chip - 1, -1)
    masks = [(ids[...] == label).astype(jnp.float32) for label in (tail_label, own_label)]
    lane = lax.broadcasted_iota(jnp.int32, (half, 2 * width), 1)
    for module, (left, right) in enumerate(((0, 2), (1, 3), (4, 5))):
        factor = summed[left * width : (left + 1) * width, :]
        high, low = two_terms(jnp.concatenate([factor * mask for mask in masks], axis=0))
        top, bottom = two_terms(summed[right * width : (right + 1) * width, :])
        product = None
        for one, two in ((high, top), (high, bottom), (low, top)):
            both = jnp.concatenate([two, two], axis=0)
            term = lax.dot_general(one, both, NT, preferred_element_type=jnp.float32)
            product = term if product is None else product + term
        products[module] = product
        for label in range(2):
            even = products[module, pl.ds(label * width, half, stride=2), :]
            odd = products[module, pl.ds(label * width + 1, half, stride=2), :]
            packed = jnp.where(lane < width, even, odd)
            row = 0
            while row < half:
                chip_to, inside = divmod(module * half + row, span)
                count = min(span - inside, half - row)
                put = slice(label * span + inside, label * span + inside + count)
                out[chip_to, put, :] = packed[row : row + count]
                row += count


def example_blocks(chips, own, other, ids):
    width = own.shape[1] // 6
    block = (3 * width // chips, 2 * width)
    return pl.pallas_call(
        functools.partial(outer, chips),
        out_shape=jax.ShapeDtypeStruct((chips,) + block, jnp.float32),
        in_specs=[pl.BlockSpec(memory_space=pltpu.VMEM)] * 3,
        out_specs=pl.BlockSpec(memory_space=pltpu.VMEM),
        scratch_shapes=[
            pltpu.VMEM(own.shape[::-1], jnp.float32),
            pltpu.VMEM((3, 2 * width, 2 * width), jnp.float32),
        ],
        compiler_params=pltpu.CompilerParams(vmem_limit_bytes=6 * 2**20),
        name="outer",
    )(own, other, ids)


def score(queries, swapped, received, out, rows):
    core = lax.axis_index("mp")
    chips, height, lanes = received.shape
    span = height // 2
    rows[: chips * height, :] = received[...].reshape(chips * height, lanes)
    rows[chips * height :, :] = jnp.zeros((8, lanes), jnp.float32)
    grads = []
    for at in range(span):
        own = rows[pl.ds(span + at, chips, stride=height), :]
        tail = rows[pl.ds(at, chips, stride=height), :]
        tail = jnp.concatenate([tail[1:], jnp.zeros_like(tail[:1])], axis=0)
        grads.append(own + tail)
    terms = jnp.concatenate(two_terms(jnp.concatenate(grads, axis=1)), axis=0)
    coords = queries.shape[1]
    first = core == 0
    mine = jnp.where(first, terms[:, :coords], terms[:, coords:])
    theirs = jnp.where(first, terms[:, coords:], terms[:, :coords])
    scores = lax.dot_general(mine, queries[...], NT, preferred_element_type=jnp.float32)
    scores += lax.dot_general(theirs, swapped[...], NT, preferred_element_type=jnp.float32)
    out[...] = scores[:chips] + scores[chips:]


def partial_scores(queries, swapped, received):
    chips, height, lanes = received.shape
    return pl.pallas_call(
        score,
        out_shape=jax.ShapeDtypeStruct((chips, queries.shape[0]), jnp.float32),
        in_specs=[pl.BlockSpec(memory_space=pltpu.VMEM)] * 3,
        out_specs=pl.BlockSpec(memory_space=pltpu.VMEM),
        scratch_shapes=[pltpu.VMEM((chips * height + 8, lanes), jnp.float32)],
        compiler_params=pltpu.CompilerParams(vmem_limit_bytes=6 * 2**20),
        name="score",
    )(queries, swapped, received)


def body(
    inputs,
    gate_pre,
    up_pre,
    hidden_grad,
    out_grad,
    example_ids,
    gate_in,
    gate_out,
    up_in,
    up_out,
    down_in,
    down_out,
    queries,
):
    chips = lax.axis_size("dp")
    swap = [(0, 1), (1, 0)]
    bases = [base.T for base in (gate_in, gate_out, up_in, up_out, down_in, down_out)]
    own = projections(inputs, gate_pre, up_pre, hidden_grad, out_grad, *bases)
    own, queries = lax.optimization_barrier((own, queries))
    other = lax.ppermute(own, "mp", swap)
    swapped = lax.ppermute(queries, "mp", swap)
    blocks = example_blocks(chips, own, other, example_ids.reshape(1, -1))
    received = lax.all_to_all(blocks, "dp", split_axis=0, concat_axis=0, tiled=True)
    scores = partial_scores(queries, swapped, received)[:, None]
    pieces = lax.all_to_all(scores, "dp", split_axis=0, concat_axis=0, tiled=True)
    return jnp.sum(pieces, axis=0)


def solution(mesh):
    placed = (
        P(("parts", "dp"), "mp"),
        P(("parts", "dp"), "mp"),
        P(("parts", "dp"), "mp"),
        P(("parts", "dp"), "mp"),
        P(("parts", "dp"), "mp"),
        P(("parts", "dp")),
        P("mp", None),
        P("mp", None),
        P("mp", None),
        P("mp", None),
        P("mp", None),
        P("mp", None),
        P(None, ("dp", "mp")),
    )
    return jax.shard_map(
        body, mesh=mesh, in_specs=placed, out_specs=P(("parts", "dp", "mp"), None), check_vma=False
    )
```

```python
import functools

import jax
import jax.numpy as jnp
from jax import lax
from jax.experimental import pallas as pl
from jax.experimental.pallas import tpu as pltpu
from jax.sharding import PartitionSpec as P

NT = (((1,), (1,)), ((), ()))
STEP = 1024
TILE = 256
ROWS = 16
AHEAD = 2


def project(
    inputs,
    gate_pre,
    up_pre,
    hidden_grad,
    out_grad,
    gate_in,
    gate_out,
    up_in,
    up_out,
    down_in,
    down_out,
    out,
    v_inputs,
    v_gate,
    v_up,
    v_back,
    v_out_grad,
    v_in,
    v_gate_out,
    v_up_out,
    v_down_in,
    v_down_out,
    sum_in,
    sums,
    sems,
):
    width = gate_in.shape[0]
    tokens = inputs.shape[0]
    hidden, model = gate_pre.shape[1], inputs.shape[1]
    steps = hidden // STEP
    activations = ((gate_pre, v_gate), (up_pre, v_up), (hidden_grad, v_back))
    hidden_bases = ((gate_out, v_gate_out), (up_out, v_up_out), (down_in, v_down_in))
    model_bases = (
        (gate_in, v_in.at[pl.ds(0, width), :]),
        (up_in, v_in.at[pl.ds(width, width), :]),
        (down_out, v_down_out),
    )
    tokens_wide = ((inputs, v_inputs), (out_grad, v_out_grad))
    first_model = 2
    groups = []
    for step in range(steps):
        pairs = [(pair, step * STEP, STEP) for pair in activations]
        if step == 0:
            pairs += [(pair, 0, hidden // 2) for pair in hidden_bases]
        if step == steps // 2:
            pairs += [(pair, hidden // 2, hidden // 2) for pair in hidden_bases]
        if step == first_model - 1:
            pairs += [(pair, 0, model) for pair in model_bases]
        if step == first_model:
            pairs += [(pair, 0, model // 2) for pair in tokens_wide]
        if step == first_model + model // STEP // 2:
            pairs += [(pair, model // 2, model // 2) for pair in tokens_wide]
        groups.append(pairs)

    def start(step):
        for (source, target), low, length in groups[step]:
            at = pl.ds(low, length)
            pltpu.make_async_copy(source.at[:, at], target.at[:, at], sems.at[step]).start()

    def wait(step):
        count = sum(source.shape[0] * length for (source, _), _, length in groups[step])
        at = pl.ds(0, count // tokens)
        pltpu.make_async_copy(gate_pre.at[:, at], v_gate.at[:, at], sems.at[step]).wait()

    def products(step, left):
        parts = []
        for top in range(0, tokens, ROWS):
            at = (slice(top, top + ROWS), slice(step * STEP + left, step * STEP + left + TILE))
            half = 0.5 * v_gate[at].astype(jnp.float32)
            up = v_up[at].astype(jnp.float32)
            back = v_back[at].astype(jnp.float32)
            tanh = jnp.tanh(half)
            plus = 1.0 + tanh
            silu = half * plus
            slope = plus + silu * (1.0 - tanh)
            values = (back * up * slope, back * silu, silu * up)
            parts.append([value.astype(jnp.bfloat16) for value in values])
        return [jnp.concatenate(column, axis=0) for column in zip(*parts)]

    def add(total, values, base, first):
        value = lax.dot_general(values, base, NT, preferred_element_type=jnp.float32)
        if first:
            total[...] = value
        else:
            total[...] += value

    def hidden_dots(step, left):
        at = slice(step * STEP + left, step * STEP + left + TILE)
        bases = (v_gate_out, v_up_out, v_down_in)
        for which, value in enumerate(products(step, left)):
            add(sums.at[which], value, bases[which][:, at], step == 0 and left == 0)

    def model_dots(left):
        at = slice(left, left + TILE)
        add(sum_in, v_inputs[:, at], v_in[:, at], left == 0)
        add(sums.at[3], v_out_grad[:, at], v_down_out[:, at], left == 0)

    for step in range(AHEAD):
        start(step)
    for step in range(steps):
        if step + AHEAD < steps:
            start(step + AHEAD)
        wait(step)
        for left in range(0, STEP, TILE):
            hidden_dots(step, left)
            model_left = (step - first_model) * STEP + left
            if 0 <= model_left < model:
                model_dots(model_left)
    out[:, : 2 * width] = sum_in[...]
    out[:, 2 * width : 4 * width] = jnp.concatenate([0.5 * sums[0], sums[1]], axis=1)
    out[:, 4 * width :] = jnp.concatenate([sums[2], sums[3]], axis=1)


def projections(*operands):
    inputs, gate_pre = operands[:2]
    width = operands[5].shape[0]
    tokens, model = inputs.shape
    hidden = gate_pre.shape[1]
    assert hidden % STEP == 0 and model % (2 * STEP) == 0 and tokens % ROWS == 0
    assert 2 * STEP + model <= hidden and hidden % 256 == 0 and tokens == 3 * width
    bf16 = jnp.bfloat16
    return pl.pallas_call(
        project,
        out_shape=jax.ShapeDtypeStruct((tokens, 6 * width), jnp.float32),
        in_specs=[pl.BlockSpec(memory_space=pltpu.HBM)] * len(operands),
        out_specs=pl.BlockSpec(memory_space=pltpu.VMEM),
        scratch_shapes=[
            pltpu.VMEM((tokens, model), bf16),
            pltpu.VMEM((tokens, hidden), bf16),
            pltpu.VMEM((tokens, hidden), bf16),
            pltpu.VMEM((tokens, hidden), bf16),
            pltpu.VMEM((tokens, model), bf16),
            pltpu.VMEM((2 * width, model), bf16),
            pltpu.VMEM((width, hidden), bf16),
            pltpu.VMEM((width, hidden), bf16),
            pltpu.VMEM((width, hidden), bf16),
            pltpu.VMEM((width, model), bf16),
            pltpu.VMEM((tokens, 2 * width), jnp.float32),
            pltpu.VMEM((4, tokens, width), jnp.float32),
            pltpu.SemaphoreType.DMA((hidden // STEP,)),
        ],
        compiler_params=pltpu.CompilerParams(vmem_limit_bytes=427 * 2**17),
        cost_estimate=pl.CostEstimate(
            flops=6 * tokens * width * (model + hidden),
            bytes_accessed=2 * (2 * tokens * model + 3 * tokens * hidden),
            transcendentals=tokens * hidden,
        ),
        name="project",
    )(*operands)


def two_terms(value):
    high = value.astype(jnp.bfloat16)
    return high, (value - high.astype(jnp.float32)).astype(jnp.bfloat16)


def outer(chips, own, other, ids, out, summed, products):
    chip, core = lax.axis_index("dp"), lax.axis_index("mp")
    width = own.shape[1] // 6
    half = width // 2
    span = 3 * half // chips
    summed[...] = (own[...] + other[...]).T
    own_label = 2 * chip + core
    tail_label = jnp.where(core == 1, 2 * chip - 1, -1)
    masks = [(ids[...] == label).astype(jnp.float32) for label in (tail_label, own_label)]
    lane = lax.broadcasted_iota(jnp.int32, (half, 2 * width), 1)
    for module, (left, right) in enumerate(((0, 2), (1, 3), (4, 5))):
        factor = summed[left * width : (left + 1) * width, :]
        high, low = two_terms(jnp.concatenate([factor * mask for mask in masks], axis=0))
        top, bottom = two_terms(summed[right * width : (right + 1) * width, :])
        product = None
        for one, two in ((high, top), (high, bottom), (low, top)):
            both = jnp.concatenate([two, two], axis=0)
            term = lax.dot_general(one, both, NT, preferred_element_type=jnp.float32)
            product = term if product is None else product + term
        products[module] = product
        for label in range(2):
            even = products[module, pl.ds(label * width, half, stride=2), :]
            odd = products[module, pl.ds(label * width + 1, half, stride=2), :]
            packed = jnp.where(lane < width, even, odd)
            row = 0
            while row < half:
                chip_to, inside = divmod(module * half + row, span)
                count = min(span - inside, half - row)
                put = slice(label * span + inside, label * span + inside + count)
                out[chip_to, put, :] = packed[row : row + count]
                row += count


def example_blocks(chips, own, other, ids):
    width = own.shape[1] // 6
    block = (3 * width // chips, 2 * width)
    return pl.pallas_call(
        functools.partial(outer, chips),
        out_shape=jax.ShapeDtypeStruct((chips,) + block, jnp.float32),
        in_specs=[pl.BlockSpec(memory_space=pltpu.VMEM)] * 3,
        out_specs=pl.BlockSpec(memory_space=pltpu.VMEM),
        scratch_shapes=[
            pltpu.VMEM(own.shape[::-1], jnp.float32),
            pltpu.VMEM((3, 2 * width, 2 * width), jnp.float32),
        ],
        compiler_params=pltpu.CompilerParams(vmem_limit_bytes=6 * 2**20),
        name="outer",
    )(own, other, ids)


def score(queries, swapped, received, out, rows):
    core = lax.axis_index("mp")
    chips, height, lanes = received.shape
    span = height // 2
    rows[: chips * height, :] = received[...].reshape(chips * height, lanes)
    rows[chips * height :, :] = jnp.zeros((8, lanes), jnp.float32)
    grads = []
    for at in range(span):
        own = rows[pl.ds(span + at, chips, stride=height), :]
        tail = rows[pl.ds(at, chips, stride=height), :]
        tail = jnp.concatenate([tail[1:], jnp.zeros_like(tail[:1])], axis=0)
        grads.append(own + tail)
    terms = jnp.concatenate(two_terms(jnp.concatenate(grads, axis=1)), axis=0)
    coords = queries.shape[1]
    first = core == 0
    mine = jnp.where(first, terms[:, :coords], terms[:, coords:])
    theirs = jnp.where(first, terms[:, coords:], terms[:, :coords])
    scores = lax.dot_general(mine, queries[...], NT, preferred_element_type=jnp.float32)
    scores += lax.dot_general(theirs, swapped[...], NT, preferred_element_type=jnp.float32)
    out[...] = scores[:chips] + scores[chips:]


def partial_scores(queries, swapped, received):
    chips, height, lanes = received.shape
    return pl.pallas_call(
        score,
        out_shape=jax.ShapeDtypeStruct((chips, queries.shape[0]), jnp.float32),
        in_specs=[pl.BlockSpec(memory_space=pltpu.VMEM)] * 3,
        out_specs=pl.BlockSpec(memory_space=pltpu.VMEM),
        scratch_shapes=[pltpu.VMEM((chips * height + 8, lanes), jnp.float32)],
        compiler_params=pltpu.CompilerParams(vmem_limit_bytes=6 * 2**20),
        name="score",
    )(queries, swapped, received)


def body(
    inputs,
    gate_pre,
    up_pre,
    hidden_grad,
    out_grad,
    example_ids,
    gate_in,
    gate_out,
    up_in,
    up_out,
    down_in,
    down_out,
    queries,
):
    chips = lax.axis_size("dp")
    swap = [(0, 1), (1, 0)]
    swapped = lax.ppermute(queries, "mp", swap)
    bases = [base.T for base in (gate_in, gate_out, up_in, up_out, down_in, down_out)]
    own = projections(inputs, gate_pre, up_pre, hidden_grad, out_grad, *bases)
    other = lax.ppermute(own, "mp", swap)
    blocks = example_blocks(chips, own, other, example_ids.reshape(1, -1))
    received = lax.all_to_all(blocks, "dp", split_axis=0, concat_axis=0, tiled=True)
    scores = partial_scores(queries, swapped, received)[:, None]
    pieces = lax.all_to_all(scores, "dp", split_axis=0, concat_axis=0, tiled=True)
    return jnp.sum(pieces, axis=0)


def solution(mesh):
    placed = (
        P(("parts", "dp"), "mp"),
        P(("parts", "dp"), "mp"),
        P(("parts", "dp"), "mp"),
        P(("parts", "dp"), "mp"),
        P(("parts", "dp"), "mp"),
        P(("parts", "dp")),
        P("mp", None),
        P("mp", None),
        P("mp", None),
        P("mp", None),
        P("mp", None),
        P("mp", None),
        P(None, ("dp", "mp")),
    )
    return jax.shard_map(
        body, mesh=mesh, in_specs=placed, out_specs=P(("parts", "dp", "mp"), None), check_vma=False
    )
```

```python
import functools

import jax
import jax.numpy as jnp
from jax import lax
from jax.experimental import pallas as pl
from jax.experimental.pallas import tpu as pltpu
from jax.sharding import PartitionSpec as P

NT = (((1,), (1,)), ((), ()))
STEP = 1024
TILE = 256
ROWS = 32
AHEAD = 2


def project(
    inputs,
    gate_pre,
    up_pre,
    hidden_grad,
    out_grad,
    gate_in,
    gate_out,
    up_in,
    up_out,
    down_in,
    down_out,
    out,
    v_inputs,
    v_gate,
    v_up,
    v_back,
    v_out_grad,
    v_in,
    v_gate_out,
    v_up_out,
    v_down_in,
    v_down_out,
    sum_in,
    sums,
    sems,
):
    width = gate_in.shape[0]
    tokens = inputs.shape[0]
    hidden, model = gate_pre.shape[1], inputs.shape[1]
    steps = hidden // STEP
    activations = ((gate_pre, v_gate), (up_pre, v_up), (hidden_grad, v_back))
    hidden_bases = ((gate_out, v_gate_out), (up_out, v_up_out), (down_in, v_down_in))
    model_bases = (
        (gate_in, v_in.at[pl.ds(0, width), :]),
        (up_in, v_in.at[pl.ds(width, width), :]),
        (down_out, v_down_out),
    )
    tokens_wide = ((inputs, v_inputs), (out_grad, v_out_grad))
    first_model = 2
    groups = []
    for step in range(steps):
        pairs = [(pair, step * STEP, STEP) for pair in activations]
        if step == 0:
            pairs += [(pair, 0, hidden // 2) for pair in hidden_bases]
        if step == steps // 2:
            pairs += [(pair, hidden // 2, hidden // 2) for pair in hidden_bases]
        if step == first_model - 1:
            pairs += [(pair, 0, model) for pair in model_bases]
        if step == first_model:
            pairs += [(pair, 0, model // 2) for pair in tokens_wide]
        if step == first_model + model // STEP // 2:
            pairs += [(pair, model // 2, model // 2) for pair in tokens_wide]
        groups.append(pairs)

    def start(step):
        for (source, target), low, length in groups[step]:
            at = pl.ds(low, length)
            pltpu.make_async_copy(source.at[:, at], target.at[:, at], sems.at[step]).start()

    def wait(step):
        count = sum(source.shape[0] * length for (source, _), _, length in groups[step])
        at = pl.ds(0, count // tokens)
        pltpu.make_async_copy(gate_pre.at[:, at], v_gate.at[:, at], sems.at[step]).wait()

    def products(step, left):
        parts = []
        for top in range(0, tokens, ROWS):
            at = (slice(top, top + ROWS), slice(step * STEP + left, step * STEP + left + TILE))
            half = 0.5 * v_gate[at].astype(jnp.float32)
            up = v_up[at].astype(jnp.float32)
            back = v_back[at].astype(jnp.float32)
            tanh = jnp.tanh(half)
            plus = 1.0 + tanh
            silu = half * plus
            slope = plus + silu * (1.0 - tanh)
            values = (back * up * slope, back * silu, silu * up)
            parts.append([value.astype(jnp.bfloat16) for value in values])
        return [jnp.concatenate(column, axis=0) for column in zip(*parts)]

    def add(total, values, base, first):
        value = lax.dot_general(values, base, NT, preferred_element_type=jnp.float32)
        if first:
            total[...] = value
        else:
            total[...] += value

    def hidden_dots(step, left):
        at = slice(step * STEP + left, step * STEP + left + TILE)
        bases = (v_gate_out, v_up_out, v_down_in)
        for which, value in enumerate(products(step, left)):
            add(sums.at[which], value, bases[which][:, at], step == 0 and left == 0)

    def model_dots(left):
        at = slice(left, left + TILE)
        add(sum_in, v_inputs[:, at], v_in[:, at], left == 0)
        add(sums.at[3], v_out_grad[:, at], v_down_out[:, at], left == 0)

    for step in range(AHEAD):
        start(step)
    for step in range(steps):
        if step + AHEAD < steps:
            start(step + AHEAD)
        wait(step)
        for left in range(0, STEP, TILE):
            hidden_dots(step, left)
            model_left = (step - first_model) * STEP + left
            if 0 <= model_left < model:
                model_dots(model_left)
    out[:, : 2 * width] = sum_in[...]
    out[:, 2 * width : 4 * width] = jnp.concatenate([0.5 * sums[0], sums[1]], axis=1)
    out[:, 4 * width :] = jnp.concatenate([sums[2], sums[3]], axis=1)


def projections(*operands):
    inputs, gate_pre = operands[:2]
    width = operands[5].shape[0]
    tokens, model = inputs.shape
    hidden = gate_pre.shape[1]
    assert hidden % STEP == 0 and model % (2 * STEP) == 0 and tokens % ROWS == 0
    assert 2 * STEP + model <= hidden and hidden % 256 == 0 and tokens == 3 * width
    bf16 = jnp.bfloat16
    return pl.pallas_call(
        project,
        out_shape=jax.ShapeDtypeStruct((tokens, 6 * width), jnp.float32),
        in_specs=[pl.BlockSpec(memory_space=pltpu.HBM)] * len(operands),
        out_specs=pl.BlockSpec(memory_space=pltpu.VMEM),
        scratch_shapes=[
            pltpu.VMEM((tokens, model), bf16),
            pltpu.VMEM((tokens, hidden), bf16),
            pltpu.VMEM((tokens, hidden), bf16),
            pltpu.VMEM((tokens, hidden), bf16),
            pltpu.VMEM((tokens, model), bf16),
            pltpu.VMEM((2 * width, model), bf16),
            pltpu.VMEM((width, hidden), bf16),
            pltpu.VMEM((width, hidden), bf16),
            pltpu.VMEM((width, hidden), bf16),
            pltpu.VMEM((width, model), bf16),
            pltpu.VMEM((tokens, 2 * width), jnp.float32),
            pltpu.VMEM((4, tokens, width), jnp.float32),
            pltpu.SemaphoreType.DMA((hidden // STEP,)),
        ],
        compiler_params=pltpu.CompilerParams(vmem_limit_bytes=427 * 2**17),
        cost_estimate=pl.CostEstimate(
            flops=6 * tokens * width * (model + hidden),
            bytes_accessed=2 * (2 * tokens * model + 3 * tokens * hidden),
            transcendentals=tokens * hidden,
        ),
        name="project",
    )(*operands)


def two_terms(value):
    high = value.astype(jnp.bfloat16)
    return high, (value - high.astype(jnp.float32)).astype(jnp.bfloat16)


def outer(chips, own, other, ids, out, summed, products):
    chip, core = lax.axis_index("dp"), lax.axis_index("mp")
    width = own.shape[1] // 6
    half = width // 2
    span = 3 * half // chips
    summed[...] = (own[...] + other[...]).T
    own_label = 2 * chip + core
    tail_label = jnp.where(core == 1, 2 * chip - 1, -1)
    masks = [(ids[...] == label).astype(jnp.float32) for label in (tail_label, own_label)]
    lane = lax.broadcasted_iota(jnp.int32, (half, 2 * width), 1)
    for module, (left, right) in enumerate(((0, 2), (1, 3), (4, 5))):
        factor = summed[left * width : (left + 1) * width, :]
        high, low = two_terms(jnp.concatenate([factor * mask for mask in masks], axis=0))
        top, bottom = two_terms(summed[right * width : (right + 1) * width, :])
        product = None
        for one, two in ((high, top), (high, bottom), (low, top)):
            both = jnp.concatenate([two, two], axis=0)
            term = lax.dot_general(one, both, NT, preferred_element_type=jnp.float32)
            product = term if product is None else product + term
        products[module] = product
        for label in range(2):
            even = products[module, pl.ds(label * width, half, stride=2), :]
            odd = products[module, pl.ds(label * width + 1, half, stride=2), :]
            packed = jnp.where(lane < width, even, odd)
            row = 0
            while row < half:
                chip_to, inside = divmod(module * half + row, span)
                count = min(span - inside, half - row)
                put = slice(label * span + inside, label * span + inside + count)
                out[chip_to, put, :] = packed[row : row + count]
                row += count


def example_blocks(chips, own, other, ids):
    width = own.shape[1] // 6
    block = (3 * width // chips, 2 * width)
    return pl.pallas_call(
        functools.partial(outer, chips),
        out_shape=jax.ShapeDtypeStruct((chips,) + block, jnp.float32),
        in_specs=[pl.BlockSpec(memory_space=pltpu.VMEM)] * 3,
        out_specs=pl.BlockSpec(memory_space=pltpu.VMEM),
        scratch_shapes=[
            pltpu.VMEM(own.shape[::-1], jnp.float32),
            pltpu.VMEM((3, 2 * width, 2 * width), jnp.float32),
        ],
        compiler_params=pltpu.CompilerParams(vmem_limit_bytes=6 * 2**20),
        name="outer",
    )(own, other, ids)


def score(queries, swapped, received, out, rows):
    core = lax.axis_index("mp")
    chips, height, lanes = received.shape
    span = height // 2
    rows[: chips * height, :] = received[...].reshape(chips * height, lanes)
    rows[chips * height :, :] = jnp.zeros((8, lanes), jnp.float32)
    grads = []
    for at in range(span):
        own = rows[pl.ds(span + at, chips, stride=height), :]
        tail = rows[pl.ds(at, chips, stride=height), :]
        tail = jnp.concatenate([tail[1:], jnp.zeros_like(tail[:1])], axis=0)
        grads.append(own + tail)
    terms = jnp.concatenate(two_terms(jnp.concatenate(grads, axis=1)), axis=0)
    coords = queries.shape[1]
    first = core == 0
    mine = jnp.where(first, terms[:, :coords], terms[:, coords:])
    theirs = jnp.where(first, terms[:, coords:], terms[:, :coords])
    scores = lax.dot_general(mine, queries[...], NT, preferred_element_type=jnp.float32)
    scores += lax.dot_general(theirs, swapped[...], NT, preferred_element_type=jnp.float32)
    out[...] = scores[:chips] + scores[chips:]


def partial_scores(queries, swapped, received):
    chips, height, lanes = received.shape
    return pl.pallas_call(
        score,
        out_shape=jax.ShapeDtypeStruct((chips, queries.shape[0]), jnp.float32),
        in_specs=[pl.BlockSpec(memory_space=pltpu.VMEM)] * 3,
        out_specs=pl.BlockSpec(memory_space=pltpu.VMEM),
        scratch_shapes=[pltpu.VMEM((chips * height + 8, lanes), jnp.float32)],
        compiler_params=pltpu.CompilerParams(vmem_limit_bytes=6 * 2**20),
        name="score",
    )(queries, swapped, received)


def body(
    inputs,
    gate_pre,
    up_pre,
    hidden_grad,
    out_grad,
    example_ids,
    gate_in,
    gate_out,
    up_in,
    up_out,
    down_in,
    down_out,
    queries,
):
    chips = lax.axis_size("dp")
    swap = [(0, 1), (1, 0)]
    swapped = lax.ppermute(queries, "mp", swap)
    bases = [base.T for base in (gate_in, gate_out, up_in, up_out, down_in, down_out)]
    own = projections(inputs, gate_pre, up_pre, hidden_grad, out_grad, *bases)
    other = lax.ppermute(own, "mp", swap)
    blocks = example_blocks(chips, own, other, example_ids.reshape(1, -1))
    received = lax.all_to_all(blocks, "dp", split_axis=0, concat_axis=0, tiled=True)
    scores = partial_scores(queries, swapped, received)[:, None]
    pieces = lax.all_to_all(scores, "dp", split_axis=0, concat_axis=0, tiled=True)
    return jnp.sum(pieces, axis=0)


def solution(mesh):
    placed = (
        P(("parts", "dp"), "mp"),
        P(("parts", "dp"), "mp"),
        P(("parts", "dp"), "mp"),
        P(("parts", "dp"), "mp"),
        P(("parts", "dp"), "mp"),
        P(("parts", "dp")),
        P("mp", None),
        P("mp", None),
        P("mp", None),
        P("mp", None),
        P("mp", None),
        P("mp", None),
        P(None, ("dp", "mp")),
    )
    return jax.shard_map(
        body, mesh=mesh, in_specs=placed, out_specs=P(("parts", "dp", "mp"), None), check_vma=False
    )
```

```python
import functools

import jax
import jax.numpy as jnp
from jax import lax
from jax.experimental import pallas as pl
from jax.experimental.pallas import tpu as pltpu
from jax.sharding import PartitionSpec as P

NT = (((1,), (1,)), ((), ()))
STEP = 1024
TILE = 256
ROWS = 16
AHEAD = 3


def project(
    inputs,
    gate_pre,
    up_pre,
    hidden_grad,
    out_grad,
    gate_in,
    gate_out,
    up_in,
    up_out,
    down_in,
    down_out,
    out,
    v_inputs,
    v_gate,
    v_up,
    v_back,
    v_out_grad,
    v_in,
    v_gate_out,
    v_up_out,
    v_down_in,
    v_down_out,
    sum_in,
    sums,
    sems,
):
    width = gate_in.shape[0]
    tokens = inputs.shape[0]
    hidden, model = gate_pre.shape[1], inputs.shape[1]
    edges = [0] + list(range(STEP // 2, hidden, STEP)) + [hidden]
    steps = len(edges) - 1
    activations = ((gate_pre, v_gate), (up_pre, v_up), (hidden_grad, v_back))
    hidden_bases = ((gate_out, v_gate_out), (up_out, v_up_out), (down_in, v_down_in))
    model_bases = (
        (gate_in, v_in.at[pl.ds(0, width), :]),
        (up_in, v_in.at[pl.ds(width, width), :]),
        (down_out, v_down_out),
    )
    tokens_wide = ((inputs, v_inputs), (out_grad, v_out_grad))
    first_model = 3
    second_model = first_model + model // STEP // 2
    groups = []
    for step in range(steps):
        low, high = edges[step], edges[step + 1]
        pairs = [(pair, low, high - low) for pair in activations]
        if step == 0:
            pairs += [(pair, low, high - low) for pair in hidden_bases]
        if step == 1:
            pairs += [(pair, low, hidden // 2 - low) for pair in hidden_bases]
        if low == hidden // 2:
            pairs += [(pair, low, hidden // 2) for pair in hidden_bases]
        if step == first_model - 1:
            pairs += [(pair, 0, model) for pair in model_bases]
        if step == first_model:
            pairs += [(pair, 0, model // 2) for pair in tokens_wide]
        if step == second_model:
            pairs += [(pair, model // 2, model // 2) for pair in tokens_wide]
        groups.append(pairs)

    def start(step):
        for (source, target), low, length in groups[step]:
            at = pl.ds(low, length)
            pltpu.make_async_copy(source.at[:, at], target.at[:, at], sems.at[step]).start()

    def wait(step):
        count = sum(source.shape[0] * length for (source, _), _, length in groups[step])
        at = pl.ds(0, count // tokens)
        pltpu.make_async_copy(gate_pre.at[:, at], v_gate.at[:, at], sems.at[step]).wait()

    def products(left):
        parts = []
        for top in range(0, tokens, ROWS):
            at = (slice(top, top + ROWS), slice(left, left + TILE))
            half = 0.5 * v_gate[at].astype(jnp.float32)
            up = v_up[at].astype(jnp.float32)
            back = v_back[at].astype(jnp.float32)
            tanh = jnp.tanh(half)
            plus = 1.0 + tanh
            silu = half * plus
            slope = plus + silu * (1.0 - tanh)
            values = (back * up * slope, back * silu, silu * up)
            parts.append([value.astype(jnp.bfloat16) for value in values])
        return [jnp.concatenate(column, axis=0) for column in zip(*parts)]

    def add(total, values, base, first):
        value = lax.dot_general(values, base, NT, preferred_element_type=jnp.float32)
        if first:
            total[...] = value
        else:
            total[...] += value

    def hidden_dots(left):
        at = slice(left, left + TILE)
        bases = (v_gate_out, v_up_out, v_down_in)
        for which, value in enumerate(products(left)):
            add(sums.at[which], value, bases[which][:, at], left == 0)

    def model_dots(left):
        at = slice(left, left + TILE)
        add(sum_in, v_inputs[:, at], v_in[:, at], left == 0)
        add(sums.at[3], v_out_grad[:, at], v_down_out[:, at], left == 0)

    for step in range(AHEAD):
        start(step)
    for step in range(steps):
        if step + AHEAD < steps:
            start(step + AHEAD)
        wait(step)
        for left in range(edges[step], edges[step + 1], TILE):
            hidden_dots(left)
            model_left = left - edges[first_model]
            if 0 <= model_left < model:
                model_dots(model_left)
    out[:, : 2 * width] = sum_in[...]
    out[:, 2 * width : 4 * width] = jnp.concatenate([0.5 * sums[0], sums[1]], axis=1)
    out[:, 4 * width :] = jnp.concatenate([sums[2], sums[3]], axis=1)


def projections(*operands):
    inputs, gate_pre = operands[:2]
    width = operands[5].shape[0]
    tokens, model = inputs.shape
    hidden = gate_pre.shape[1]
    assert hidden % (2 * STEP) == STEP and model % (2 * STEP) == 0 and tokens % ROWS == 0
    assert 3 * STEP + model <= hidden and tokens == 3 * width
    bf16 = jnp.bfloat16
    return pl.pallas_call(
        project,
        out_shape=jax.ShapeDtypeStruct((tokens, 6 * width), jnp.float32),
        in_specs=[pl.BlockSpec(memory_space=pltpu.HBM)] * len(operands),
        out_specs=pl.BlockSpec(memory_space=pltpu.VMEM),
        scratch_shapes=[
            pltpu.VMEM((tokens, model), bf16),
            pltpu.VMEM((tokens, hidden), bf16),
            pltpu.VMEM((tokens, hidden), bf16),
            pltpu.VMEM((tokens, hidden), bf16),
            pltpu.VMEM((tokens, model), bf16),
            pltpu.VMEM((2 * width, model), bf16),
            pltpu.VMEM((width, hidden), bf16),
            pltpu.VMEM((width, hidden), bf16),
            pltpu.VMEM((width, hidden), bf16),
            pltpu.VMEM((width, model), bf16),
            pltpu.VMEM((tokens, 2 * width), jnp.float32),
            pltpu.VMEM((4, tokens, width), jnp.float32),
            pltpu.SemaphoreType.DMA((hidden // STEP + 1,)),
        ],
        compiler_params=pltpu.CompilerParams(vmem_limit_bytes=427 * 2**17),
        cost_estimate=pl.CostEstimate(
            flops=6 * tokens * width * (model + hidden),
            bytes_accessed=2 * (2 * tokens * model + 3 * tokens * hidden),
            transcendentals=tokens * hidden,
        ),
        name="project",
    )(*operands)


def two_terms(value):
    high = value.astype(jnp.bfloat16)
    return high, (value - high.astype(jnp.float32)).astype(jnp.bfloat16)


def outer(chips, own, other, ids, out, summed, products):
    chip, core = lax.axis_index("dp"), lax.axis_index("mp")
    width = own.shape[1] // 6
    half = width // 2
    span = 3 * half // chips
    summed[...] = (own[...] + other[...]).T
    own_label = 2 * chip + core
    tail_label = jnp.where(core == 1, 2 * chip - 1, -1)
    masks = [(ids[...] == label).astype(jnp.float32) for label in (tail_label, own_label)]
    lane = lax.broadcasted_iota(jnp.int32, (half, 2 * width), 1)
    for module, (left, right) in enumerate(((0, 2), (1, 3), (4, 5))):
        factor = summed[left * width : (left + 1) * width, :]
        high, low = two_terms(jnp.concatenate([factor * mask for mask in masks], axis=0))
        top, bottom = two_terms(summed[right * width : (right + 1) * width, :])
        product = None
        for one, two in ((high, top), (high, bottom), (low, top)):
            both = jnp.concatenate([two, two], axis=0)
            term = lax.dot_general(one, both, NT, preferred_element_type=jnp.float32)
            product = term if product is None else product + term
        products[module] = product
        for label in range(2):
            even = products[module, pl.ds(label * width, half, stride=2), :]
            odd = products[module, pl.ds(label * width + 1, half, stride=2), :]
            packed = jnp.where(lane < width, even, odd)
            row = 0
            while row < half:
                chip_to, inside = divmod(module * half + row, span)
                count = min(span - inside, half - row)
                put = slice(label * span + inside, label * span + inside + count)
                out[chip_to, put, :] = packed[row : row + count]
                row += count


def example_blocks(chips, own, other, ids):
    width = own.shape[1] // 6
    block = (3 * width // chips, 2 * width)
    return pl.pallas_call(
        functools.partial(outer, chips),
        out_shape=jax.ShapeDtypeStruct((chips,) + block, jnp.float32),
        in_specs=[pl.BlockSpec(memory_space=pltpu.VMEM)] * 3,
        out_specs=pl.BlockSpec(memory_space=pltpu.VMEM),
        scratch_shapes=[
            pltpu.VMEM(own.shape[::-1], jnp.float32),
            pltpu.VMEM((3, 2 * width, 2 * width), jnp.float32),
        ],
        compiler_params=pltpu.CompilerParams(vmem_limit_bytes=6 * 2**20),
        name="outer",
    )(own, other, ids)


def score(queries, swapped, received, out, rows):
    core = lax.axis_index("mp")
    chips, height, lanes = received.shape
    span = height // 2
    rows[: chips * height, :] = received[...].reshape(chips * height, lanes)
    rows[chips * height :, :] = jnp.zeros((8, lanes), jnp.float32)
    grads = []
    for at in range(span):
        own = rows[pl.ds(span + at, chips, stride=height), :]
        tail = rows[pl.ds(at, chips, stride=height), :]
        tail = jnp.concatenate([tail[1:], jnp.zeros_like(tail[:1])], axis=0)
        grads.append(own + tail)
    terms = jnp.concatenate(two_terms(jnp.concatenate(grads, axis=1)), axis=0)
    coords = queries.shape[1]
    first = core == 0
    mine = jnp.where(first, terms[:, :coords], terms[:, coords:])
    theirs = jnp.where(first, terms[:, coords:], terms[:, :coords])
    scores = lax.dot_general(mine, queries[...], NT, preferred_element_type=jnp.float32)
    scores += lax.dot_general(theirs, swapped[...], NT, preferred_element_type=jnp.float32)
    out[...] = scores[:chips] + scores[chips:]


def partial_scores(queries, swapped, received):
    chips, height, lanes = received.shape
    return pl.pallas_call(
        score,
        out_shape=jax.ShapeDtypeStruct((chips, queries.shape[0]), jnp.float32),
        in_specs=[pl.BlockSpec(memory_space=pltpu.VMEM)] * 3,
        out_specs=pl.BlockSpec(memory_space=pltpu.VMEM),
        scratch_shapes=[pltpu.VMEM((chips * height + 8, lanes), jnp.float32)],
        compiler_params=pltpu.CompilerParams(vmem_limit_bytes=6 * 2**20),
        name="score",
    )(queries, swapped, received)


def body(
    inputs,
    gate_pre,
    up_pre,
    hidden_grad,
    out_grad,
    example_ids,
    gate_in,
    gate_out,
    up_in,
    up_out,
    down_in,
    down_out,
    queries,
):
    chips = lax.axis_size("dp")
    swap = [(0, 1), (1, 0)]
    swapped = lax.ppermute(queries, "mp", swap)
    bases = [base.T for base in (gate_in, gate_out, up_in, up_out, down_in, down_out)]
    own = projections(inputs, gate_pre, up_pre, hidden_grad, out_grad, *bases)
    other = lax.ppermute(own, "mp", swap)
    blocks = example_blocks(chips, own, other, example_ids.reshape(1, -1))
    received = lax.all_to_all(blocks, "dp", split_axis=0, concat_axis=0, tiled=True)
    scores = partial_scores(queries, swapped, received)[:, None]
    pieces = lax.all_to_all(scores, "dp", split_axis=0, concat_axis=0, tiled=True)
    return jnp.sum(pieces, axis=0)


def solution(mesh):
    placed = (
        P(("parts", "dp"), "mp"),
        P(("parts", "dp"), "mp"),
        P(("parts", "dp"), "mp"),
        P(("parts", "dp"), "mp"),
        P(("parts", "dp"), "mp"),
        P(("parts", "dp")),
        P("mp", None),
        P("mp", None),
        P("mp", None),
        P("mp", None),
        P("mp", None),
        P("mp", None),
        P(None, ("dp", "mp")),
    )
    return jax.shard_map(
        body, mesh=mesh, in_specs=placed, out_specs=P(("parts", "dp", "mp"), None), check_vma=False
    )
```

```python
import functools

import jax
import jax.numpy as jnp
from jax import lax
from jax.experimental import pallas as pl
from jax.experimental.pallas import tpu as pltpu
from jax.sharding import PartitionSpec as P

NT = (((1,), (1,)), ((), ()))
STEP = 1024
TILE = 256
ROWS = 16
AHEAD = 3


def project(
    inputs,
    gate_pre,
    up_pre,
    hidden_grad,
    out_grad,
    gate_in,
    gate_out,
    up_in,
    up_out,
    down_in,
    down_out,
    out,
    v_inputs,
    v_gate,
    v_up,
    v_back,
    v_out_grad,
    v_in,
    v_gate_out,
    v_up_out,
    v_down_in,
    v_down_out,
    sum_in,
    sums,
    sems,
):
    width = gate_in.shape[0]
    tokens = inputs.shape[0]
    hidden, model = gate_pre.shape[1], inputs.shape[1]
    edges = [0] + list(range(STEP // 2, hidden, STEP)) + [hidden]
    steps = len(edges) - 1
    activations = ((gate_pre, v_gate), (up_pre, v_up), (hidden_grad, v_back))
    hidden_bases = ((gate_out, v_gate_out), (up_out, v_up_out), (down_in, v_down_in))
    model_bases = (
        (gate_in, v_in.at[pl.ds(0, width), :]),
        (up_in, v_in.at[pl.ds(width, width), :]),
        (down_out, v_down_out),
    )
    tokens_wide = ((inputs, v_inputs), (out_grad, v_out_grad))
    first_model = 3
    second_model = first_model + model // STEP // 2
    groups = []
    for step in range(steps):
        low, high = edges[step], edges[step + 1]
        pairs = [(pair, low, high - low) for pair in activations]
        if step == 0:
            pairs += [(pair, low, high - low) for pair in hidden_bases]
        if step == 1:
            pairs += [(pair, low, hidden // 2 - low) for pair in hidden_bases]
        if low == hidden // 2:
            pairs += [(pair, low, hidden // 2) for pair in hidden_bases]
        if step == first_model - 1:
            pairs += [(pair, 0, model) for pair in model_bases]
        if step == first_model:
            pairs += [(pair, 0, model // 2) for pair in tokens_wide]
        if step == second_model:
            pairs += [(pair, model // 2, model // 2) for pair in tokens_wide]
        groups.append(pairs)

    def start(step):
        for (source, target), low, length in groups[step]:
            at = pl.ds(low, length)
            pltpu.make_async_copy(source.at[:, at], target.at[:, at], sems.at[step]).start()

    def wait(step):
        count = sum(source.shape[0] * length for (source, _), _, length in groups[step])
        at = pl.ds(0, count // tokens)
        pltpu.make_async_copy(gate_pre.at[:, at], v_gate.at[:, at], sems.at[step]).wait()

    def products(left):
        parts = []
        for top in range(0, tokens, ROWS):
            at = (slice(top, top + ROWS), slice(left, left + TILE))
            half = 0.5 * v_gate[at].astype(jnp.float32)
            up = v_up[at].astype(jnp.float32)
            back = v_back[at].astype(jnp.float32)
            tanh = jnp.tanh(half)
            plus = 1.0 + tanh
            silu = half * plus
            slope = plus + silu * (1.0 - tanh)
            values = (back * up * slope, back * silu, silu * up)
            parts.append([value.astype(jnp.bfloat16) for value in values])
        return [jnp.concatenate(column, axis=0) for column in zip(*parts)]

    def add(total, values, base, first):
        value = lax.dot_general(values, base, NT, preferred_element_type=jnp.float32)
        if first:
            total[...] = value
        else:
            total[...] += value

    def hidden_dots(left):
        at = slice(left, left + TILE)
        bases = (v_gate_out, v_up_out, v_down_in)
        for which, value in enumerate(products(left)):
            add(sums.at[which], value, bases[which][:, at], left == 0)

    def model_dots(left):
        at = slice(left, left + TILE)
        add(sum_in, v_inputs[:, at], v_in[:, at], left == 0)
        add(sums.at[3], v_out_grad[:, at], v_down_out[:, at], left == 0)

    for step in range(AHEAD):
        start(step)
    for step in range(steps):
        if step + AHEAD < steps:
            start(step + AHEAD)
        wait(step)
        for left in range(edges[step], edges[step + 1], TILE):
            hidden_dots(left)
            model_left = left - edges[first_model]
            if 0 <= model_left < model:
                model_dots(model_left)
    out[:, : 2 * width] = sum_in[...]
    out[:, 2 * width : 4 * width] = jnp.concatenate([0.5 * sums[0], sums[1]], axis=1)
    out[:, 4 * width :] = jnp.concatenate([sums[2], sums[3]], axis=1)


def projections(*operands):
    inputs, gate_pre = operands[:2]
    width = operands[5].shape[0]
    tokens, model = inputs.shape
    hidden = gate_pre.shape[1]
    assert hidden % (2 * STEP) == STEP and model % (2 * STEP) == 0 and tokens % ROWS == 0
    assert 3 * STEP + model <= hidden and tokens == 3 * width
    bf16 = jnp.bfloat16
    return pl.pallas_call(
        project,
        out_shape=jax.ShapeDtypeStruct((tokens, 6 * width), jnp.float32),
        in_specs=[pl.BlockSpec(memory_space=pltpu.HBM)] * len(operands),
        out_specs=pl.BlockSpec(memory_space=pltpu.VMEM),
        scratch_shapes=[
            pltpu.VMEM((tokens, model), bf16),
            pltpu.VMEM((tokens, hidden), bf16),
            pltpu.VMEM((tokens, hidden), bf16),
            pltpu.VMEM((tokens, hidden), bf16),
            pltpu.VMEM((tokens, model), bf16),
            pltpu.VMEM((2 * width, model), bf16),
            pltpu.VMEM((width, hidden), bf16),
            pltpu.VMEM((width, hidden), bf16),
            pltpu.VMEM((width, hidden), bf16),
            pltpu.VMEM((width, model), bf16),
            pltpu.VMEM((tokens, 2 * width), jnp.float32),
            pltpu.VMEM((4, tokens, width), jnp.float32),
            pltpu.SemaphoreType.DMA((hidden // STEP + 1,)),
        ],
        compiler_params=pltpu.CompilerParams(vmem_limit_bytes=427 * 2**17),
        cost_estimate=pl.CostEstimate(
            flops=6 * tokens * width * (model + hidden),
            bytes_accessed=2 * (2 * tokens * model + 3 * tokens * hidden),
            transcendentals=tokens * hidden,
        ),
        name="project",
    )(*operands)


def two_terms(value):
    high = value.astype(jnp.bfloat16)
    return high, (value - high.astype(jnp.float32)).astype(jnp.bfloat16)


def outer(chips, own, other, ids, out, summed, products):
    chip, core = lax.axis_index("dp"), lax.axis_index("mp")
    width = own.shape[1] // 6
    half = width // 2
    span = 3 * half // chips
    summed[...] = (own[...] + other[...]).T
    own_label = 2 * chip + core
    tail_label = jnp.where(core == 1, 2 * chip - 1, -1)
    masks = [(ids[...] == label).astype(jnp.float32) for label in (tail_label, own_label)]
    lane = lax.broadcasted_iota(jnp.int32, (half, 2 * width), 1)
    for module, (left, right) in enumerate(((0, 2), (1, 3), (4, 5))):
        factor = summed[left * width : (left + 1) * width, :]
        high, low = two_terms(jnp.concatenate([factor * mask for mask in masks], axis=0))
        top, bottom = two_terms(summed[right * width : (right + 1) * width, :])
        product = None
        for one, two in ((high, top), (high, bottom), (low, top)):
            both = jnp.concatenate([two, two], axis=0)
            term = lax.dot_general(one, both, NT, preferred_element_type=jnp.float32)
            product = term if product is None else product + term
        products[module] = product
        for label in range(2):
            even = products[module, pl.ds(label * width, half, stride=2), :]
            odd = products[module, pl.ds(label * width + 1, half, stride=2), :]
            packed = jnp.where(lane < width, even, odd)
            row = 0
            while row < half:
                chip_to, inside = divmod(module * half + row, span)
                count = min(span - inside, half - row)
                put = slice(label * span + inside, label * span + inside + count)
                out[(chip_to + chips // 2) % chips, put, :] = packed[row : row + count]
                row += count


def example_blocks(chips, own, other, ids):
    width = own.shape[1] // 6
    block = (3 * width // chips, 2 * width)
    return pl.pallas_call(
        functools.partial(outer, chips),
        out_shape=jax.ShapeDtypeStruct((chips,) + block, jnp.float32),
        in_specs=[pl.BlockSpec(memory_space=pltpu.VMEM)] * 3,
        out_specs=pl.BlockSpec(memory_space=pltpu.VMEM),
        scratch_shapes=[
            pltpu.VMEM(own.shape[::-1], jnp.float32),
            pltpu.VMEM((3, 2 * width, 2 * width), jnp.float32),
        ],
        compiler_params=pltpu.CompilerParams(vmem_limit_bytes=6 * 2**20),
        name="outer",
    )(own, other, ids)


def score(queries, swapped, received, out, rows):
    core = lax.axis_index("mp")
    chips, height, lanes = received.shape
    span = height // 2
    middle = chips // 2
    rows[: middle * height, :] = received[middle:].reshape(middle * height, lanes)
    rows[middle * height : chips * height, :] = received[:middle].reshape(middle * height, lanes)
    rows[chips * height :, :] = jnp.zeros((8, lanes), jnp.float32)
    grads = []
    for at in range(span):
        own = rows[pl.ds(span + at, chips, stride=height), :]
        tail = rows[pl.ds(at, chips, stride=height), :]
        tail = jnp.concatenate([tail[1:], jnp.zeros_like(tail[:1])], axis=0)
        grads.append(own + tail)
    terms = jnp.concatenate(two_terms(jnp.concatenate(grads, axis=1)), axis=0)
    coords = queries.shape[1]
    first = core == 0
    mine = jnp.where(first, terms[:, :coords], terms[:, coords:])
    theirs = jnp.where(first, terms[:, coords:], terms[:, :coords])
    scores = lax.dot_general(mine, queries[...], NT, preferred_element_type=jnp.float32)
    scores += lax.dot_general(theirs, swapped[...], NT, preferred_element_type=jnp.float32)
    total = scores[:chips] + scores[chips:]
    out[...] = jnp.concatenate([total[middle:], total[:middle]], axis=0)


def partial_scores(queries, swapped, received):
    chips, height, lanes = received.shape
    return pl.pallas_call(
        score,
        out_shape=jax.ShapeDtypeStruct((chips, queries.shape[0]), jnp.float32),
        in_specs=[pl.BlockSpec(memory_space=pltpu.VMEM)] * 3,
        out_specs=pl.BlockSpec(memory_space=pltpu.VMEM),
        scratch_shapes=[pltpu.VMEM((chips * height + 8, lanes), jnp.float32)],
        compiler_params=pltpu.CompilerParams(vmem_limit_bytes=6 * 2**20),
        name="score",
    )(queries, swapped, received)


def to_all(blocks):
    chips = blocks.shape[0]
    order = [(i + chips // 2) % chips for i in range(chips)]
    return lax.all_to_all(
        blocks, "dp", split_axis=0, concat_axis=0, axis_index_groups=[order], tiled=True
    )


def body(
    inputs,
    gate_pre,
    up_pre,
    hidden_grad,
    out_grad,
    example_ids,
    gate_in,
    gate_out,
    up_in,
    up_out,
    down_in,
    down_out,
    queries,
):
    chips = lax.axis_size("dp")
    swap = [(0, 1), (1, 0)]
    swapped = lax.ppermute(queries, "mp", swap)
    bases = [base.T for base in (gate_in, gate_out, up_in, up_out, down_in, down_out)]
    own = projections(inputs, gate_pre, up_pre, hidden_grad, out_grad, *bases)
    other = lax.ppermute(own, "mp", swap)
    blocks = example_blocks(chips, own, other, example_ids.reshape(1, -1))
    received = to_all(blocks)
    scores = partial_scores(queries, swapped, received)[:, None]
    pieces = to_all(scores)
    return jnp.sum(pieces, axis=0)


def solution(mesh):
    placed = (
        P(("parts", "dp"), "mp"),
        P(("parts", "dp"), "mp"),
        P(("parts", "dp"), "mp"),
        P(("parts", "dp"), "mp"),
        P(("parts", "dp"), "mp"),
        P(("parts", "dp")),
        P("mp", None),
        P("mp", None),
        P("mp", None),
        P("mp", None),
        P("mp", None),
        P("mp", None),
        P(None, ("dp", "mp")),
    )
    return jax.shard_map(
        body, mesh=mesh, in_specs=placed, out_specs=P(("parts", "dp", "mp"), None), check_vma=False
    )
```

```python
import functools

import jax
import jax.numpy as jnp
from jax import lax
from jax.experimental import pallas as pl
from jax.experimental.pallas import tpu as pltpu
from jax.sharding import PartitionSpec as P

NT = (((1,), (1,)), ((), ()))
STEP = 1024
TILE = 256
ROWS = 16
AHEAD = 3


def project(
    inputs,
    gate_pre,
    up_pre,
    hidden_grad,
    out_grad,
    gate_in,
    gate_out,
    up_in,
    up_out,
    down_in,
    down_out,
    out,
    v_inputs,
    v_gate,
    v_up,
    v_back,
    v_out_grad,
    v_in,
    v_gate_out,
    v_up_out,
    v_down_in,
    v_down_out,
    sum_in,
    sums,
    sems,
):
    width = gate_in.shape[0]
    tokens = inputs.shape[0]
    hidden, model = gate_pre.shape[1], inputs.shape[1]
    edges = [0] + list(range(STEP // 2, hidden, STEP)) + [hidden]
    steps = len(edges) - 1
    activations = ((gate_pre, v_gate), (up_pre, v_up), (hidden_grad, v_back))
    hidden_bases = ((gate_out, v_gate_out), (up_out, v_up_out), (down_in, v_down_in))
    model_bases = (
        (gate_in, v_in.at[pl.ds(0, width), :]),
        (up_in, v_in.at[pl.ds(width, width), :]),
        (down_out, v_down_out),
    )
    tokens_wide = ((inputs, v_inputs), (out_grad, v_out_grad))
    first_model = 3
    second_model = first_model + model // STEP // 2
    groups = []
    for step in range(steps):
        low, high = edges[step], edges[step + 1]
        pairs = [(pair, low, high - low) for pair in activations]
        if step == 0:
            pairs += [(pair, low, high - low) for pair in hidden_bases]
        if step == 1:
            pairs += [(pair, low, hidden // 2 - low) for pair in hidden_bases]
        if low == hidden // 2:
            pairs += [(pair, low, hidden // 2) for pair in hidden_bases]
        if step == first_model - 1:
            pairs += [(pair, 0, model) for pair in model_bases]
        if step == first_model:
            pairs += [(pair, 0, model // 2) for pair in tokens_wide]
        if step == second_model:
            pairs += [(pair, model // 2, model // 2) for pair in tokens_wide]
        groups.append(pairs)

    def start(step):
        for (source, target), low, length in groups[step]:
            at = pl.ds(low, length)
            pltpu.make_async_copy(source.at[:, at], target.at[:, at], sems.at[step]).start()

    def wait(step):
        count = sum(source.shape[0] * length for (source, _), _, length in groups[step])
        at = pl.ds(0, count // tokens)
        pltpu.make_async_copy(gate_pre.at[:, at], v_gate.at[:, at], sems.at[step]).wait()

    def products(left):
        parts = []
        for top in range(0, tokens, ROWS):
            at = (slice(top, top + ROWS), slice(left, left + TILE))
            half = 0.5 * v_gate[at].astype(jnp.float32)
            up = v_up[at].astype(jnp.float32)
            back = v_back[at].astype(jnp.float32)
            tanh = jnp.tanh(half)
            plus = 1.0 + tanh
            silu = half * plus
            slope = plus + silu * (1.0 - tanh)
            values = (back * up * slope, back * silu, silu * up)
            parts.append([value.astype(jnp.bfloat16) for value in values])
        return [jnp.concatenate(column, axis=0) for column in zip(*parts)]

    def add(total, values, base, first):
        value = lax.dot_general(values, base, NT, preferred_element_type=jnp.float32)
        if first:
            total[...] = value
        else:
            total[...] += value

    def hidden_dots(left):
        at = slice(left, left + TILE)
        bases = (v_gate_out, v_up_out, v_down_in)
        for which, value in enumerate(products(left)):
            add(sums.at[which], value, bases[which][:, at], left == 0)

    def model_dots(left):
        at = slice(left, left + TILE)
        add(sum_in, v_inputs[:, at], v_in[:, at], left == 0)
        add(sums.at[3], v_out_grad[:, at], v_down_out[:, at], left == 0)

    for step in range(AHEAD):
        start(step)
    for step in range(steps):
        if step + AHEAD < steps:
            start(step + AHEAD)
        wait(step)
        for left in range(edges[step], edges[step + 1], TILE):
            hidden_dots(left)
            model_left = left - edges[first_model]
            if 0 <= model_left < model:
                model_dots(model_left)
    out[:, : 2 * width] = sum_in[...]
    out[:, 2 * width : 4 * width] = jnp.concatenate([0.5 * sums[0], sums[1]], axis=1)
    out[:, 4 * width :] = jnp.concatenate([sums[2], sums[3]], axis=1)


def projections(*operands):
    inputs, gate_pre = operands[:2]
    width = operands[5].shape[0]
    tokens, model = inputs.shape
    hidden = gate_pre.shape[1]
    assert hidden % (2 * STEP) == STEP and model % (2 * STEP) == 0 and tokens % ROWS == 0
    assert 3 * STEP + model <= hidden and tokens == 3 * width
    bf16 = jnp.bfloat16
    return pl.pallas_call(
        project,
        out_shape=jax.ShapeDtypeStruct((tokens, 6 * width), jnp.float32),
        in_specs=[pl.BlockSpec(memory_space=pltpu.HBM)] * len(operands),
        out_specs=pl.BlockSpec(memory_space=pltpu.VMEM),
        scratch_shapes=[
            pltpu.VMEM((tokens, model), bf16),
            pltpu.VMEM((tokens, hidden), bf16),
            pltpu.VMEM((tokens, hidden), bf16),
            pltpu.VMEM((tokens, hidden), bf16),
            pltpu.VMEM((tokens, model), bf16),
            pltpu.VMEM((2 * width, model), bf16),
            pltpu.VMEM((width, hidden), bf16),
            pltpu.VMEM((width, hidden), bf16),
            pltpu.VMEM((width, hidden), bf16),
            pltpu.VMEM((width, model), bf16),
            pltpu.VMEM((tokens, 2 * width), jnp.float32),
            pltpu.VMEM((4, tokens, width), jnp.float32),
            pltpu.SemaphoreType.DMA((hidden // STEP + 1,)),
        ],
        compiler_params=pltpu.CompilerParams(vmem_limit_bytes=427 * 2**17),
        cost_estimate=pl.CostEstimate(
            flops=6 * tokens * width * (model + hidden),
            bytes_accessed=2 * (2 * tokens * model + 3 * tokens * hidden),
            transcendentals=tokens * hidden,
        ),
        name="project",
    )(*operands)


def first_chip(chips):
    return chips // 2 + 1


def two_terms(value):
    high = value.astype(jnp.bfloat16)
    return high, (value - high.astype(jnp.float32)).astype(jnp.bfloat16)


def outer(chips, own, other, ids, out, summed, products):
    chip, core = lax.axis_index("dp"), lax.axis_index("mp")
    width = own.shape[1] // 6
    half = width // 2
    span = 3 * half // chips
    summed[...] = (own[...] + other[...]).T
    own_label = 2 * chip + core
    tail_label = jnp.where(core == 1, 2 * chip - 1, -1)
    masks = [(ids[...] == label).astype(jnp.float32) for label in (tail_label, own_label)]
    lane = lax.broadcasted_iota(jnp.int32, (half, 2 * width), 1)
    for module, (left, right) in enumerate(((0, 2), (1, 3), (4, 5))):
        factor = summed[left * width : (left + 1) * width, :]
        high, low = two_terms(jnp.concatenate([factor * mask for mask in masks], axis=0))
        top, bottom = two_terms(summed[right * width : (right + 1) * width, :])
        product = None
        for one, two in ((high, top), (high, bottom), (low, top)):
            both = jnp.concatenate([two, two], axis=0)
            term = lax.dot_general(one, both, NT, preferred_element_type=jnp.float32)
            product = term if product is None else product + term
        products[module] = product
        for label in range(2):
            even = products[module, pl.ds(label * width, half, stride=2), :]
            odd = products[module, pl.ds(label * width + 1, half, stride=2), :]
            packed = jnp.where(lane < width, even, odd)
            row = 0
            while row < half:
                chip_to, inside = divmod(module * half + row, span)
                count = min(span - inside, half - row)
                put = slice(label * span + inside, label * span + inside + count)
                out[(chip_to - first_chip(chips)) % chips, put, :] = packed[row : row + count]
                row += count


def example_blocks(chips, own, other, ids):
    width = own.shape[1] // 6
    block = (3 * width // chips, 2 * width)
    return pl.pallas_call(
        functools.partial(outer, chips),
        out_shape=jax.ShapeDtypeStruct((chips,) + block, jnp.float32),
        in_specs=[pl.BlockSpec(memory_space=pltpu.VMEM)] * 3,
        out_specs=pl.BlockSpec(memory_space=pltpu.VMEM),
        scratch_shapes=[
            pltpu.VMEM(own.shape[::-1], jnp.float32),
            pltpu.VMEM((3, 2 * width, 2 * width), jnp.float32),
        ],
        compiler_params=pltpu.CompilerParams(vmem_limit_bytes=6 * 2**20),
        name="outer",
    )(own, other, ids)


def score(queries, swapped, received, out, rows):
    core = lax.axis_index("mp")
    chips, height, lanes = received.shape
    span = height // 2
    first = first_chip(chips)
    rows[: first * height, :] = received[chips - first :].reshape(first * height, lanes)
    rows[first * height : chips * height, :] = received[: chips - first].reshape((chips - first) * height, lanes)
    rows[chips * height :, :] = jnp.zeros((8, lanes), jnp.float32)
    grads = []
    for at in range(span):
        own = rows[pl.ds(span + at, chips, stride=height), :]
        tail = rows[pl.ds(at, chips, stride=height), :]
        tail = jnp.concatenate([tail[1:], jnp.zeros_like(tail[:1])], axis=0)
        grads.append(own + tail)
    terms = jnp.concatenate(two_terms(jnp.concatenate(grads, axis=1)), axis=0)
    coords = queries.shape[1]
    even = core == 0
    mine = jnp.where(even, terms[:, :coords], terms[:, coords:])
    theirs = jnp.where(even, terms[:, coords:], terms[:, :coords])
    scores = lax.dot_general(mine, queries[...], NT, preferred_element_type=jnp.float32)
    scores += lax.dot_general(theirs, swapped[...], NT, preferred_element_type=jnp.float32)
    total = scores[:chips] + scores[chips:]
    out[...] = jnp.concatenate([total[first:], total[:first]], axis=0)


def partial_scores(queries, swapped, received):
    chips, height, lanes = received.shape
    return pl.pallas_call(
        score,
        out_shape=jax.ShapeDtypeStruct((chips, queries.shape[0]), jnp.float32),
        in_specs=[pl.BlockSpec(memory_space=pltpu.VMEM)] * 3,
        out_specs=pl.BlockSpec(memory_space=pltpu.VMEM),
        scratch_shapes=[pltpu.VMEM((chips * height + 8, lanes), jnp.float32)],
        compiler_params=pltpu.CompilerParams(vmem_limit_bytes=6 * 2**20),
        name="score",
    )(queries, swapped, received)


def to_all(blocks):
    chips = blocks.shape[0]
    order = [(i + first_chip(chips)) % chips for i in range(chips)]
    return lax.all_to_all(
        blocks, "dp", split_axis=0, concat_axis=0, axis_index_groups=[order], tiled=True
    )


def body(
    inputs,
    gate_pre,
    up_pre,
    hidden_grad,
    out_grad,
    example_ids,
    gate_in,
    gate_out,
    up_in,
    up_out,
    down_in,
    down_out,
    queries,
):
    chips = lax.axis_size("dp")
    swap = [(0, 1), (1, 0)]
    swapped = lax.ppermute(queries, "mp", swap)
    bases = [base.T for base in (gate_in, gate_out, up_in, up_out, down_in, down_out)]
    own = projections(inputs, gate_pre, up_pre, hidden_grad, out_grad, *bases)
    other = lax.ppermute(own, "mp", swap)
    blocks = example_blocks(chips, own, other, example_ids.reshape(1, -1))
    received = to_all(blocks)
    scores = partial_scores(queries, swapped, received)[:, None]
    pieces = to_all(scores)
    return jnp.sum(pieces, axis=0)


def solution(mesh):
    placed = (
        P(("parts", "dp"), "mp"),
        P(("parts", "dp"), "mp"),
        P(("parts", "dp"), "mp"),
        P(("parts", "dp"), "mp"),
        P(("parts", "dp"), "mp"),
        P(("parts", "dp")),
        P("mp", None),
        P("mp", None),
        P("mp", None),
        P("mp", None),
        P("mp", None),
        P("mp", None),
        P(None, ("dp", "mp")),
    )
    return jax.shard_map(
        body, mesh=mesh, in_specs=placed, out_specs=P(("parts", "dp", "mp"), None), check_vma=False
    )
```

```python
import functools

import jax
import jax.numpy as jnp
from jax import lax
from jax.experimental import pallas as pl
from jax.experimental.pallas import tpu as pltpu
from jax.sharding import PartitionSpec as P

NT = (((1,), (1,)), ((), ()))
STEP = 1024
TILE = 256
ROWS = 16
AHEAD = 3


def project(
    inputs,
    gate_pre,
    up_pre,
    hidden_grad,
    out_grad,
    gate_in,
    gate_out,
    up_in,
    up_out,
    down_in,
    down_out,
    out,
    v_inputs,
    v_gate,
    v_up,
    v_back,
    v_out_grad,
    v_in,
    v_gate_out,
    v_up_out,
    v_down_in,
    v_down_out,
    sum_in,
    sums,
    sems,
):
    width = gate_in.shape[0]
    tokens = inputs.shape[0]
    hidden, model = gate_pre.shape[1], inputs.shape[1]
    edges = [0] + list(range(STEP // 2, hidden, STEP)) + [hidden]
    steps = len(edges) - 1
    activations = ((gate_pre, v_gate), (up_pre, v_up), (hidden_grad, v_back))
    hidden_bases = ((gate_out, v_gate_out), (up_out, v_up_out), (down_in, v_down_in))
    model_bases = (
        (gate_in, v_in.at[pl.ds(0, width), :]),
        (up_in, v_in.at[pl.ds(width, width), :]),
        (down_out, v_down_out),
    )
    tokens_wide = ((inputs, v_inputs), (out_grad, v_out_grad))
    first_model = 3
    second_model = first_model + model // STEP // 2
    groups = []
    for step in range(steps):
        low, high = edges[step], edges[step + 1]
        pairs = [(pair, low, high - low) for pair in activations]
        if step == 0:
            pairs += [(pair, low, high - low) for pair in hidden_bases]
        if step == 1:
            pairs += [(pair, low, hidden // 2 - low) for pair in hidden_bases]
        if low == hidden // 2:
            pairs += [(pair, low, hidden // 2) for pair in hidden_bases]
        if step == first_model - 1:
            pairs += [(pair, 0, model) for pair in model_bases]
        if step == first_model:
            pairs += [(pair, 0, model // 2) for pair in tokens_wide]
        if step == second_model:
            pairs += [(pair, model // 2, model // 2) for pair in tokens_wide]
        groups.append(pairs)

    def start(step):
        for (source, target), low, length in groups[step]:
            at = pl.ds(low, length)
            pltpu.make_async_copy(source.at[:, at], target.at[:, at], sems.at[step]).start()

    def wait(step):
        count = sum(source.shape[0] * length for (source, _), _, length in groups[step])
        at = pl.ds(0, count // tokens)
        pltpu.make_async_copy(gate_pre.at[:, at], v_gate.at[:, at], sems.at[step]).wait()

    def products(left):
        parts = []
        for top in range(0, tokens, ROWS):
            at = (slice(top, top + ROWS), slice(left, left + TILE))
            half = 0.5 * v_gate[at].astype(jnp.float32)
            up = v_up[at].astype(jnp.float32)
            back = v_back[at].astype(jnp.float32)
            tanh = jnp.tanh(half)
            plus = 1.0 + tanh
            silu = half * plus
            slope = plus + silu * (1.0 - tanh)
            values = (back * up * slope, back * silu, silu * up)
            parts.append([value.astype(jnp.bfloat16) for value in values])
        return [jnp.concatenate(column, axis=0) for column in zip(*parts)]

    def add(total, values, base, first):
        value = lax.dot_general(values, base, NT, preferred_element_type=jnp.float32)
        if first:
            total[...] = value
        else:
            total[...] += value

    def hidden_dots(left):
        at = slice(left, left + TILE)
        bases = (v_gate_out, v_up_out, v_down_in)
        for which, value in enumerate(products(left)):
            add(sums.at[which], value, bases[which][:, at], left == 0)

    def model_dots(left):
        at = slice(left, left + TILE)
        add(sum_in, v_inputs[:, at], v_in[:, at], left == 0)
        add(sums.at[3], v_out_grad[:, at], v_down_out[:, at], left == 0)

    for step in range(AHEAD):
        start(step)
    for step in range(steps):
        if step + AHEAD < steps:
            start(step + AHEAD)
        wait(step)
        for left in range(edges[step], edges[step + 1], TILE):
            hidden_dots(left)
            model_left = left - edges[first_model]
            if 0 <= model_left < model:
                model_dots(model_left)
    out[:, : 2 * width] = sum_in[...]
    out[:, 2 * width : 4 * width] = jnp.concatenate([0.5 * sums[0], sums[1]], axis=1)
    out[:, 4 * width :] = jnp.concatenate([sums[2], sums[3]], axis=1)


def projections(*operands):
    inputs, gate_pre = operands[:2]
    width = operands[5].shape[0]
    tokens, model = inputs.shape
    hidden = gate_pre.shape[1]
    assert hidden % (2 * STEP) == STEP and model % (2 * STEP) == 0 and tokens % ROWS == 0
    assert 3 * STEP + model <= hidden and tokens == 3 * width
    bf16 = jnp.bfloat16
    return pl.pallas_call(
        project,
        out_shape=jax.ShapeDtypeStruct((tokens, 6 * width), jnp.float32),
        in_specs=[pl.BlockSpec(memory_space=pltpu.HBM)] * len(operands),
        out_specs=pl.BlockSpec(memory_space=pltpu.VMEM),
        scratch_shapes=[
            pltpu.VMEM((tokens, model), bf16),
            pltpu.VMEM((tokens, hidden), bf16),
            pltpu.VMEM((tokens, hidden), bf16),
            pltpu.VMEM((tokens, hidden), bf16),
            pltpu.VMEM((tokens, model), bf16),
            pltpu.VMEM((2 * width, model), bf16),
            pltpu.VMEM((width, hidden), bf16),
            pltpu.VMEM((width, hidden), bf16),
            pltpu.VMEM((width, hidden), bf16),
            pltpu.VMEM((width, model), bf16),
            pltpu.VMEM((tokens, 2 * width), jnp.float32),
            pltpu.VMEM((4, tokens, width), jnp.float32),
            pltpu.SemaphoreType.DMA((hidden // STEP + 1,)),
        ],
        compiler_params=pltpu.CompilerParams(vmem_limit_bytes=427 * 2**17),
        cost_estimate=pl.CostEstimate(
            flops=6 * tokens * width * (model + hidden),
            bytes_accessed=2 * (2 * tokens * model + 3 * tokens * hidden),
            transcendentals=tokens * hidden,
        ),
        name="project",
    )(*operands)


def first_chip(chips):
    return chips // 2 + 1


def first_device(chips):
    return 2 * first_chip(chips) + 1


def two_terms(value):
    high = value.astype(jnp.bfloat16)
    return high, (value - high.astype(jnp.float32)).astype(jnp.bfloat16)


def outer(chips, own, other, ids, out, summed, products):
    chip, core = lax.axis_index("dp"), lax.axis_index("mp")
    width = own.shape[1] // 6
    half = width // 2
    span = 3 * half // chips
    summed[...] = (own[...] + other[...]).T
    own_label = 2 * chip + core
    tail_label = jnp.where(core == 1, 2 * chip - 1, -1)
    masks = [(ids[...] == label).astype(jnp.float32) for label in (tail_label, own_label)]
    lane = lax.broadcasted_iota(jnp.int32, (half, 2 * width), 1)
    for module, (left, right) in enumerate(((0, 2), (1, 3), (4, 5))):
        factor = summed[left * width : (left + 1) * width, :]
        high, low = two_terms(jnp.concatenate([factor * mask for mask in masks], axis=0))
        top, bottom = two_terms(summed[right * width : (right + 1) * width, :])
        product = None
        for one, two in ((high, top), (high, bottom), (low, top)):
            both = jnp.concatenate([two, two], axis=0)
            term = lax.dot_general(one, both, NT, preferred_element_type=jnp.float32)
            product = term if product is None else product + term
        products[module] = product
        for label in range(2):
            even = products[module, pl.ds(label * width, half, stride=2), :]
            odd = products[module, pl.ds(label * width + 1, half, stride=2), :]
            packed = jnp.where(lane < width, even, odd)
            row = 0
            while row < half:
                chip_to, inside = divmod(module * half + row, span)
                count = min(span - inside, half - row)
                put = slice(label * span + inside, label * span + inside + count)
                out[(chip_to - first_chip(chips)) % chips, put, :] = packed[row : row + count]
                row += count


def example_blocks(chips, own, other, ids):
    width = own.shape[1] // 6
    block = (3 * width // chips, 2 * width)
    return pl.pallas_call(
        functools.partial(outer, chips),
        out_shape=jax.ShapeDtypeStruct((chips,) + block, jnp.float32),
        in_specs=[pl.BlockSpec(memory_space=pltpu.VMEM)] * 3,
        out_specs=pl.BlockSpec(memory_space=pltpu.VMEM),
        scratch_shapes=[
            pltpu.VMEM(own.shape[::-1], jnp.float32),
            pltpu.VMEM((3, 2 * width, 2 * width), jnp.float32),
        ],
        compiler_params=pltpu.CompilerParams(vmem_limit_bytes=6 * 2**20),
        name="outer",
    )(own, other, ids)


def score(queries, swapped, received, out, rows):
    core = lax.axis_index("mp")
    chips, height, lanes = received.shape
    span = height // 2
    first = first_chip(chips)
    rows[: first * height, :] = received[chips - first :].reshape(first * height, lanes)
    rows[first * height : chips * height, :] = received[: chips - first].reshape((chips - first) * height, lanes)
    rows[chips * height :, :] = jnp.zeros((8, lanes), jnp.float32)
    grads = []
    for at in range(span):
        own = rows[pl.ds(span + at, chips, stride=height), :]
        tail = rows[pl.ds(at, chips, stride=height), :]
        tail = jnp.concatenate([tail[1:], jnp.zeros_like(tail[:1])], axis=0)
        grads.append(own + tail)
    terms = jnp.concatenate(two_terms(jnp.concatenate(grads, axis=1)), axis=0)
    coords = queries.shape[1]
    even = core == 0
    mine = jnp.where(even, terms[:, :coords], terms[:, coords:])
    theirs = jnp.where(even, terms[:, coords:], terms[:, :coords])
    scores = lax.dot_general(mine, queries[...], NT, preferred_element_type=jnp.float32)
    scores += lax.dot_general(theirs, swapped[...], NT, preferred_element_type=jnp.float32)
    total = scores[:chips] + scores[chips:]
    for device in range(2 * chips):
        place = (device - first_device(chips)) % (2 * chips)
        row = total[device // 2 : device // 2 + 1]
        out[place : place + 1, :] = jnp.where(core == device % 2, row, 0.0)


def partial_scores(queries, swapped, received):
    chips, height, lanes = received.shape
    return pl.pallas_call(
        score,
        out_shape=jax.ShapeDtypeStruct((2 * chips, queries.shape[0]), jnp.float32),
        in_specs=[pl.BlockSpec(memory_space=pltpu.VMEM)] * 3,
        out_specs=pl.BlockSpec(memory_space=pltpu.VMEM),
        scratch_shapes=[pltpu.VMEM((chips * height + 8, lanes), jnp.float32)],
        compiler_params=pltpu.CompilerParams(vmem_limit_bytes=6 * 2**20),
        name="score",
    )(queries, swapped, received)


def to_all(blocks, axes, first):
    count = blocks.shape[0]
    order = [(i + first) % count for i in range(count)]
    return lax.all_to_all(
        blocks, axes, split_axis=0, concat_axis=0, axis_index_groups=[order], tiled=True
    )


def body(
    inputs,
    gate_pre,
    up_pre,
    hidden_grad,
    out_grad,
    example_ids,
    gate_in,
    gate_out,
    up_in,
    up_out,
    down_in,
    down_out,
    queries,
):
    chips = lax.axis_size("dp")
    swap = [(0, 1), (1, 0)]
    swapped = lax.ppermute(queries, "mp", swap)
    bases = [base.T for base in (gate_in, gate_out, up_in, up_out, down_in, down_out)]
    own = projections(inputs, gate_pre, up_pre, hidden_grad, out_grad, *bases)
    other = lax.ppermute(own, "mp", swap)
    blocks = example_blocks(chips, own, other, example_ids.reshape(1, -1))
    received = to_all(blocks, "dp", first_chip(chips))
    scores = partial_scores(queries, swapped, received)[:, None]
    pieces = to_all(scores, ("dp", "mp"), first_device(chips))
    return jnp.sum(pieces, axis=0)


def solution(mesh):
    placed = (
        P(("parts", "dp"), "mp"),
        P(("parts", "dp"), "mp"),
        P(("parts", "dp"), "mp"),
        P(("parts", "dp"), "mp"),
        P(("parts", "dp"), "mp"),
        P(("parts", "dp")),
        P("mp", None),
        P("mp", None),
        P("mp", None),
        P("mp", None),
        P("mp", None),
        P("mp", None),
        P(None, ("dp", "mp")),
    )
    return jax.shard_map(
        body, mesh=mesh, in_specs=placed, out_specs=P(("parts", "dp", "mp"), None), check_vma=False
    )
```

```python
import functools

import jax
import jax.numpy as jnp
from jax import lax
from jax.experimental import pallas as pl
from jax.experimental.pallas import tpu as pltpu
from jax.sharding import PartitionSpec as P

NT = (((1,), (1,)), ((), ()))
STEP = 1024
TILE = 256
ROWS = 16
AHEAD = 8


def project(
    inputs,
    gate_pre,
    up_pre,
    hidden_grad,
    out_grad,
    gate_in,
    gate_out,
    up_in,
    up_out,
    down_in,
    down_out,
    out,
    v_inputs,
    v_gate,
    v_up,
    v_back,
    v_out_grad,
    v_in,
    v_gate_out,
    v_up_out,
    v_down_in,
    v_down_out,
    sum_in,
    sums,
    sems,
):
    width = gate_in.shape[0]
    tokens = inputs.shape[0]
    hidden, model = gate_pre.shape[1], inputs.shape[1]
    edges = [0] + list(range(STEP // 2, hidden, STEP)) + [hidden]
    steps = len(edges) - 1
    activations = ((gate_pre, v_gate), (up_pre, v_up), (hidden_grad, v_back))
    hidden_bases = ((gate_out, v_gate_out), (up_out, v_up_out), (down_in, v_down_in))
    model_bases = (
        (gate_in, v_in.at[pl.ds(0, width), :]),
        (up_in, v_in.at[pl.ds(width, width), :]),
        (down_out, v_down_out),
    )
    tokens_wide = ((inputs, v_inputs), (out_grad, v_out_grad))
    first_model = 3
    second_model = first_model + model // STEP // 2
    groups = []
    for step in range(steps):
        low, high = edges[step], edges[step + 1]
        pairs = [(pair, low, high - low) for pair in activations]
        if step == 0:
            pairs += [(pair, low, high - low) for pair in hidden_bases]
        if step == 1:
            pairs += [(pair, low, hidden // 2 - low) for pair in hidden_bases]
        if low == hidden // 2:
            pairs += [(pair, low, hidden // 2) for pair in hidden_bases]
        if step == first_model - 1:
            pairs += [(pair, 0, model) for pair in model_bases]
        if step == first_model:
            pairs += [(pair, 0, model // 2) for pair in tokens_wide]
        if step == second_model:
            pairs += [(pair, model // 2, model // 2) for pair in tokens_wide]
        groups.append(pairs)

    def start(step):
        for (source, target), low, length in groups[step]:
            at = pl.ds(low, length)
            pltpu.make_async_copy(source.at[:, at], target.at[:, at], sems.at[step]).start()

    def wait(step):
        count = sum(source.shape[0] * length for (source, _), _, length in groups[step])
        at = pl.ds(0, count // tokens)
        pltpu.make_async_copy(gate_pre.at[:, at], v_gate.at[:, at], sems.at[step]).wait()

    def products(left):
        parts = []
        for top in range(0, tokens, ROWS):
            at = (slice(top, top + ROWS), slice(left, left + TILE))
            half = 0.5 * v_gate[at].astype(jnp.float32)
            up = v_up[at].astype(jnp.float32)
            back = v_back[at].astype(jnp.float32)
            tanh = jnp.tanh(half)
            plus = 1.0 + tanh
            silu = half * plus
            slope = plus + silu * (1.0 - tanh)
            values = (back * up * slope, back * silu, silu * up)
            parts.append([value.astype(jnp.bfloat16) for value in values])
        return [jnp.concatenate(column, axis=0) for column in zip(*parts)]

    def add(total, values, base, first):
        value = lax.dot_general(values, base, NT, preferred_element_type=jnp.float32)
        if first:
            total[...] = value
        else:
            total[...] += value

    def hidden_dots(left):
        at = slice(left, left + TILE)
        bases = (v_gate_out, v_up_out, v_down_in)
        for which, value in enumerate(products(left)):
            add(sums.at[which], value, bases[which][:, at], left == 0)

    def model_dots(left):
        at = slice(left, left + TILE)
        add(sum_in, v_inputs[:, at], v_in[:, at], left == 0)
        add(sums.at[3], v_out_grad[:, at], v_down_out[:, at], left == 0)

    for step in range(AHEAD):
        start(step)
    for step in range(steps):
        if step + AHEAD < steps:
            start(step + AHEAD)
        wait(step)
        for left in range(edges[step], edges[step + 1], TILE):
            hidden_dots(left)
            model_left = left - edges[first_model]
            if 0 <= model_left < model:
                model_dots(model_left)
    out[:, : 2 * width] = sum_in[...]
    out[:, 2 * width : 4 * width] = jnp.concatenate([0.5 * sums[0], sums[1]], axis=1)
    out[:, 4 * width :] = jnp.concatenate([sums[2], sums[3]], axis=1)


def projections(*operands):
    inputs, gate_pre = operands[:2]
    width = operands[5].shape[0]
    tokens, model = inputs.shape
    hidden = gate_pre.shape[1]
    assert hidden % (2 * STEP) == STEP and model % (2 * STEP) == 0 and tokens % ROWS == 0
    assert 3 * STEP + model <= hidden and tokens == 3 * width
    bf16 = jnp.bfloat16
    return pl.pallas_call(
        project,
        out_shape=jax.ShapeDtypeStruct((tokens, 6 * width), jnp.float32),
        in_specs=[pl.BlockSpec(memory_space=pltpu.HBM)] * len(operands),
        out_specs=pl.BlockSpec(memory_space=pltpu.VMEM),
        scratch_shapes=[
            pltpu.VMEM((tokens, model), bf16),
            pltpu.VMEM((tokens, hidden), bf16),
            pltpu.VMEM((tokens, hidden), bf16),
            pltpu.VMEM((tokens, hidden), bf16),
            pltpu.VMEM((tokens, model), bf16),
            pltpu.VMEM((2 * width, model), bf16),
            pltpu.VMEM((width, hidden), bf16),
            pltpu.VMEM((width, hidden), bf16),
            pltpu.VMEM((width, hidden), bf16),
            pltpu.VMEM((width, model), bf16),
            pltpu.VMEM((tokens, 2 * width), jnp.float32),
            pltpu.VMEM((4, tokens, width), jnp.float32),
            pltpu.SemaphoreType.DMA((hidden // STEP + 1,)),
        ],
        compiler_params=pltpu.CompilerParams(vmem_limit_bytes=427 * 2**17),
        cost_estimate=pl.CostEstimate(
            flops=6 * tokens * width * (model + hidden),
            bytes_accessed=2 * (2 * tokens * model + 3 * tokens * hidden),
            transcendentals=tokens * hidden,
        ),
        name="project",
    )(*operands)


def first_chip(chips):
    return chips // 2 + 1


def two_terms(value):
    high = value.astype(jnp.bfloat16)
    return high, (value - high.astype(jnp.float32)).astype(jnp.bfloat16)


def outer(chips, own, other, ids, out, summed, products):
    chip, core = lax.axis_index("dp"), lax.axis_index("mp")
    width = own.shape[1] // 6
    half = width // 2
    span = 3 * half // chips
    summed[...] = (own[...] + other[...]).T
    own_label = 2 * chip + core
    tail_label = jnp.where(core == 1, 2 * chip - 1, -1)
    masks = [(ids[...] == label).astype(jnp.float32) for label in (tail_label, own_label)]
    lane = lax.broadcasted_iota(jnp.int32, (half, 2 * width), 1)
    for module, (left, right) in enumerate(((0, 2), (1, 3), (4, 5))):
        factor = summed[left * width : (left + 1) * width, :]
        high, low = two_terms(jnp.concatenate([factor * mask for mask in masks], axis=0))
        top, bottom = two_terms(summed[right * width : (right + 1) * width, :])
        product = None
        for one, two in ((high, top), (high, bottom), (low, top)):
            both = jnp.concatenate([two, two], axis=0)
            term = lax.dot_general(one, both, NT, preferred_element_type=jnp.float32)
            product = term if product is None else product + term
        products[module] = product
        for label in range(2):
            even = products[module, pl.ds(label * width, half, stride=2), :]
            odd = products[module, pl.ds(label * width + 1, half, stride=2), :]
            packed = jnp.where(lane < width, even, odd)
            row = 0
            while row < half:
                chip_to, inside = divmod(module * half + row, span)
                count = min(span - inside, half - row)
                put = slice(label * span + inside, label * span + inside + count)
                out[(chip_to - first_chip(chips)) % chips, put, :] = packed[row : row + count]
                row += count


def example_blocks(chips, own, other, ids):
    width = own.shape[1] // 6
    block = (3 * width // chips, 2 * width)
    return pl.pallas_call(
        functools.partial(outer, chips),
        out_shape=jax.ShapeDtypeStruct((chips,) + block, jnp.float32),
        in_specs=[pl.BlockSpec(memory_space=pltpu.VMEM)] * 3,
        out_specs=pl.BlockSpec(memory_space=pltpu.VMEM),
        scratch_shapes=[
            pltpu.VMEM(own.shape[::-1], jnp.float32),
            pltpu.VMEM((3, 2 * width, 2 * width), jnp.float32),
        ],
        compiler_params=pltpu.CompilerParams(vmem_limit_bytes=6 * 2**20),
        name="outer",
    )(own, other, ids)


def score(queries, swapped, received, out, rows):
    core = lax.axis_index("mp")
    chips, height, lanes = received.shape
    span = height // 2
    first = first_chip(chips)
    rows[: first * height, :] = received[chips - first :].reshape(first * height, lanes)
    rows[first * height : chips * height, :] = received[: chips - first].reshape((chips - first) * height, lanes)
    rows[chips * height :, :] = jnp.zeros((8, lanes), jnp.float32)
    grads = []
    for at in range(span):
        own = rows[pl.ds(span + at, chips, stride=height), :]
        tail = rows[pl.ds(at, chips, stride=height), :]
        tail = jnp.concatenate([tail[1:], jnp.zeros_like(tail[:1])], axis=0)
        grads.append(own + tail)
    terms = jnp.concatenate(two_terms(jnp.concatenate(grads, axis=1)), axis=0)
    coords = queries.shape[1]
    even = core == 0
    mine = jnp.where(even, terms[:, :coords], terms[:, coords:])
    theirs = jnp.where(even, terms[:, coords:], terms[:, :coords])
    scores = lax.dot_general(mine, queries[...], NT, preferred_element_type=jnp.float32)
    scores += lax.dot_general(theirs, swapped[...], NT, preferred_element_type=jnp.float32)
    total = scores[:chips] + scores[chips:]
    out[...] = jnp.concatenate([total[first:], total[:first]], axis=0)


def partial_scores(queries, swapped, received):
    chips, height, lanes = received.shape
    return pl.pallas_call(
        score,
        out_shape=jax.ShapeDtypeStruct((chips, queries.shape[0]), jnp.float32),
        in_specs=[pl.BlockSpec(memory_space=pltpu.VMEM)] * 3,
        out_specs=pl.BlockSpec(memory_space=pltpu.VMEM),
        scratch_shapes=[pltpu.VMEM((chips * height + 8, lanes), jnp.float32)],
        compiler_params=pltpu.CompilerParams(vmem_limit_bytes=6 * 2**20),
        name="score",
    )(queries, swapped, received)


def to_all(blocks):
    chips = blocks.shape[0]
    order = [(i + first_chip(chips)) % chips for i in range(chips)]
    return lax.all_to_all(
        blocks, "dp", split_axis=0, concat_axis=0, axis_index_groups=[order], tiled=True
    )


def body(
    inputs,
    gate_pre,
    up_pre,
    hidden_grad,
    out_grad,
    example_ids,
    gate_in,
    gate_out,
    up_in,
    up_out,
    down_in,
    down_out,
    queries,
):
    chips = lax.axis_size("dp")
    swap = [(0, 1), (1, 0)]
    swapped = lax.ppermute(queries, "mp", swap)
    bases = [base.T for base in (gate_in, gate_out, up_in, up_out, down_in, down_out)]
    own = projections(inputs, gate_pre, up_pre, hidden_grad, out_grad, *bases)
    other = lax.ppermute(own, "mp", swap)
    blocks = example_blocks(chips, own, other, example_ids.reshape(1, -1))
    received = to_all(blocks)
    scores = partial_scores(queries, swapped, received)[:, None]
    pieces = to_all(scores)
    return jnp.sum(pieces, axis=0)


def solution(mesh):
    placed = (
        P(("parts", "dp"), "mp"),
        P(("parts", "dp"), "mp"),
        P(("parts", "dp"), "mp"),
        P(("parts", "dp"), "mp"),
        P(("parts", "dp"), "mp"),
        P(("parts", "dp")),
        P("mp", None),
        P("mp", None),
        P("mp", None),
        P("mp", None),
        P("mp", None),
        P("mp", None),
        P(None, ("dp", "mp")),
    )
    return jax.shard_map(
        body, mesh=mesh, in_specs=placed, out_specs=P(("parts", "dp", "mp"), None), check_vma=False
    )
```

```python
import functools

import jax
import jax.numpy as jnp
from jax import lax
from jax.experimental import pallas as pl
from jax.experimental.pallas import tpu as pltpu
from jax.sharding import PartitionSpec as P

NT = (((1,), (1,)), ((), ()))
STEP = 1024
TILE = 256
ROWS = 16
AHEAD = 8


def project(
    inputs,
    gate_pre,
    up_pre,
    hidden_grad,
    out_grad,
    gate_in,
    gate_out,
    up_in,
    up_out,
    down_in,
    down_out,
    out,
    v_inputs,
    v_gate,
    v_up,
    v_back,
    v_out_grad,
    v_in,
    v_gate_out,
    v_up_out,
    v_down_in,
    v_down_out,
    sum_in,
    sums,
    sems,
):
    width = gate_in.shape[0]
    tokens = inputs.shape[0]
    hidden, model = gate_pre.shape[1], inputs.shape[1]
    edges = [0] + list(range(STEP // 2, hidden, STEP)) + [hidden]
    steps = len(edges) - 1
    activations = ((gate_pre, v_gate), (up_pre, v_up), (hidden_grad, v_back))
    hidden_bases = ((gate_out, v_gate_out), (up_out, v_up_out), (down_in, v_down_in))
    model_bases = (
        (gate_in, v_in.at[pl.ds(0, width), :]),
        (up_in, v_in.at[pl.ds(width, width), :]),
        (down_out, v_down_out),
    )
    tokens_wide = ((inputs, v_inputs), (out_grad, v_out_grad))
    first_model = 3
    second_model = first_model + model // STEP // 2
    groups = []
    for step in range(steps):
        low, high = edges[step], edges[step + 1]
        pairs = [(pair, low, high - low) for pair in activations]
        if step == 0:
            pairs += [(pair, low, high - low) for pair in hidden_bases]
        if step == 1:
            pairs += [(pair, low, hidden // 2 - low) for pair in hidden_bases]
        if low == hidden // 2:
            pairs += [(pair, low, hidden // 2) for pair in hidden_bases]
        if step == first_model - 1:
            pairs += [(pair, 0, model) for pair in model_bases]
        if step == first_model:
            pairs += [(pair, 0, model // 2) for pair in tokens_wide]
        if step == second_model:
            pairs += [(pair, model // 2, model // 2) for pair in tokens_wide]
        groups.append(pairs)

    def start(step):
        for (source, target), low, length in groups[step]:
            at = pl.ds(low, length)
            pltpu.make_async_copy(source.at[:, at], target.at[:, at], sems.at[step]).start()

    def wait(step):
        count = sum(source.shape[0] * length for (source, _), _, length in groups[step])
        at = pl.ds(0, count // tokens)
        pltpu.make_async_copy(gate_pre.at[:, at], v_gate.at[:, at], sems.at[step]).wait()

    def products(left):
        parts = []
        for top in range(0, tokens, ROWS):
            at = (slice(top, top + ROWS), slice(left, left + TILE))
            half = 0.5 * v_gate[at].astype(jnp.float32)
            up = v_up[at].astype(jnp.float32)
            back = v_back[at].astype(jnp.float32)
            tanh = jnp.tanh(half)
            plus = 1.0 + tanh
            silu = half * plus
            slope = plus + silu * (1.0 - tanh)
            values = (back * up * slope, back * silu, silu * up)
            parts.append([value.astype(jnp.bfloat16) for value in values])
        return [jnp.concatenate(column, axis=0) for column in zip(*parts)]

    def add(total, values, base, first):
        value = lax.dot_general(values, base, NT, preferred_element_type=jnp.float32)
        if first:
            total[...] = value
        else:
            total[...] += value

    def hidden_dots(left):
        at = slice(left, left + TILE)
        bases = (v_gate_out, v_up_out, v_down_in)
        for which, value in enumerate(products(left)):
            add(sums.at[which], value, bases[which][:, at], left == 0)

    def model_dots(left):
        at = slice(left, left + TILE)
        add(sum_in, v_inputs[:, at], v_in[:, at], left == 0)
        add(sums.at[3], v_out_grad[:, at], v_down_out[:, at], left == 0)

    for step in range(AHEAD):
        start(step)
    for step in range(steps):
        if step + AHEAD < steps:
            start(step + AHEAD)
        wait(step)
        for left in range(edges[step], edges[step + 1], TILE):
            hidden_dots(left)
            model_left = left - edges[first_model]
            if 0 <= model_left < model:
                model_dots(model_left)
    out[:, : 2 * width] = sum_in[...]
    out[:, 2 * width : 4 * width] = jnp.concatenate([0.5 * sums[0], sums[1]], axis=1)
    out[:, 4 * width :] = jnp.concatenate([sums[2], sums[3]], axis=1)


def projections(*operands):
    inputs, gate_pre = operands[:2]
    width = operands[5].shape[0]
    tokens, model = inputs.shape
    hidden = gate_pre.shape[1]
    assert hidden % (2 * STEP) == STEP and model % (2 * STEP) == 0 and tokens % ROWS == 0
    assert 3 * STEP + model <= hidden and tokens == 3 * width
    bf16 = jnp.bfloat16
    return pl.pallas_call(
        project,
        out_shape=jax.ShapeDtypeStruct((tokens, 6 * width), jnp.float32),
        in_specs=[pl.BlockSpec(memory_space=pltpu.HBM)] * len(operands),
        out_specs=pl.BlockSpec(memory_space=pltpu.VMEM),
        scratch_shapes=[
            pltpu.VMEM((tokens, model), bf16),
            pltpu.VMEM((tokens, hidden), bf16),
            pltpu.VMEM((tokens, hidden), bf16),
            pltpu.VMEM((tokens, hidden), bf16),
            pltpu.VMEM((tokens, model), bf16),
            pltpu.VMEM((2 * width, model), bf16),
            pltpu.VMEM((width, hidden), bf16),
            pltpu.VMEM((width, hidden), bf16),
            pltpu.VMEM((width, hidden), bf16),
            pltpu.VMEM((width, model), bf16),
            pltpu.VMEM((tokens, 2 * width), jnp.float32),
            pltpu.VMEM((4, tokens, width), jnp.float32),
            pltpu.SemaphoreType.DMA((hidden // STEP + 1,)),
        ],
        compiler_params=pltpu.CompilerParams(vmem_limit_bytes=427 * 2**17),
        cost_estimate=pl.CostEstimate(
            flops=6 * tokens * width * (model + hidden),
            bytes_accessed=2 * (2 * tokens * model + 3 * tokens * hidden),
            transcendentals=tokens * hidden,
        ),
        name="project",
    )(*operands)


def first_chip(chips):
    return chips // 2 + 1


def two_terms(value):
    high = value.astype(jnp.bfloat16)
    return high, (value - high.astype(jnp.float32)).astype(jnp.bfloat16)


def outer(chips, own, other, ids, out, summed, products):
    chip, core = lax.axis_index("dp"), lax.axis_index("mp")
    width = own.shape[1] // 6
    half = width // 2
    span = 3 * half // chips
    summed[...] = (own[...] + other[...]).T
    own_label = 2 * chip + core
    tail_label = jnp.where(core == 1, 2 * chip - 1, -1)
    masks = [(ids[...] == label).astype(jnp.float32) for label in (tail_label, own_label)]
    lane = lax.broadcasted_iota(jnp.int32, (half, 2 * width), 1)
    for module, (left, right) in enumerate(((0, 2), (1, 3), (4, 5))):
        factor = summed[left * width : (left + 1) * width, :]
        high, low = two_terms(jnp.concatenate([factor * mask for mask in masks], axis=0))
        top, bottom = two_terms(summed[right * width : (right + 1) * width, :])
        product = None
        for one, two in ((high, top), (high, bottom), (low, top)):
            both = jnp.concatenate([two, two], axis=0)
            term = lax.dot_general(one, both, NT, preferred_element_type=jnp.float32)
            product = term if product is None else product + term
        products[module] = product
        for label in range(2):
            even = products[module, pl.ds(label * width, half, stride=2), :]
            odd = products[module, pl.ds(label * width + 1, half, stride=2), :]
            packed = jnp.where(lane < width, even, odd)
            row = 0
            while row < half:
                chip_to, inside = divmod(module * half + row, span)
                count = min(span - inside, half - row)
                put = slice(label * span + inside, label * span + inside + count)
                out[(chip_to - first_chip(chips)) % chips, put, :] = packed[row : row + count]
                row += count


def example_blocks(chips, own, other, ids):
    width = own.shape[1] // 6
    block = (3 * width // chips, 2 * width)
    return pl.pallas_call(
        functools.partial(outer, chips),
        out_shape=jax.ShapeDtypeStruct((chips,) + block, jnp.float32),
        in_specs=[pl.BlockSpec(memory_space=pltpu.VMEM)] * 3,
        out_specs=pl.BlockSpec(memory_space=pltpu.VMEM),
        scratch_shapes=[
            pltpu.VMEM(own.shape[::-1], jnp.float32),
            pltpu.VMEM((3, 2 * width, 2 * width), jnp.float32),
        ],
        compiler_params=pltpu.CompilerParams(vmem_limit_bytes=6 * 2**20),
        name="outer",
    )(own, other, ids)


def score(queries, swapped, received, out, rows):
    core = lax.axis_index("mp")
    chips, height, lanes = received.shape
    span = height // 2
    first = first_chip(chips)
    rows[: first * height, :] = received[chips - first :].reshape(first * height, lanes)
    rows[first * height : chips * height, :] = received[: chips - first].reshape((chips - first) * height, lanes)
    rows[chips * height :, :] = jnp.zeros((8, lanes), jnp.float32)
    grads = []
    for at in range(span):
        own = rows[pl.ds(span + at, chips, stride=height), :]
        tail = rows[pl.ds(at, chips, stride=height), :]
        tail = jnp.concatenate([tail[1:], jnp.zeros_like(tail[:1])], axis=0)
        grads.append(own + tail)
    terms = jnp.concatenate(two_terms(jnp.concatenate(grads, axis=1)), axis=0)
    coords = queries.shape[1]
    even = core == 0
    mine = jnp.where(even, terms[:, :coords], terms[:, coords:])
    theirs = jnp.where(even, terms[:, coords:], terms[:, :coords])
    scores = lax.dot_general(mine, queries[...], NT, preferred_element_type=jnp.float32)
    scores += lax.dot_general(theirs, swapped[...], NT, preferred_element_type=jnp.float32)
    total = scores[:chips] + scores[chips:]
    out[...] = jnp.concatenate([total[first:], total[:first]], axis=0)


def partial_scores(queries, swapped, received):
    chips, height, lanes = received.shape
    return pl.pallas_call(
        score,
        out_shape=jax.ShapeDtypeStruct((chips, queries.shape[0]), jnp.float32),
        in_specs=[pl.BlockSpec(memory_space=pltpu.VMEM)] * 3,
        out_specs=pl.BlockSpec(memory_space=pltpu.VMEM),
        scratch_shapes=[pltpu.VMEM((chips * height + 8, lanes), jnp.float32)],
        compiler_params=pltpu.CompilerParams(vmem_limit_bytes=6 * 2**20),
        name="score",
    )(queries, swapped, received)


def to_all(blocks):
    chips = blocks.shape[0]
    order = [(i + first_chip(chips)) % chips for i in range(chips)]
    return lax.all_to_all(
        blocks, "dp", split_axis=0, concat_axis=0, axis_index_groups=[order], tiled=True
    )


def body(
    inputs,
    gate_pre,
    up_pre,
    hidden_grad,
    out_grad,
    example_ids,
    gate_in,
    gate_out,
    up_in,
    up_out,
    down_in,
    down_out,
    queries,
):
    chips = lax.axis_size("dp")
    swap = [(0, 1), (1, 0)]
    bases = [base.T for base in (gate_in, gate_out, up_in, up_out, down_in, down_out)]
    own = projections(inputs, gate_pre, up_pre, hidden_grad, out_grad, *bases)
    other = lax.ppermute(own, "mp", swap)
    other, queries = lax.optimization_barrier((other, queries))
    swapped = lax.ppermute(queries, "mp", swap)
    blocks = example_blocks(chips, own, other, example_ids.reshape(1, -1))
    received = to_all(blocks)
    scores = partial_scores(queries, swapped, received)[:, None]
    pieces = to_all(scores)
    return jnp.sum(pieces, axis=0)


def solution(mesh):
    placed = (
        P(("parts", "dp"), "mp"),
        P(("parts", "dp"), "mp"),
        P(("parts", "dp"), "mp"),
        P(("parts", "dp"), "mp"),
        P(("parts", "dp"), "mp"),
        P(("parts", "dp")),
        P("mp", None),
        P("mp", None),
        P("mp", None),
        P("mp", None),
        P("mp", None),
        P("mp", None),
        P(None, ("dp", "mp")),
    )
    return jax.shard_map(
        body, mesh=mesh, in_specs=placed, out_specs=P(("parts", "dp", "mp"), None), check_vma=False
    )
```

```python
import functools

import jax
import jax.numpy as jnp
from jax import lax
from jax.experimental import pallas as pl
from jax.experimental.pallas import tpu as pltpu
from jax.sharding import PartitionSpec as P

NT = (((1,), (1,)), ((), ()))
STEP = 1024
TILE = 256
ROWS = 16
AHEAD = 8


def project(
    inputs,
    gate_pre,
    up_pre,
    hidden_grad,
    out_grad,
    gate_in,
    gate_out,
    up_in,
    up_out,
    down_in,
    down_out,
    out,
    v_inputs,
    v_gate,
    v_up,
    v_back,
    v_out_grad,
    v_in,
    v_gate_out,
    v_up_out,
    v_down_in,
    v_down_out,
    sum_in,
    sums,
    sems,
):
    width = gate_in.shape[0]
    tokens = inputs.shape[0]
    hidden, model = gate_pre.shape[1], inputs.shape[1]
    edges = [0] + list(range(STEP // 2, hidden, STEP)) + [hidden]
    steps = len(edges) - 1
    activations = ((gate_pre, v_gate), (up_pre, v_up), (hidden_grad, v_back))
    hidden_bases = ((gate_out, v_gate_out), (up_out, v_up_out), (down_in, v_down_in))
    model_bases = (
        (gate_in, v_in.at[pl.ds(0, width), :]),
        (up_in, v_in.at[pl.ds(width, width), :]),
        (down_out, v_down_out),
    )
    tokens_wide = ((inputs, v_inputs), (out_grad, v_out_grad))
    first_model = 3
    second_model = first_model + model // STEP // 2
    groups = []
    for step in range(steps):
        low, high = edges[step], edges[step + 1]
        pairs = [(pair, low, high - low) for pair in activations]
        if step == 0:
            pairs += [(pair, low, high - low) for pair in hidden_bases]
        if step == 1:
            pairs += [(pair, low, hidden // 2 - low) for pair in hidden_bases]
        if low == hidden // 2:
            pairs += [(pair, low, hidden // 2) for pair in hidden_bases]
        if step == first_model - 1:
            pairs += [(pair, 0, model) for pair in model_bases]
        if step == first_model:
            pairs += [(pair, 0, model // 2) for pair in tokens_wide]
        if step == second_model:
            pairs += [(pair, model // 2, model // 2) for pair in tokens_wide]
        groups.append(pairs)

    def start(step):
        for (source, target), low, length in groups[step]:
            at = pl.ds(low, length)
            pltpu.make_async_copy(source.at[:, at], target.at[:, at], sems.at[step]).start()

    def wait(step):
        count = sum(source.shape[0] * length for (source, _), _, length in groups[step])
        at = pl.ds(0, count // tokens)
        pltpu.make_async_copy(gate_pre.at[:, at], v_gate.at[:, at], sems.at[step]).wait()

    def products(left):
        parts = []
        for top in range(0, tokens, ROWS):
            at = (slice(top, top + ROWS), slice(left, left + TILE))
            half = 0.5 * v_gate[at].astype(jnp.float32)
            up = v_up[at].astype(jnp.float32)
            back = v_back[at].astype(jnp.float32)
            tanh = jnp.tanh(half)
            plus = 1.0 + tanh
            silu = half * plus
            slope = plus + silu * (1.0 - tanh)
            values = (back * up * slope, back * silu, silu * up)
            parts.append([value.astype(jnp.bfloat16) for value in values])
        return [jnp.concatenate(column, axis=0) for column in zip(*parts)]

    def add(total, values, base, first):
        value = lax.dot_general(values, base, NT, preferred_element_type=jnp.float32)
        if first:
            total[...] = value
        else:
            total[...] += value

    def hidden_dots(left):
        at = slice(left, left + TILE)
        bases = (v_gate_out, v_up_out, v_down_in)
        for which, value in enumerate(products(left)):
            add(sums.at[which], value, bases[which][:, at], left == 0)

    def model_dots(left):
        at = slice(left, left + TILE)
        add(sum_in, v_inputs[:, at], v_in[:, at], left == 0)
        add(sums.at[3], v_out_grad[:, at], v_down_out[:, at], left == 0)

    for step in range(AHEAD):
        start(step)
    for step in range(steps):
        if step + AHEAD < steps:
            start(step + AHEAD)
        wait(step)
        for left in range(edges[step], edges[step + 1], TILE):
            hidden_dots(left)
            model_left = left - edges[first_model]
            if 0 <= model_left < model:
                model_dots(model_left)
    out[:, : 2 * width] = sum_in[...]
    out[:, 2 * width : 4 * width] = jnp.concatenate([0.5 * sums[0], sums[1]], axis=1)
    out[:, 4 * width :] = jnp.concatenate([sums[2], sums[3]], axis=1)


def projections(*operands):
    inputs, gate_pre = operands[:2]
    width = operands[5].shape[0]
    tokens, model = inputs.shape
    hidden = gate_pre.shape[1]
    assert hidden % (2 * STEP) == STEP and model % (2 * STEP) == 0 and tokens % ROWS == 0
    assert 3 * STEP + model <= hidden and tokens == 3 * width
    bf16 = jnp.bfloat16
    return pl.pallas_call(
        project,
        out_shape=jax.ShapeDtypeStruct((tokens, 6 * width), jnp.float32),
        in_specs=[pl.BlockSpec(memory_space=pltpu.HBM)] * len(operands),
        out_specs=pl.BlockSpec(memory_space=pltpu.VMEM),
        scratch_shapes=[
            pltpu.VMEM((tokens, model), bf16),
            pltpu.VMEM((tokens, hidden), bf16),
            pltpu.VMEM((tokens, hidden), bf16),
            pltpu.VMEM((tokens, hidden), bf16),
            pltpu.VMEM((tokens, model), bf16),
            pltpu.VMEM((2 * width, model), bf16),
            pltpu.VMEM((width, hidden), bf16),
            pltpu.VMEM((width, hidden), bf16),
            pltpu.VMEM((width, hidden), bf16),
            pltpu.VMEM((width, model), bf16),
            pltpu.VMEM((tokens, 2 * width), jnp.float32),
            pltpu.VMEM((4, tokens, width), jnp.float32),
            pltpu.SemaphoreType.DMA((hidden // STEP + 1,)),
        ],
        compiler_params=pltpu.CompilerParams(vmem_limit_bytes=427 * 2**17),
        cost_estimate=pl.CostEstimate(
            flops=6 * tokens * width * (model + hidden),
            bytes_accessed=2 * (2 * tokens * model + 3 * tokens * hidden),
            transcendentals=tokens * hidden,
        ),
        name="project",
    )(*operands)


def listed(chips):
    first = chips // 2 + 1
    return [first] + [chip for chip in range(chips) if chip != first]


def two_terms(value):
    high = value.astype(jnp.bfloat16)
    return high, (value - high.astype(jnp.float32)).astype(jnp.bfloat16)


def outer(chips, own, other, ids, out, summed, products):
    chip, core = lax.axis_index("dp"), lax.axis_index("mp")
    width = own.shape[1] // 6
    half = width // 2
    span = 3 * half // chips
    order = listed(chips)
    summed[...] = (own[...] + other[...]).T
    own_label = 2 * chip + core
    tail_label = jnp.where(core == 1, 2 * chip - 1, -1)
    masks = [(ids[...] == label).astype(jnp.float32) for label in (tail_label, own_label)]
    lane = lax.broadcasted_iota(jnp.int32, (half, 2 * width), 1)
    for module, (left, right) in enumerate(((0, 2), (1, 3), (4, 5))):
        factor = summed[left * width : (left + 1) * width, :]
        high, low = two_terms(jnp.concatenate([factor * mask for mask in masks], axis=0))
        top, bottom = two_terms(summed[right * width : (right + 1) * width, :])
        product = None
        for one, two in ((high, top), (high, bottom), (low, top)):
            both = jnp.concatenate([two, two], axis=0)
            term = lax.dot_general(one, both, NT, preferred_element_type=jnp.float32)
            product = term if product is None else product + term
        products[module] = product
        for label in range(2):
            even = products[module, pl.ds(label * width, half, stride=2), :]
            odd = products[module, pl.ds(label * width + 1, half, stride=2), :]
            packed = jnp.where(lane < width, even, odd)
            row = 0
            while row < half:
                chip_to, inside = divmod(module * half + row, span)
                count = min(span - inside, half - row)
                put = slice(label * span + inside, label * span + inside + count)
                out[order.index(chip_to), put, :] = packed[row : row + count]
                row += count


def example_blocks(chips, own, other, ids):
    width = own.shape[1] // 6
    block = (3 * width // chips, 2 * width)
    return pl.pallas_call(
        functools.partial(outer, chips),
        out_shape=jax.ShapeDtypeStruct((chips,) + block, jnp.float32),
        in_specs=[pl.BlockSpec(memory_space=pltpu.VMEM)] * 3,
        out_specs=pl.BlockSpec(memory_space=pltpu.VMEM),
        scratch_shapes=[
            pltpu.VMEM(own.shape[::-1], jnp.float32),
            pltpu.VMEM((3, 2 * width, 2 * width), jnp.float32),
        ],
        compiler_params=pltpu.CompilerParams(vmem_limit_bytes=6 * 2**20),
        name="outer",
    )(own, other, ids)


def score(queries, swapped, received, out, rows):
    core = lax.axis_index("mp")
    chips, height, lanes = received.shape
    span = height // 2
    order = listed(chips)
    for place, chip in enumerate(order):
        rows[chip * height : (chip + 1) * height, :] = received[place]
    rows[chips * height :, :] = jnp.zeros((8, lanes), jnp.float32)
    grads = []
    for at in range(span):
        own = rows[pl.ds(span + at, chips, stride=height), :]
        tail = rows[pl.ds(at, chips, stride=height), :]
        tail = jnp.concatenate([tail[1:], jnp.zeros_like(tail[:1])], axis=0)
        grads.append(own + tail)
    terms = jnp.concatenate(two_terms(jnp.concatenate(grads, axis=1)), axis=0)
    coords = queries.shape[1]
    even = core == 0
    mine = jnp.where(even, terms[:, :coords], terms[:, coords:])
    theirs = jnp.where(even, terms[:, coords:], terms[:, :coords])
    scores = lax.dot_general(mine, queries[...], NT, preferred_element_type=jnp.float32)
    scores += lax.dot_general(theirs, swapped[...], NT, preferred_element_type=jnp.float32)
    total = scores[:chips] + scores[chips:]
    out[...] = jnp.concatenate([total[chip : chip + 1] for chip in order], axis=0)


def partial_scores(queries, swapped, received):
    chips, height, lanes = received.shape
    return pl.pallas_call(
        score,
        out_shape=jax.ShapeDtypeStruct((chips, queries.shape[0]), jnp.float32),
        in_specs=[pl.BlockSpec(memory_space=pltpu.VMEM)] * 3,
        out_specs=pl.BlockSpec(memory_space=pltpu.VMEM),
        scratch_shapes=[pltpu.VMEM((chips * height + 8, lanes), jnp.float32)],
        compiler_params=pltpu.CompilerParams(vmem_limit_bytes=6 * 2**20),
        name="score",
    )(queries, swapped, received)


def to_all(blocks):
    chips = blocks.shape[0]
    return lax.all_to_all(
        blocks, "dp", split_axis=0, concat_axis=0, axis_index_groups=[listed(chips)], tiled=True
    )


def body(
    inputs,
    gate_pre,
    up_pre,
    hidden_grad,
    out_grad,
    example_ids,
    gate_in,
    gate_out,
    up_in,
    up_out,
    down_in,
    down_out,
    queries,
):
    chips = lax.axis_size("dp")
    swap = [(0, 1), (1, 0)]
    swapped = lax.ppermute(queries, "mp", swap)
    bases = [base.T for base in (gate_in, gate_out, up_in, up_out, down_in, down_out)]
    own = projections(inputs, gate_pre, up_pre, hidden_grad, out_grad, *bases)
    other = lax.ppermute(own, "mp", swap)
    blocks = example_blocks(chips, own, other, example_ids.reshape(1, -1))
    received = to_all(blocks)
    scores = partial_scores(queries, swapped, received)[:, None]
    pieces = to_all(scores)
    return jnp.sum(pieces, axis=0)


def solution(mesh):
    placed = (
        P(("parts", "dp"), "mp"),
        P(("parts", "dp"), "mp"),
        P(("parts", "dp"), "mp"),
        P(("parts", "dp"), "mp"),
        P(("parts", "dp"), "mp"),
        P(("parts", "dp")),
        P("mp", None),
        P("mp", None),
        P("mp", None),
        P("mp", None),
        P("mp", None),
        P("mp", None),
        P(None, ("dp", "mp")),
    )
    return jax.shard_map(
        body, mesh=mesh, in_specs=placed, out_specs=P(("parts", "dp", "mp"), None), check_vma=False
    )
```

```python
import functools

import jax
import jax.numpy as jnp
from jax import lax
from jax.experimental import pallas as pl
from jax.experimental.pallas import tpu as pltpu
from jax.sharding import PartitionSpec as P

NT = (((1,), (1,)), ((), ()))
STEP = 1024
TILE = 256
ROWS = 16
AHEAD = 8


def project(
    inputs,
    gate_pre,
    up_pre,
    hidden_grad,
    out_grad,
    gate_in,
    gate_out,
    up_in,
    up_out,
    down_in,
    down_out,
    kept,
    given,
    v_inputs,
    v_gate,
    v_up,
    v_back,
    v_out_grad,
    v_in,
    v_gate_out,
    v_up_out,
    v_down_in,
    v_down_out,
    sum_in,
    sums,
    sems,
):
    width = gate_in.shape[0]
    tokens = inputs.shape[0]
    hidden, model = gate_pre.shape[1], inputs.shape[1]
    edges = [0] + list(range(STEP // 2, hidden, STEP)) + [hidden]
    steps = len(edges) - 1
    activations = ((gate_pre, v_gate), (up_pre, v_up), (hidden_grad, v_back))
    hidden_bases = ((gate_out, v_gate_out), (up_out, v_up_out), (down_in, v_down_in))
    model_bases = (
        (gate_in, v_in.at[pl.ds(0, width), :]),
        (up_in, v_in.at[pl.ds(width, width), :]),
        (down_out, v_down_out),
    )
    tokens_wide = ((inputs, v_inputs), (out_grad, v_out_grad))
    first_model = 3
    second_model = first_model + model // STEP // 2
    groups = []
    for step in range(steps):
        low, high = edges[step], edges[step + 1]
        pairs = [(pair, low, high - low) for pair in activations]
        if step == 0:
            pairs += [(pair, low, high - low) for pair in hidden_bases]
        if step == 1:
            pairs += [(pair, low, hidden // 2 - low) for pair in hidden_bases]
        if low == hidden // 2:
            pairs += [(pair, low, hidden // 2) for pair in hidden_bases]
        if step == first_model - 1:
            pairs += [(pair, 0, model) for pair in model_bases]
        if step == first_model:
            pairs += [(pair, 0, model // 2) for pair in tokens_wide]
        if step == second_model:
            pairs += [(pair, model // 2, model // 2) for pair in tokens_wide]
        groups.append(pairs)

    def start(step):
        for (source, target), low, length in groups[step]:
            at = pl.ds(low, length)
            pltpu.make_async_copy(source.at[:, at], target.at[:, at], sems.at[step]).start()

    def wait(step):
        count = sum(source.shape[0] * length for (source, _), _, length in groups[step])
        at = pl.ds(0, count // tokens)
        pltpu.make_async_copy(gate_pre.at[:, at], v_gate.at[:, at], sems.at[step]).wait()

    def products(left):
        parts = []
        for top in range(0, tokens, ROWS):
            at = (slice(top, top + ROWS), slice(left, left + TILE))
            half = 0.5 * v_gate[at].astype(jnp.float32)
            up = v_up[at].astype(jnp.float32)
            back = v_back[at].astype(jnp.float32)
            tanh = jnp.tanh(half)
            plus = 1.0 + tanh
            silu = half * plus
            slope = plus + silu * (1.0 - tanh)
            values = (back * up * slope, back * silu, silu * up)
            parts.append([value.astype(jnp.bfloat16) for value in values])
        return [jnp.concatenate(column, axis=0) for column in zip(*parts)]

    def add(total, values, base, first):
        value = lax.dot_general(values, base, NT, preferred_element_type=jnp.float32)
        if first:
            total[...] = value
        else:
            total[...] += value

    def hidden_dots(left):
        at = slice(left, left + TILE)
        bases = (v_gate_out, v_up_out, v_down_in)
        for which, value in enumerate(products(left)):
            add(sums.at[which], value, bases[which][:, at], left == 0)

    def model_dots(left):
        at = slice(left, left + TILE)
        add(sum_in, v_inputs[:, at], v_in[:, at], left == 0)
        add(sums.at[3], v_out_grad[:, at], v_down_out[:, at], left == 0)

    for step in range(AHEAD):
        start(step)
    for step in range(steps):
        if step + AHEAD < steps:
            start(step + AHEAD)
        wait(step)
        for left in range(edges[step], edges[step + 1], TILE):
            hidden_dots(left)
            model_left = left - edges[first_model]
            if 0 <= model_left < model:
                model_dots(model_left)
    core = lax.axis_index("mp")
    half = tokens // 2
    for out, which in ((kept, core), (given, 1 - core)):
        rows = pl.ds(pl.multiple_of(which * half, half), half)
        out[:, : 2 * width] = sum_in[rows, :]
        out[:, 2 * width : 4 * width] = jnp.concatenate(
            [0.5 * sums[0, rows, :], sums[1, rows, :]], axis=1
        )
        out[:, 4 * width :] = jnp.concatenate([sums[2, rows, :], sums[3, rows, :]], axis=1)


def projections(*operands):
    inputs, gate_pre = operands[:2]
    width = operands[5].shape[0]
    tokens, model = inputs.shape
    hidden = gate_pre.shape[1]
    assert hidden % (2 * STEP) == STEP and model % (2 * STEP) == 0 and tokens % ROWS == 0
    assert 3 * STEP + model <= hidden and tokens == 3 * width
    bf16 = jnp.bfloat16
    return pl.pallas_call(
        project,
        out_shape=[jax.ShapeDtypeStruct((tokens // 2, 6 * width), jnp.float32)] * 2,
        in_specs=[pl.BlockSpec(memory_space=pltpu.HBM)] * len(operands),
        out_specs=[pl.BlockSpec(memory_space=pltpu.VMEM)] * 2,
        scratch_shapes=[
            pltpu.VMEM((tokens, model), bf16),
            pltpu.VMEM((tokens, hidden), bf16),
            pltpu.VMEM((tokens, hidden), bf16),
            pltpu.VMEM((tokens, hidden), bf16),
            pltpu.VMEM((tokens, model), bf16),
            pltpu.VMEM((2 * width, model), bf16),
            pltpu.VMEM((width, hidden), bf16),
            pltpu.VMEM((width, hidden), bf16),
            pltpu.VMEM((width, hidden), bf16),
            pltpu.VMEM((width, model), bf16),
            pltpu.VMEM((tokens, 2 * width), jnp.float32),
            pltpu.VMEM((4, tokens, width), jnp.float32),
            pltpu.SemaphoreType.DMA((hidden // STEP + 1,)),
        ],
        compiler_params=pltpu.CompilerParams(vmem_limit_bytes=427 * 2**17),
        cost_estimate=pl.CostEstimate(
            flops=6 * tokens * width * (model + hidden),
            bytes_accessed=2 * (2 * tokens * model + 3 * tokens * hidden),
            transcendentals=tokens * hidden,
        ),
        name="project",
    )(*operands)


def first_chip(chips):
    return chips // 2 + 1


def first_device(chips):
    return 2 * first_chip(chips) + 1


def two_terms(value):
    high = value.astype(jnp.bfloat16)
    return high, (value - high.astype(jnp.float32)).astype(jnp.bfloat16)


def outer(chips, own, other, ids, out, summed, products):
    chip, core = lax.axis_index("dp"), lax.axis_index("mp")
    width = own.shape[1] // 6
    half = width // 2
    span = 3 * half // chips
    summed[...] = (own[...] + other[...]).T
    label = 2 * chip + core
    mine = ids[pl.ds(core, 1), :]
    masks = [(mine == each).astype(jnp.float32) for each in (label - 1, label)]
    lane = lax.broadcasted_iota(jnp.int32, (half, 2 * width), 1)
    for module, (left, right) in enumerate(((0, 2), (1, 3), (4, 5))):
        factor = summed[left * width : (left + 1) * width, :]
        high, low = two_terms(jnp.concatenate([factor * mask for mask in masks], axis=0))
        top, bottom = two_terms(summed[right * width : (right + 1) * width, :])
        product = None
        for one, two in ((high, top), (high, bottom), (low, top)):
            both = jnp.concatenate([two, two], axis=0)
            term = lax.dot_general(one, both, NT, preferred_element_type=jnp.float32)
            product = term if product is None else product + term
        products[module] = product
        for label in range(2):
            even = products[module, pl.ds(label * width, half, stride=2), :]
            odd = products[module, pl.ds(label * width + 1, half, stride=2), :]
            packed = jnp.where(lane < width, even, odd)
            row = 0
            while row < half:
                chip_to, inside = divmod(module * half + row, span)
                count = min(span - inside, half - row)
                put = slice(label * span + inside, label * span + inside + count)
                out[(chip_to - first_chip(chips)) % chips, put, :] = packed[row : row + count]
                row += count


def example_blocks(chips, own, other, ids):
    width = own.shape[1] // 6
    block = (3 * width // chips, 2 * width)
    return pl.pallas_call(
        functools.partial(outer, chips),
        out_shape=jax.ShapeDtypeStruct((chips,) + block, jnp.float32),
        in_specs=[pl.BlockSpec(memory_space=pltpu.VMEM)] * 3,
        out_specs=pl.BlockSpec(memory_space=pltpu.VMEM),
        scratch_shapes=[
            pltpu.VMEM(own.shape[::-1], jnp.float32),
            pltpu.VMEM((3, 2 * width, 2 * width), jnp.float32),
        ],
        compiler_params=pltpu.CompilerParams(vmem_limit_bytes=6 * 2**20),
        name="outer",
    )(own, other, ids)


def score(queries, swapped, received, out, rows):
    core = lax.axis_index("mp")
    chips, height, lanes = received.shape
    span = height // 2
    first = first_chip(chips)
    rows[: first * height, :] = received[chips - first :].reshape(first * height, lanes)
    rows[first * height : chips * height, :] = received[: chips - first].reshape((chips - first) * height, lanes)
    grads = []
    for label in range(2):
        parts = [rows[pl.ds(label * span + at, chips, stride=height), :] for at in range(span)]
        grads.append(jnp.concatenate(parts, axis=1))
    terms = jnp.concatenate(two_terms(jnp.concatenate(grads, axis=0)), axis=0)
    coords = queries.shape[1]
    even = core == 0
    mine = jnp.where(even, terms[:, :coords], terms[:, coords:])
    theirs = jnp.where(even, terms[:, coords:], terms[:, :coords])
    scores = lax.dot_general(mine, queries[...], NT, preferred_element_type=jnp.float32)
    scores += lax.dot_general(theirs, swapped[...], NT, preferred_element_type=jnp.float32)
    total = scores[: 2 * chips] + scores[2 * chips :]
    none = jnp.zeros_like(total[:1])
    tails = [total[chip : chip + 1] for chip in range(chips)] + [none]
    owns = [total[chips + chip : chips + chip + 1] for chip in range(chips)]
    for device in range(2 * chips):
        place = (device - first_device(chips)) % (2 * chips)
        chip = device // 2
        if device % 2 == 0:
            row = jnp.where(even, owns[chip], tails[chip])
        else:
            row = jnp.where(even, tails[chip + 1], owns[chip])
        out[place : place + 1, :] = row


def partial_scores(queries, swapped, received):
    chips, height, lanes = received.shape
    return pl.pallas_call(
        score,
        out_shape=jax.ShapeDtypeStruct((2 * chips, queries.shape[0]), jnp.float32),
        in_specs=[pl.BlockSpec(memory_space=pltpu.VMEM)] * 3,
        out_specs=pl.BlockSpec(memory_space=pltpu.VMEM),
        scratch_shapes=[pltpu.VMEM((chips * height, lanes), jnp.float32)],
        compiler_params=pltpu.CompilerParams(vmem_limit_bytes=6 * 2**20),
        name="score",
    )(queries, swapped, received)


def to_all(blocks, axes, first):
    count = blocks.shape[0]
    order = [(i + first) % count for i in range(count)]
    return lax.all_to_all(
        blocks, axes, split_axis=0, concat_axis=0, axis_index_groups=[order], tiled=True
    )


def body(
    inputs,
    gate_pre,
    up_pre,
    hidden_grad,
    out_grad,
    example_ids,
    gate_in,
    gate_out,
    up_in,
    up_out,
    down_in,
    down_out,
    queries,
):
    chips = lax.axis_size("dp")
    swap = [(0, 1), (1, 0)]
    swapped = lax.ppermute(queries, "mp", swap)
    bases = [base.T for base in (gate_in, gate_out, up_in, up_out, down_in, down_out)]
    own, given = projections(inputs, gate_pre, up_pre, hidden_grad, out_grad, *bases)
    other = lax.ppermute(given, "mp", swap)
    blocks = example_blocks(chips, own, other, example_ids.reshape(2, -1))
    received = to_all(blocks, "dp", first_chip(chips))
    scores = partial_scores(queries, swapped, received)[:, None]
    pieces = to_all(scores, ("dp", "mp"), first_device(chips))
    return jnp.sum(pieces, axis=0)


def solution(mesh):
    placed = (
        P(("parts", "dp"), "mp"),
        P(("parts", "dp"), "mp"),
        P(("parts", "dp"), "mp"),
        P(("parts", "dp"), "mp"),
        P(("parts", "dp"), "mp"),
        P(("parts", "dp")),
        P("mp", None),
        P("mp", None),
        P("mp", None),
        P("mp", None),
        P("mp", None),
        P("mp", None),
        P(None, ("dp", "mp")),
    )
    return jax.shard_map(
        body, mesh=mesh, in_specs=placed, out_specs=P(("parts", "dp", "mp"), None), check_vma=False
    )
```

```python
import functools

import jax
import jax.numpy as jnp
from jax import lax
from jax.experimental import pallas as pl
from jax.experimental.pallas import tpu as pltpu
from jax.sharding import PartitionSpec as P

NT = (((1,), (1,)), ((), ()))
STEP = 1024
TILE = 256
ROWS = 16
AHEAD = 8


def project(
    inputs,
    gate_pre,
    up_pre,
    hidden_grad,
    out_grad,
    gate_in,
    gate_out,
    up_in,
    up_out,
    down_in,
    down_out,
    kept,
    given,
    v_inputs,
    v_gate,
    v_up,
    v_back,
    v_out_grad,
    v_in,
    v_gate_out,
    v_up_out,
    v_down_in,
    v_down_out,
    sum_in,
    sums,
    sems,
):
    width = gate_in.shape[0]
    tokens = inputs.shape[0]
    hidden, model = gate_pre.shape[1], inputs.shape[1]
    edges = [0] + list(range(STEP // 2, hidden, STEP)) + [hidden]
    steps = len(edges) - 1
    activations = ((gate_pre, v_gate), (up_pre, v_up), (hidden_grad, v_back))
    hidden_bases = ((gate_out, v_gate_out), (up_out, v_up_out), (down_in, v_down_in))
    model_bases = (
        (gate_in, v_in.at[pl.ds(0, width), :]),
        (up_in, v_in.at[pl.ds(width, width), :]),
        (down_out, v_down_out),
    )
    tokens_wide = ((inputs, v_inputs), (out_grad, v_out_grad))
    first_model = 3
    second_model = first_model + model // STEP // 2
    groups = []
    for step in range(steps):
        low, high = edges[step], edges[step + 1]
        pairs = [(pair, low, high - low) for pair in activations]
        if step == 0:
            pairs += [(pair, low, high - low) for pair in hidden_bases]
        if step == 1:
            pairs += [(pair, low, hidden // 2 - low) for pair in hidden_bases]
        if low == hidden // 2:
            pairs += [(pair, low, hidden // 2) for pair in hidden_bases]
        if step == first_model - 1:
            pairs += [(pair, 0, model) for pair in model_bases]
        if step == first_model:
            pairs += [(pair, 0, model // 2) for pair in tokens_wide]
        if step == second_model:
            pairs += [(pair, model // 2, model // 2) for pair in tokens_wide]
        groups.append(pairs)

    def start(step):
        for index, ((source, target), low, length) in enumerate(groups[step]):
            at = pl.ds(low, length)
            copy = pltpu.make_async_copy(source.at[:, at], target.at[:, at], sems.at[step])
            copy.start(priority=index % 2)

    def wait(step):
        count = sum(source.shape[0] * length for (source, _), _, length in groups[step])
        at = pl.ds(0, count // tokens)
        pltpu.make_async_copy(gate_pre.at[:, at], v_gate.at[:, at], sems.at[step]).wait()

    def products(left):
        parts = []
        for top in range(0, tokens, ROWS):
            at = (slice(top, top + ROWS), slice(left, left + TILE))
            half = 0.5 * v_gate[at].astype(jnp.float32)
            up = v_up[at].astype(jnp.float32)
            back = v_back[at].astype(jnp.float32)
            tanh = jnp.tanh(half)
            plus = 1.0 + tanh
            silu = half * plus
            slope = plus + silu * (1.0 - tanh)
            values = (back * up * slope, back * silu, silu * up)
            parts.append([value.astype(jnp.bfloat16) for value in values])
        return [jnp.concatenate(column, axis=0) for column in zip(*parts)]

    def add(total, values, base, first):
        value = lax.dot_general(values, base, NT, preferred_element_type=jnp.float32)
        if first:
            total[...] = value
        else:
            total[...] += value

    def hidden_dots(left):
        at = slice(left, left + TILE)
        bases = (v_gate_out, v_up_out, v_down_in)
        for which, value in enumerate(products(left)):
            add(sums.at[which], value, bases[which][:, at], left == 0)

    def model_dots(left):
        at = slice(left, left + TILE)
        add(sum_in, v_inputs[:, at], v_in[:, at], left == 0)
        add(sums.at[3], v_out_grad[:, at], v_down_out[:, at], left == 0)

    for step in range(AHEAD):
        start(step)
    for step in range(steps):
        if step + AHEAD < steps:
            start(step + AHEAD)
        wait(step)
        for left in range(edges[step], edges[step + 1], TILE):
            hidden_dots(left)
            model_left = left - edges[first_model]
            if 0 <= model_left < model:
                model_dots(model_left)
    core = lax.axis_index("mp")
    half = tokens // 2
    for out, which in ((kept, core), (given, 1 - core)):
        rows = pl.ds(pl.multiple_of(which * half, half), half)
        out[:, : 2 * width] = sum_in[rows, :]
        out[:, 2 * width : 4 * width] = jnp.concatenate(
            [0.5 * sums[0, rows, :], sums[1, rows, :]], axis=1
        )
        out[:, 4 * width :] = jnp.concatenate([sums[2, rows, :], sums[3, rows, :]], axis=1)


def projections(*operands):
    inputs, gate_pre = operands[:2]
    width = operands[5].shape[0]
    tokens, model = inputs.shape
    hidden = gate_pre.shape[1]
    assert hidden % (2 * STEP) == STEP and model % (2 * STEP) == 0 and tokens % ROWS == 0
    assert 3 * STEP + model <= hidden and tokens == 3 * width
    bf16 = jnp.bfloat16
    return pl.pallas_call(
        project,
        out_shape=[jax.ShapeDtypeStruct((tokens // 2, 6 * width), jnp.float32)] * 2,
        in_specs=[pl.BlockSpec(memory_space=pltpu.HBM)] * len(operands),
        out_specs=[pl.BlockSpec(memory_space=pltpu.VMEM)] * 2,
        scratch_shapes=[
            pltpu.VMEM((tokens, model), bf16),
            pltpu.VMEM((tokens, hidden), bf16),
            pltpu.VMEM((tokens, hidden), bf16),
            pltpu.VMEM((tokens, hidden), bf16),
            pltpu.VMEM((tokens, model), bf16),
            pltpu.VMEM((2 * width, model), bf16),
            pltpu.VMEM((width, hidden), bf16),
            pltpu.VMEM((width, hidden), bf16),
            pltpu.VMEM((width, hidden), bf16),
            pltpu.VMEM((width, model), bf16),
            pltpu.VMEM((tokens, 2 * width), jnp.float32),
            pltpu.VMEM((4, tokens, width), jnp.float32),
            pltpu.SemaphoreType.DMA((hidden // STEP + 1,)),
        ],
        compiler_params=pltpu.CompilerParams(vmem_limit_bytes=427 * 2**17),
        cost_estimate=pl.CostEstimate(
            flops=6 * tokens * width * (model + hidden),
            bytes_accessed=2 * (2 * tokens * model + 3 * tokens * hidden),
            transcendentals=tokens * hidden,
        ),
        name="project",
    )(*operands)


def first_chip(chips):
    return chips // 2 + 1


def first_device(chips):
    return 2 * first_chip(chips) + 1


def two_terms(value):
    high = value.astype(jnp.bfloat16)
    return high, (value - high.astype(jnp.float32)).astype(jnp.bfloat16)


def outer(chips, own, other, ids, out, summed, products):
    chip, core = lax.axis_index("dp"), lax.axis_index("mp")
    width = own.shape[1] // 6
    half = width // 2
    span = 3 * half // chips
    summed[...] = (own[...] + other[...]).T
    label = 2 * chip + core
    mine = ids[pl.ds(core, 1), :]
    masks = [(mine == each).astype(jnp.float32) for each in (label - 1, label)]
    lane = lax.broadcasted_iota(jnp.int32, (half, 2 * width), 1)
    for module, (left, right) in enumerate(((0, 2), (1, 3), (4, 5))):
        factor = summed[left * width : (left + 1) * width, :]
        high, low = two_terms(jnp.concatenate([factor * mask for mask in masks], axis=0))
        top, bottom = two_terms(summed[right * width : (right + 1) * width, :])
        product = None
        for one, two in ((high, top), (high, bottom), (low, top)):
            both = jnp.concatenate([two, two], axis=0)
            term = lax.dot_general(one, both, NT, preferred_element_type=jnp.float32)
            product = term if product is None else product + term
        products[module] = product
        for label in range(2):
            even = products[module, pl.ds(label * width, half, stride=2), :]
            odd = products[module, pl.ds(label * width + 1, half, stride=2), :]
            packed = jnp.where(lane < width, even, odd)
            row = 0
            while row < half:
                chip_to, inside = divmod(module * half + row, span)
                count = min(span - inside, half - row)
                put = slice(label * span + inside, label * span + inside + count)
                out[(chip_to - first_chip(chips)) % chips, put, :] = packed[row : row + count]
                row += count


def example_blocks(chips, own, other, ids):
    width = own.shape[1] // 6
    block = (3 * width // chips, 2 * width)
    return pl.pallas_call(
        functools.partial(outer, chips),
        out_shape=jax.ShapeDtypeStruct((chips,) + block, jnp.float32),
        in_specs=[pl.BlockSpec(memory_space=pltpu.VMEM)] * 3,
        out_specs=pl.BlockSpec(memory_space=pltpu.VMEM),
        scratch_shapes=[
            pltpu.VMEM(own.shape[::-1], jnp.float32),
            pltpu.VMEM((3, 2 * width, 2 * width), jnp.float32),
        ],
        compiler_params=pltpu.CompilerParams(vmem_limit_bytes=6 * 2**20),
        name="outer",
    )(own, other, ids)


def score(queries, swapped, received, out, rows):
    core = lax.axis_index("mp")
    chips, height, lanes = received.shape
    span = height // 2
    first = first_chip(chips)
    rows[: first * height, :] = received[chips - first :].reshape(first * height, lanes)
    rows[first * height : chips * height, :] = received[: chips - first].reshape((chips - first) * height, lanes)
    grads = []
    for label in range(2):
        parts = [rows[pl.ds(label * span + at, chips, stride=height), :] for at in range(span)]
        grads.append(jnp.concatenate(parts, axis=1))
    terms = jnp.concatenate(two_terms(jnp.concatenate(grads, axis=0)), axis=0)
    coords = queries.shape[1]
    even = core == 0
    mine = jnp.where(even, terms[:, :coords], terms[:, coords:])
    theirs = jnp.where(even, terms[:, coords:], terms[:, :coords])
    scores = lax.dot_general(mine, queries[...], NT, preferred_element_type=jnp.float32)
    scores += lax.dot_general(theirs, swapped[...], NT, preferred_element_type=jnp.float32)
    total = scores[: 2 * chips] + scores[2 * chips :]
    none = jnp.zeros_like(total[:1])
    tails = [total[chip : chip + 1] for chip in range(chips)] + [none]
    owns = [total[chips + chip : chips + chip + 1] for chip in range(chips)]
    for device in range(2 * chips):
        place = (device - first_device(chips)) % (2 * chips)
        chip = device // 2
        if device % 2 == 0:
            row = jnp.where(even, owns[chip], tails[chip])
        else:
            row = jnp.where(even, tails[chip + 1], owns[chip])
        out[place : place + 1, :] = row


def partial_scores(queries, swapped, received):
    chips, height, lanes = received.shape
    return pl.pallas_call(
        score,
        out_shape=jax.ShapeDtypeStruct((2 * chips, queries.shape[0]), jnp.float32),
        in_specs=[pl.BlockSpec(memory_space=pltpu.VMEM)] * 3,
        out_specs=pl.BlockSpec(memory_space=pltpu.VMEM),
        scratch_shapes=[pltpu.VMEM((chips * height, lanes), jnp.float32)],
        compiler_params=pltpu.CompilerParams(vmem_limit_bytes=6 * 2**20),
        name="score",
    )(queries, swapped, received)


def to_all(blocks, axes, first):
    count = blocks.shape[0]
    order = [(i + first) % count for i in range(count)]
    return lax.all_to_all(
        blocks, axes, split_axis=0, concat_axis=0, axis_index_groups=[order], tiled=True
    )


def body(
    inputs,
    gate_pre,
    up_pre,
    hidden_grad,
    out_grad,
    example_ids,
    gate_in,
    gate_out,
    up_in,
    up_out,
    down_in,
    down_out,
    queries,
):
    chips = lax.axis_size("dp")
    swap = [(0, 1), (1, 0)]
    swapped = lax.ppermute(queries, "mp", swap)
    bases = [base.T for base in (gate_in, gate_out, up_in, up_out, down_in, down_out)]
    own, given = projections(inputs, gate_pre, up_pre, hidden_grad, out_grad, *bases)
    other = lax.ppermute(given, "mp", swap)
    blocks = example_blocks(chips, own, other, example_ids.reshape(2, -1))
    received = to_all(blocks, "dp", first_chip(chips))
    scores = partial_scores(queries, swapped, received)[:, None]
    pieces = to_all(scores, ("dp", "mp"), first_device(chips))
    return jnp.sum(pieces, axis=0)


def solution(mesh):
    placed = (
        P(("parts", "dp"), "mp"),
        P(("parts", "dp"), "mp"),
        P(("parts", "dp"), "mp"),
        P(("parts", "dp"), "mp"),
        P(("parts", "dp"), "mp"),
        P(("parts", "dp")),
        P("mp", None),
        P("mp", None),
        P("mp", None),
        P("mp", None),
        P("mp", None),
        P("mp", None),
        P(None, ("dp", "mp")),
    )
    return jax.shard_map(
        body, mesh=mesh, in_specs=placed, out_specs=P(("parts", "dp", "mp"), None), check_vma=False
    )
```

```python
import functools

import jax
import jax.numpy as jnp
from jax import lax
from jax.experimental import pallas as pl
from jax.experimental.pallas import tpu as pltpu
from jax.sharding import PartitionSpec as P

NT = (((1,), (1,)), ((), ()))
STEP = 1024
TILE = 256
ROWS = 16
AHEAD = 8


def project(
    inputs,
    gate_pre,
    up_pre,
    hidden_grad,
    out_grad,
    gate_in,
    gate_out,
    up_in,
    up_out,
    down_in,
    down_out,
    kept,
    given,
    v_inputs,
    v_gate,
    v_up,
    v_back,
    v_out_grad,
    v_in,
    v_gate_out,
    v_up_out,
    v_down_in,
    v_down_out,
    sum_in,
    sums,
    sems,
):
    width = gate_in.shape[0]
    tokens = inputs.shape[0]
    hidden, model = gate_pre.shape[1], inputs.shape[1]
    edges = [0] + list(range(STEP // 2, hidden, STEP)) + [hidden]
    steps = len(edges) - 1
    activations = ((gate_pre, v_gate), (up_pre, v_up), (hidden_grad, v_back))
    hidden_bases = ((gate_out, v_gate_out), (up_out, v_up_out), (down_in, v_down_in))
    model_bases = (
        (gate_in, v_in.at[pl.ds(0, width), :]),
        (up_in, v_in.at[pl.ds(width, width), :]),
        (down_out, v_down_out),
    )
    tokens_wide = ((inputs, v_inputs), (out_grad, v_out_grad))
    first_model = 3
    second_model = first_model + model // STEP // 2
    groups = []
    for step in range(steps):
        low, high = edges[step], edges[step + 1]
        pairs = [(pair, low, high - low) for pair in activations]
        if step == 0:
            pairs += [(pair, low, high - low) for pair in hidden_bases]
        if step == 1:
            pairs += [(pair, low, hidden // 2 - low) for pair in hidden_bases]
        if low == hidden // 2:
            pairs += [(pair, low, hidden // 2) for pair in hidden_bases]
        if step == first_model - 1:
            pairs += [(pair, 0, model) for pair in model_bases]
        if step == first_model:
            pairs += [(pair, 0, model // 2) for pair in tokens_wide]
        if step == second_model:
            pairs += [(pair, model // 2, model // 2) for pair in tokens_wide]
        groups.append(pairs)

    def start(step):
        for (source, target), low, length in groups[step]:
            at = pl.ds(low, length)
            pltpu.make_async_copy(source.at[:, at], target.at[:, at], sems.at[step]).start()

    def wait(step):
        count = sum(source.shape[0] * length for (source, _), _, length in groups[step])
        at = pl.ds(0, count // tokens)
        pltpu.make_async_copy(gate_pre.at[:, at], v_gate.at[:, at], sems.at[step]).wait()

    def products(left):
        parts = []
        for top in range(0, tokens, ROWS):
            at = (slice(top, top + ROWS), slice(left, left + TILE))
            half = 0.5 * v_gate[at].astype(jnp.float32)
            up = v_up[at].astype(jnp.float32)
            back = v_back[at].astype(jnp.float32)
            tanh = jnp.tanh(half)
            plus = 1.0 + tanh
            silu = half * plus
            slope = plus + silu * (1.0 - tanh)
            values = (back * up * slope, back * silu, silu * up)
            parts.append([value.astype(jnp.bfloat16) for value in values])
        return [jnp.concatenate(column, axis=0) for column in zip(*parts)]

    def add(total, values, base, first):
        value = lax.dot_general(values, base, NT, preferred_element_type=jnp.float32)
        if first:
            total[...] = value
        else:
            total[...] += value

    def hidden_dots(left):
        at = slice(left, left + TILE)
        bases = (v_gate_out, v_up_out, v_down_in)
        for which, value in enumerate(products(left)):
            add(sums.at[which], value, bases[which][:, at], left == 0)

    def model_dots(left):
        at = slice(left, left + TILE)
        add(sum_in, v_inputs[:, at], v_in[:, at], left == 0)
        add(sums.at[3], v_out_grad[:, at], v_down_out[:, at], left == 0)

    for step in range(AHEAD):
        start(step)
    for step in range(steps):
        if step + AHEAD < steps:
            start(step + AHEAD)
        wait(step)
        for left in range(edges[step], edges[step + 1], TILE):
            hidden_dots(left)
            model_left = left - edges[first_model]
            if 0 <= model_left < model:
                model_dots(model_left)
    core = lax.axis_index("mp")
    half = tokens // 2
    for out, which in ((kept, core), (given, 1 - core)):
        rows = pl.ds(pl.multiple_of(which * half, half), half)
        out[:, : 2 * width] = sum_in[rows, :]
        out[:, 2 * width : 4 * width] = jnp.concatenate(
            [0.5 * sums[0, rows, :], sums[1, rows, :]], axis=1
        )
        out[:, 4 * width :] = jnp.concatenate([sums[2, rows, :], sums[3, rows, :]], axis=1)


def projections(*operands):
    inputs, gate_pre = operands[:2]
    width = operands[5].shape[0]
    tokens, model = inputs.shape
    hidden = gate_pre.shape[1]
    assert hidden % (2 * STEP) == STEP and model % (2 * STEP) == 0 and tokens % ROWS == 0
    assert 3 * STEP + model <= hidden and tokens == 3 * width
    bf16 = jnp.bfloat16
    return pl.pallas_call(
        project,
        out_shape=[jax.ShapeDtypeStruct((tokens // 2, 6 * width), jnp.float32)] * 2,
        in_specs=[pl.BlockSpec(memory_space=pltpu.HBM)] * len(operands),
        out_specs=[pl.BlockSpec(memory_space=pltpu.VMEM)] * 2,
        scratch_shapes=[
            pltpu.VMEM((tokens, model), bf16),
            pltpu.VMEM((tokens, hidden), bf16),
            pltpu.VMEM((tokens, hidden), bf16),
            pltpu.VMEM((tokens, hidden), bf16),
            pltpu.VMEM((tokens, model), bf16),
            pltpu.VMEM((2 * width, model), bf16),
            pltpu.VMEM((width, hidden), bf16),
            pltpu.VMEM((width, hidden), bf16),
            pltpu.VMEM((width, hidden), bf16),
            pltpu.VMEM((width, model), bf16),
            pltpu.VMEM((tokens, 2 * width), jnp.float32),
            pltpu.VMEM((4, tokens, width), jnp.float32),
            pltpu.SemaphoreType.DMA((hidden // STEP + 1,)),
        ],
        compiler_params=pltpu.CompilerParams(vmem_limit_bytes=427 * 2**17),
        cost_estimate=pl.CostEstimate(
            flops=6 * tokens * width * (model + hidden),
            bytes_accessed=2 * (2 * tokens * model + 3 * tokens * hidden),
            transcendentals=tokens * hidden,
        ),
        name="project",
    )(*operands)


def first_chip(chips):
    return chips // 2 + 1


def first_device(chips):
    return 2 * first_chip(chips) + 1


def two_terms(value):
    high = value.astype(jnp.bfloat16)
    return high, (value - high.astype(jnp.float32)).astype(jnp.bfloat16)


def outer(chips, own, other, ids, out, summed, products):
    chip, core = lax.axis_index("dp"), lax.axis_index("mp")
    width = own.shape[1] // 6
    half = width // 2
    span = 3 * half // chips
    summed[...] = (own[...] + other[...]).T
    label = 2 * chip + core
    mine = ids[pl.ds(core, 1), :]
    masks = [(mine == each).astype(jnp.float32) for each in (label - 1, label)]
    lane = lax.broadcasted_iota(jnp.int32, (half, 2 * width), 1)
    for module, (left, right) in enumerate(((0, 2), (1, 3), (4, 5))):
        factor = summed[left * width : (left + 1) * width, :]
        high, low = two_terms(jnp.concatenate([factor * mask for mask in masks], axis=0))
        top, bottom = two_terms(summed[right * width : (right + 1) * width, :])
        product = None
        for one, two in ((high, top), (high, bottom), (low, top)):
            both = jnp.concatenate([two, two], axis=0)
            term = lax.dot_general(one, both, NT, preferred_element_type=jnp.float32)
            product = term if product is None else product + term
        products[module, : 2 * width, :] = product
        for label in range(2):
            even = products[module, pl.ds(label * width, half, stride=2), :]
            odd = products[module, pl.ds(label * width + 1, half, stride=2), :]
            packed = jnp.where(lane < width, even, odd)
            row = 0
            while row < half:
                chip_to, inside = divmod(module * half + row, span)
                count = min(span - inside, half - row)
                put = slice(label * span + inside, label * span + inside + count)
                out[(chip_to - first_chip(chips)) % chips, put, :] = packed[row : row + count]
                row += count


def example_blocks(chips, own, other, ids):
    width = own.shape[1] // 6
    block = (3 * width // chips, 2 * width)
    return pl.pallas_call(
        functools.partial(outer, chips),
        out_shape=jax.ShapeDtypeStruct((chips,) + block, jnp.float32),
        in_specs=[pl.BlockSpec(memory_space=pltpu.VMEM)] * 3,
        out_specs=pl.BlockSpec(memory_space=pltpu.VMEM),
        scratch_shapes=[
            pltpu.VMEM(own.shape[::-1], jnp.float32),
            pltpu.VMEM((3, 2 * width + 8, 2 * width), jnp.float32),
        ],
        compiler_params=pltpu.CompilerParams(vmem_limit_bytes=6 * 2**20),
        name="outer",
    )(own, other, ids)


def score(queries, swapped, received, out, rows):
    core = lax.axis_index("mp")
    chips, height, lanes = received.shape
    span = height // 2
    first = first_chip(chips)
    rows[: first * height, :] = received[chips - first :].reshape(first * height, lanes)
    rows[first * height : chips * height, :] = received[: chips - first].reshape((chips - first) * height, lanes)
    grads = []
    for label in range(2):
        parts = [rows[pl.ds(label * span + at, chips, stride=height), :] for at in range(span)]
        grads.append(jnp.concatenate(parts, axis=1))
    terms = jnp.concatenate(two_terms(jnp.concatenate(grads, axis=0)), axis=0)
    coords = queries.shape[1]
    even = core == 0
    mine = jnp.where(even, terms[:, :coords], terms[:, coords:])
    theirs = jnp.where(even, terms[:, coords:], terms[:, :coords])
    scores = lax.dot_general(mine, queries[...], NT, preferred_element_type=jnp.float32)
    scores += lax.dot_general(theirs, swapped[...], NT, preferred_element_type=jnp.float32)
    total = scores[: 2 * chips] + scores[2 * chips :]
    none = jnp.zeros_like(total[:1])
    tails = [total[chip : chip + 1] for chip in range(chips)] + [none]
    owns = [total[chips + chip : chips + chip + 1] for chip in range(chips)]
    for device in range(2 * chips):
        place = (device - first_device(chips)) % (2 * chips)
        chip = device // 2
        if device % 2 == 0:
            row = jnp.where(even, owns[chip], tails[chip])
        else:
            row = jnp.where(even, tails[chip + 1], owns[chip])
        out[place : place + 1, :] = row


def partial_scores(queries, swapped, received):
    chips, height, lanes = received.shape
    return pl.pallas_call(
        score,
        out_shape=jax.ShapeDtypeStruct((2 * chips, queries.shape[0]), jnp.float32),
        in_specs=[pl.BlockSpec(memory_space=pltpu.VMEM)] * 3,
        out_specs=pl.BlockSpec(memory_space=pltpu.VMEM),
        scratch_shapes=[pltpu.VMEM(((chips + 1) * height, lanes), jnp.float32)],
        compiler_params=pltpu.CompilerParams(vmem_limit_bytes=6 * 2**20),
        name="score",
    )(queries, swapped, received)


def to_all(blocks, axes, first):
    count = blocks.shape[0]
    order = [(i + first) % count for i in range(count)]
    return lax.all_to_all(
        blocks, axes, split_axis=0, concat_axis=0, axis_index_groups=[order], tiled=True
    )


def body(
    inputs,
    gate_pre,
    up_pre,
    hidden_grad,
    out_grad,
    example_ids,
    gate_in,
    gate_out,
    up_in,
    up_out,
    down_in,
    down_out,
    queries,
):
    chips = lax.axis_size("dp")
    swap = [(0, 1), (1, 0)]
    swapped = lax.ppermute(queries, "mp", swap)
    bases = [base.T for base in (gate_in, gate_out, up_in, up_out, down_in, down_out)]
    own, given = projections(inputs, gate_pre, up_pre, hidden_grad, out_grad, *bases)
    other = lax.ppermute(given, "mp", swap)
    blocks = example_blocks(chips, own, other, example_ids.reshape(2, -1))
    received = to_all(blocks, "dp", first_chip(chips))
    scores = partial_scores(queries, swapped, received)[:, None]
    pieces = to_all(scores, ("dp", "mp"), first_device(chips))
    return jnp.sum(pieces, axis=0)


def solution(mesh):
    placed = (
        P(("parts", "dp"), "mp"),
        P(("parts", "dp"), "mp"),
        P(("parts", "dp"), "mp"),
        P(("parts", "dp"), "mp"),
        P(("parts", "dp"), "mp"),
        P(("parts", "dp")),
        P("mp", None),
        P("mp", None),
        P("mp", None),
        P("mp", None),
        P("mp", None),
        P("mp", None),
        P(None, ("dp", "mp")),
    )
    return jax.shard_map(
        body, mesh=mesh, in_specs=placed, out_specs=P(("parts", "dp", "mp"), None), check_vma=False
    )
```
